256 devices in a mesh: dom: 64 (over z, y, core), rep: 4 (over x).
Axes of the slice: x: 4, y: 4, z: 8, core: 2. Of those that a mesh axis runs over, the one named last changes fastest.
Arguments:
- features: bfloat16 [65536, 512], P('dom', 'rep'), may hold values from -6 to 6
- weight: bfloat16 [512, 512], P(None, 'rep'), may hold values from -0.25 to 0.25
- bias: bfloat16 [512], P('rep'), may hold values from -3 to 3
- cotangent: bfloat16 [65536, 512], P('dom', 'rep'), may hold values from -6 to 6
- tile_vals: bfloat16 [64, 160, 128, 128], P('dom'), may hold values from -0.21875 to 0.21875
- tile_row: int32 [64, 160], P('dom'), may hold values from 0 to 8, as said below
- tile_src: int32 [64, 160], P('dom'), may hold values from 0 to 135, as said below
- send_blocks: int32 [64, 64, 2], P('dom'), may hold values from 0 to 7
- send_count: int32 [64, 64], P('dom'), may hold values from 0 to 2, as said below
Outputs:
- out: bfloat16 [65536, 512], P('dom', 'rep')
- grad_input: bfloat16 [65536, 512], P('dom', 'rep')
- grad_weight: float32 [512, 512], P(None, 'rep')
- grad_bias: float32 [512], P('rep')
The draws below stay inside these ranges and needn't reach their ends.
Inputs may be any that keep to these rules, and one draw needn't show every extreme that they name: Partition q sends the first send_count[q, p] entries of send_blocks[q, p] to partition p; send_count[q, q] = 0, and every partition sends 2 blocks to some partition. `tile_row`: 8 marks an unused slot. Slots below 32 take own blocks; slot 32 + q * 2 + c is used only if c < send_count[q, p]. Partition 0 uses all its own-block slots. `tile_src`: slots below 32 name an own block below 8; slot 32 + m names source slot 8 + m.
All inputs are finite; a program needn't handle non-finite values.
Results may differ from the reference program's by a relative error of at most 0.007.
Values may be sent and summed in bfloat16 or wider, within the bound.
A program may use at most 128 MiB of HBM per device.

```python
import jax
import jax.numpy as jnp
from jax import lax

F = 512
B = 128
NB = 8
LOC = 4
CAP = 2
PARTITIONS = 64
NODES = 65536
KT = 160


def layout(key):
    base = jax.random.fold_in(key, 11)
    keys = jax.random.split(base, 5)
    index = jnp.arange(PARTITIONS, dtype=jnp.int32)
    counts = jax.random.randint(keys[0], (PARTITIONS, PARTITIONS), 0, CAP + 1, dtype=jnp.int32)
    follow = index[None, :] == (index[:, None] + 1) % PARTITIONS
    itself = index[None, :] == index[:, None]
    counts = jnp.where(follow, CAP, jnp.where(itself, 0, counts)).astype(jnp.int32)
    sends = jax.random.randint(keys[1], (PARTITIONS, PARTITIONS, CAP), 0, NB, dtype=jnp.int32)
    slot = jnp.arange(NB * LOC, dtype=jnp.int32)
    target = slot // LOC
    column = slot % LOC
    chosen = jax.random.randint(keys[2], (PARTITIONS, NB * LOC), 0, NB, dtype=jnp.int32)
    local_src = jnp.where(column[None, :] == 0, target[None, :], chosen)
    level = jax.random.randint(keys[3], (PARTITIONS,), 0, 17, dtype=jnp.int32)
    level = level.at[0].set(16)
    extra = NB * (LOC - 1) * level * level // 256
    rank = (column - 1) * NB + target
    used = (column[None, :] == 0) | (rank[None, :] < extra[:, None])
    local_row = jnp.where(used, target[None, :], NB)
    remote_slot = jnp.arange(PARTITIONS * CAP, dtype=jnp.int32)
    anchor = remote_slot // CAP
    place = remote_slot % CAP
    arriving = counts.T[:, anchor]
    remote_used = place[None, :] < arriving
    picked = jax.random.randint(keys[4], (PARTITIONS, PARTITIONS * CAP), 0, NB, dtype=jnp.int32)
    remote_row = jnp.where(remote_used, picked, NB)
    remote_src = jnp.broadcast_to(NB + remote_slot, (PARTITIONS, PARTITIONS * CAP))
    tile_rows = jnp.concatenate([local_row, remote_row], 1).astype(jnp.int32)
    tile_sources = jnp.concatenate([local_src, remote_src], 1).astype(jnp.int32)
    return (sends, counts, tile_rows, tile_sources)


def draw_send_blocks(key, part):
    return layout(key)[0]


def draw_send_count(key, part):
    return layout(key)[1]


def draw_tile_row(key, part):
    return layout(key)[2]


def draw_tile_src(key, part):
    return layout(key)[3]


def steps_of(rng, shape, cuts, low, largest):
    def one(position, shards_of):
        heights = jax.random.uniform(jax.random.fold_in(jax.random.fold_in(rng, 6), position), (shards_of,), jnp.float32, low / len(cuts), largest / len(cuts))
        return jnp.repeat(jnp.exp(heights), shape[position] // shards_of).reshape((-1,) + (1,) * (len(shape) - position - 1))

    level = one(*cuts[0])
    for cut in cuts[1:]:
        level = level * one(*cut)
    return level


def bell_draw(stream_key, shape, width, limit, pieces=(), held_as=jnp.bfloat16):
    values = width * jax.random.normal(stream_key, shape, jnp.float32)
    if pieces:
        values = values * steps_of(stream_key, shape, pieces, -0.22, 0.18)
    return jnp.clip(values, -limit, limit).astype(held_as)


def setup_inputs(seed: int = 0) -> dict:
    streams_of = jax.random.split(jax.random.key(seed), 10)
    return {
        "features": bell_draw(streams_of[0], (NODES, F), 1.0, 6.0, ((0, 64), (1, 4))),
        "weight": bell_draw(streams_of[1], (F, F), F ** -0.5, 0.25, ((1, 4),)),
        "bias": bell_draw(streams_of[2], (F,), 0.5, 3.0, ((0, 4),)),
        "cotangent": bell_draw(streams_of[3], (NODES, F), 1.0, 6.0, ((0, 64), (1, 4))),
        "tile_vals": bell_draw(streams_of[4], (PARTITIONS, KT, B, B), (B * (LOC + 2)) ** -0.5, 0.21875, ((0, 64),)),
        "tile_row": draw_tile_row(jax.random.fold_in(streams_of[9], 71), 0),
        "tile_src": draw_tile_src(jax.random.fold_in(streams_of[9], 71), 0),
        "send_blocks": draw_send_blocks(jax.random.fold_in(streams_of[9], 71), 0),
        "send_count": draw_send_count(jax.random.fold_in(streams_of[9], 71), 0),
    }


def reference(features, weight, bias, cotangent, tile_vals, tile_row, tile_src, send_blocks, send_count):
    hidden = jnp.dot(features, weight, preferred_element_type=jnp.float32).astype(jnp.bfloat16)
    hidden_blocks = hidden.reshape(PARTITIONS, NB, B, F)
    part_ids = jnp.arange(PARTITIONS, dtype=jnp.int32)
    depth = jnp.arange(CAP, dtype=jnp.int32)
    live_slot = depth[None, None, :] < send_count[:, :, None]

    def forward(part_index):
        taken = hidden_blocks[part_ids[:, None], send_blocks[:, part_index, :]]
        taken = jnp.where(live_slot[:, part_index, :, None, None], taken, jnp.zeros_like(taken))
        sources = jnp.concatenate([hidden_blocks[part_index], taken.reshape(PARTITIONS * CAP, B, F)], 0)
        picked = sources[tile_src[part_index]].astype(jnp.float32)
        product = jnp.einsum("kab,kbf->kaf", tile_vals[part_index].astype(jnp.float32), picked)
        return jax.ops.segment_sum(product, tile_row[part_index], NB + 1)[:NB]

    aggregate = lax.map(forward, part_ids).reshape(NODES, F)
    shifted = aggregate + bias.astype(jnp.float32)
    sigma = jax.nn.sigmoid(shifted)
    out = (shifted * sigma).astype(jnp.bfloat16)
    grad_pre = (cotangent.astype(jnp.float32) * sigma * (1.0 + shifted * (1.0 - sigma))).astype(jnp.bfloat16)
    pre_blocks = grad_pre.reshape(PARTITIONS, NB, B, F)
    pre_padded = jnp.concatenate([pre_blocks, jnp.zeros((PARTITIONS, 1, B, F), jnp.bfloat16)], 1)

    def backward(running, part_index):
        picked = pre_padded[part_index][tile_row[part_index]].astype(jnp.float32)
        contrib = jnp.einsum("kab,kaf->kbf", tile_vals[part_index].astype(jnp.float32), picked)
        per_slot = jax.ops.segment_sum(contrib, tile_src[part_index], NB + PARTITIONS * CAP)
        running = running.at[part_index].add(per_slot[:NB])
        remote = per_slot[NB:].reshape(PARTITIONS, CAP, B, F)
        remote = jnp.where(live_slot[:, part_index, :, None, None], remote, jnp.zeros_like(remote))
        running = running.at[part_ids[:, None], send_blocks[:, part_index, :]].add(remote)
        return running, None

    running = lax.scan(backward, jnp.zeros((PARTITIONS, NB, B, F), jnp.float32), part_ids)[0]
    grad_agg = running.reshape(NODES, F).astype(jnp.bfloat16)
    grad_weight = jnp.dot(features.T, grad_agg, preferred_element_type=jnp.float32)
    grad_bias = jnp.sum(grad_pre.astype(jnp.float32), 0)
    grad_input = jnp.dot(grad_agg, weight.T, preferred_element_type=jnp.float32).astype(jnp.bfloat16)
    return (out, grad_input, grad_weight, grad_bias)
```

```python
import jax
import jax.numpy as jnp
from jax import lax
from jax.experimental import pallas as pl
from jax.experimental.pallas import tpu as pltpu
from jax.sharding import PartitionSpec as P

B = 128
NB = 8
CAP = 2
NX, NY, NZ, NC = 4, 4, 8, 2
MESH = pl.DeviceIdType.MESH
BF = jnp.bfloat16
F32 = jnp.float32

DIST = [0, 1, -1, 2, -2, 3, -3, 4]
SLOT = {d: e for e, d in enumerate(DIST)}
SLOT[-4] = SLOT[4]


def dot(a, b):
    return lax.dot_general(a, b, (((1,), (0,)), ((), ())), preferred_element_type=F32)


def dot_t(a, b):
    return lax.dot_general(a, b, (((1,), (1,)), ((), ())), preferred_element_type=F32)


class Semaphores:
    def __init__(self):
        self.n = 0

    def take(self, count):
        first = self.n
        self.n += count
        return first


S = Semaphores()
S_FEAT = S.take(4)
S_FREL = S.take(2)
S_SB = S.take(16)
S_ROW = S.take(4)
S_TY = S.take(16)
S_TQ = S.take(8)
S_HZ = S.take(16)
S_HC = S.take(16)
S_YR = S.take(2)
S_YI = S.take(4)
S_G = S.take(4)
S_GR = S.take(2)
S_SIB = S.take(8)
S_ZR = S.take(16)
S_XR = S.take(2)
S_XI = S.take(4)
S_A1 = S.take(16)
S_A2 = S.take(4)
S_A3 = S.take(16)
S_RECV = S.n
S_TF = S.take(6)
S_SEND = S.n
L_OWN, L_LOC, L_SB, L_ROW, L_N = 0, 1, 2, 3, 4


def kernel(
    feat, weight, bias, cot, tiles, sendb, trow, row_own, src_own,
    out, gin, gw, gb,
    F, Hown, Hcore, H1, H2, H3, H4, H5, H6, H7, T, TL, agg, ysend2, ysend1, ysend3, yrel, yin, G0, G1, G2, G3, D, S0, SL, zsend, zrecv, sibsend, sibrecv,
    GAT, GA, PT, xsend2, xsend1, xsend3, xrel, xin, bsum, arsend, arin, ar2in, red, gwall,
    sbv, rowv, sbs, rows, ssem, rsem, lsem,
):
    H = [None, H1, H2, H3, H4, H5, H6, H7]
    G = [G0, G1, G2, G3]

    def hid(e, oc):
        return H[e].at[oc] if e else (Hown, Hcore)[oc]

    dom, x = lax.axis_index("dom"), lax.axis_index("rep")
    z = dom // (NY * NC)
    y = lax.rem(dom // NC, NY)
    c = lax.rem(dom, NC)

    def at(dx=0, dy=0, dz=0, oc=0):
        zz = lax.rem(z + dz + NZ, NZ)
        yy = lax.rem(y + dy + NY, NY)
        cc = lax.rem(c + oc, NC)
        return ((zz * NY + yy) * NC + cc, lax.rem(x + dx + NX, NX))

    started = []

    def copy(src, dst, sem, dev, recv=None):
        return pltpu.make_async_remote_copy(
            src_ref=src,
            dst_ref=dst,
            send_sem=ssem.at[sem],
            recv_sem=rsem.at[sem if recv is None else recv],
            device_id=dev,
            device_id_type=MESH,
        )

    def send(src, dst, sem, dev, recv=None):
        made = copy(src, dst, sem, dev, recv)
        made.start()
        started.append(made)

    here = (dom, x)

    def arrived(dst, sem):
        pltpu.make_async_remote_copy(
            src_ref=dst, dst_ref=dst, send_sem=ssem.at[0], recv_sem=rsem.at[sem], device_id=here, device_id_type=MESH
        ).wait_recv()

    half = lambda ref, h: ref.at[pl.ds(4 * h, 4)]

    own_tiles = [
        pltpu.make_async_copy(
            tiles.at[2 + lax.rem(z + DIST[e] + NZ, NZ), y], T.at[0, e], lsem.at[L_N + e]
        )
        for e in range(NZ)
    ]
    loc_tiles = pltpu.make_async_copy(tiles.at[pl.ds(0, 2)], TL, lsem.at[L_LOC])
    for made in own_tiles:
        made.start()
    loc_tiles.start()

    barrier = pltpu.get_barrier_semaphore()
    peers = [at(dz=DIST[e], oc=oc) for e in range(NZ) for oc in range(NC) if (e, oc) != (0, 0)]
    peers += [at(dy=d) for d in range(1, NY)] + [at(dx=d) for d in range(1, NX)]
    for dev in peers:
        pl.semaphore_signal(barrier, inc=1, device_id=dev, device_id_type=MESH)
    pl.semaphore_wait(barrier, len(peers))

    rows_of = lambda h: pl.ds(512 * h, 512)
    for h, g in ((0, 1), (1, 0)):
        send(feat.at[rows_of(h)], F.at[3, rows_of(h)], S_FEAT + h, at(dx=1))
        send(feat.at[rows_of(g)], F.at[1, rows_of(g)], S_FEAT + 2 + g, at(dx=-1))
    for e in range(NZ):
        for oc in range(NC):
            if (e, oc) != (0, 0):
                back = SLOT[-DIST[e]]
                send(sendb, sbv.at[back, oc], S_SB + back * 2 + oc, at(dz=DIST[e], oc=oc))
    for d in range(1, NY):
        send(trow, rowv.at[NY - d], S_ROW + NY - d, at(dy=d))
    sbv[0, 0] = sendb[...]
    rowv[0] = trow[...]

    def tile_slot(e):
        d = jnp.where(lax.rem(e, 2) == 1, (e + 1) // 2, NZ - e // 2)
        return 2 + lax.rem(z + d, NZ)

    for k in range(2):
        e = x + 4 * k
        send(tiles.at[tile_slot(e), lax.rem(y + 2, NY)], T.at[2, e], S_TQ + k, at(dy=2), S_TQ + e)
    for e in range(NZ):
        for dy, to, base in ((1, 3, 0), (-1, 1, 8)):
            send(
                tiles.at[2 + lax.rem(z + DIST[e] + NZ, NZ), lax.rem(y + dy + NY, NY)],
                T.at[to, e],
                S_TY + base + e,
                at(dy=dy),
            )

    F[0] = feat[...]
    for dy in range(NY):
        G[dy][NB] = jnp.zeros((B, B), BF)

    @pl.loop(0, NB)
    def _(i):
        for dy in range(NY):
            agg[dy, i] = jnp.zeros((B, B), F32)
        SL[i] = jnp.zeros((B, B), F32)

    arrived(F.at[3, rows_of(0)], S_FEAT + 0)
    send(F.at[3, rows_of(0)], F.at[2, rows_of(0)], S_FREL + 0, at(dx=1))
    arrived(F.at[1, rows_of(1)], S_FEAT + 3)
    send(F.at[1, rows_of(1)], F.at[2, rows_of(1)], S_FREL + 1, at(dx=-1))
    arrived(F.at[1, rows_of(0)], S_FEAT + 2)
    arrived(F.at[3, rows_of(1)], S_FEAT + 1)

    def w_rows(dx):
        return weight[pl.ds(pl.multiple_of(lax.rem(x + dx, NX) * B, B), B), :]

    def step_send(way, step, h):
        d = -step if way == 0 else step
        nd = d - 1 if way == 0 else d + 1
        send(
            half(hid(SLOT[d], 0), h), half(hid(SLOT[nd], 0), h), S_HZ + way * 8 + step * 2 + h,
            at(dz=1 if way == 0 else -1),
        )

    def core_send(e, h):
        send(half(hid(e, 0), h), half(hid(e, 1), h), S_HC + e * 2 + h, at(oc=1))

    for h in range(2):
        arrived(F.at[2, rows_of(h)], S_FREL + h)

        @pl.loop(0, 4)
        def _(b, h=h):
            r = pl.ds(pl.multiple_of(512 * h + b * B, B), B)
            acc = dot(F[0, r], w_rows(0))
            for dx in range(1, NX):
                acc += dot(F[dx, r], w_rows(dx))
            Hown[4 * h + b] = acc.astype(BF)

        step_send(0, 0, h)
        step_send(1, 0, h)
        core_send(0, h)

    for e in range(NZ):
        for oc in range(NC):
            if (e, oc) != (0, 0):
                arrived(sbv.at[e, oc], S_SB + e * 2 + oc)
    for d in range(1, NY):
        arrived(rowv.at[d], S_ROW + d)
    to_s = [
        pltpu.make_async_copy(sbv, sbs, lsem.at[L_SB]),
        pltpu.make_async_copy(rowv, rows, lsem.at[L_ROW]),
    ]
    for made in to_s:
        made.start()

    loc_tiles.wait()

    @pl.loop(0, 8)
    def _(i):
        k = i * 4
        prods = [dot(TL[i // 4, lax.rem(i, 4), j], Hown[src_own[0, k + j]]) for j in range(4)]
        tr = [row_own[0, k + j] for j in range(4)]
        for t in range(NB):
            add = jnp.where(tr[0] == t, prods[0], 0.0)
            for j in range(1, 4):
                add += jnp.where(tr[j] == t, prods[j], 0.0)
            agg[0, t] += add

    for made in to_s:
        made.wait()

    for k in range(2):
        e = x + 4 * k
        arrived(T.at[2, e], S_TQ + e)
        for i, dx in enumerate((1, -1, 2)):
            send(T.at[2, e], T.at[2, e], S_TF + k * 3 + i, at(dx=dx), S_TQ + e)
    for made in own_tiles:
        made.wait()

    def slot_row(dy, e, cc, cap):
        zz = lax.rem(z + DIST[e] + NZ, NZ)
        return rows[dy, 0, 32 + zz * 16 + y * 4 + cc * 2 + cap]

    def slot_block(dy, e, oc, cap):
        target = (z * NY + lax.rem(y + dy, NY)) * NC + c
        return sbs[e, oc, 0, target * 2 + cap]

    def forward(e):
        for dy, base in ((3, 0), (1, 8)):
            arrived(T.at[dy, e], S_TY + base + e)

        @pl.when(x != e % 4)
        def _():
            arrived(T.at[2, e], S_TQ + e)

        for h in range(2):
            arrived(half(hid(e, 1), h), S_HC + e * 2 + h)

        def add(oc):
            cc = lax.rem(c + oc, NC)
            for dy in range(NY):
                prods, tr = [], []
                for cap in range(CAP):
                    t, b = T[dy, e, cc * 2 + cap], slot_block(dy, e, oc, cap)
                    prods.append(dot(t, H[e][oc, b] if e else (Hown, Hcore)[oc][b]))
                    tr.append(slot_row(dy, e, cc, cap))
                for t in range(NB):
                    agg[dy, t] += jnp.where(tr[0] == t, prods[0], 0.0) + jnp.where(tr[1] == t, prods[1], 0.0)

        if e:
            pl.loop(0, NC)(add)
        else:
            for oc in range(NC):
                add(oc)

    pending = [0]
    for step in range(4):
        halves = ((0, 0), (1, 0), (0, 1), (1, 1)) if step < 3 else ((0, 0), (1, 1))
        for way, h in halves:
            d = -(step + 1) if way == 0 else step + 1
            arrived(half(hid(SLOT[d], 0), h), S_HZ + way * 8 + step * 2 + h)
            if step < 2 or (step == 2 and h == way):
                step_send(way, step + 1, h)
            core_send(SLOT[d], h)
        for e in pending:
            forward(e)
        pending = [SLOT[step + 1], SLOT[-step - 1]] if step < 3 else [SLOT[4]]
    for e in pending:
        forward(e)

    def to_bf16(dst, src, base, more=None):
        @pl.loop(0, 4)
        def _(i):
            value = src[base + i]
            if more is not None:
                value += more[i].astype(F32)
            dst[base + i] = value.astype(BF)

    to_bf16(ysend2, agg.at[2], 0)
    send(half(ysend2, 0), yrel.at[0], S_YR + 0, at(dy=1))
    to_bf16(ysend2, agg.at[2], 4)
    send(half(ysend2, 1), yrel.at[1], S_YR + 1, at(dy=-1))
    to_bf16(ysend1, agg.at[1], 4)
    send(half(ysend1, 1), half(yin.at[0], 1), S_YI + 1, at(dy=1))
    to_bf16(ysend3, agg.at[3], 0)
    send(half(ysend3, 0), half(yin.at[1], 0), S_YI + 2, at(dy=-1))
    arrived(yrel.at[0], S_YR + 0)
    to_bf16(ysend1, agg.at[1], 0, yrel.at[0])
    send(half(ysend1, 0), half(yin.at[0], 0), S_YI + 0, at(dy=1))
    arrived(yrel.at[1], S_YR + 1)
    to_bf16(ysend3, agg.at[3], 4, yrel.at[1])
    send(half(ysend3, 1), half(yin.at[1], 1), S_YI + 3, at(dy=-1))

    bsum[...] = jnp.zeros_like(bsum)
    for h in range(2):
        arrived(half(yin.at[0], h), S_YI + h)
        arrived(half(yin.at[1], h), S_YI + 2 + h)

        @pl.loop(0, 4)
        def _(b, h=h):
            i = 4 * h + b
            r = pl.ds(pl.multiple_of(i * B, B), B)
            pre = agg[0, i] + yin[0, i].astype(F32) + yin[1, i].astype(F32) + bias[...].astype(F32)
            sig = jax.nn.sigmoid(pre)
            out[r, :] = (pre * sig).astype(BF)
            g = (cot[r, :].astype(F32) * sig * (1.0 + pre * (1.0 - sig))).astype(BF).astype(F32)
            part = g[0:8]
            for j in range(1, 16):
                part += g[8 * j : 8 * j + 8]
            bsum[...] += part
            G[0][i] = g.T.astype(BF)

        send(half(G[0], h), half(G[3], h), S_G + h, at(dy=1))
        send(half(G[0], h), half(G[1], h), S_G + 2 + h, at(dy=-1))

    def spread(n, base, dst, tail):
        @pl.loop(0, 8)
        def _(j):
            r = pl.ds(pl.multiple_of(j * 16, 16), 16)
            parts = [D[k, r, :] for k in range(n)]
            for t in range(NB):
                acc = jnp.where(base[0] == t, parts[0], 0.0)
                for k in range(1, n):
                    acc += jnp.where(base[k] == t, parts[k], 0.0)
                tail(dst, t, r, acc)

    def add_f32(dst, t, r, acc):
        dst[t, r, :] += acc

    def put_f32(dst, t, r, acc):
        dst[t, r, :] = acc

    def put_bf16(dst, t, r, acc):
        dst[t, r, :] = acc.astype(BF)

    @pl.loop(0, 4)
    def _(i):
        k0 = i * 8
        for j in range(8):
            D[j] = dot(G[0][row_own[0, k0 + j]], TL[i // 2, lax.rem(i, 2) * 2 + j // 4, j % 4])
        spread(8, [src_own[0, k0 + j] for j in range(8)], SL, add_f32)

    arrived(half(G[3], 0), S_G + 0)
    send(half(G[3], 0), half(G[2], 0), S_GR + 0, at(dy=1))
    arrived(half(G[1], 1), S_G + 3)
    send(half(G[1], 1), half(G[2], 1), S_GR + 1, at(dy=-1))
    arrived(half(G[1], 0), S_G + 2)
    arrived(half(G[3], 1), S_G + 1)
    for h in range(2):
        arrived(half(G[2], h), S_GR + h)

    def backward(e, oc, dst, tail):
        cc = lax.rem(c + oc, NC)
        blocks = []
        for dy in range(NY):
            for cap in range(CAP):
                D[dy * 2 + cap] = dot(G[dy][slot_row(dy, e, cc, cap)], T[dy, e, cc * 2 + cap])
                blocks.append(slot_block(dy, e, oc, cap))
        spread(8, blocks, dst, tail)

    def combine(dst, e, h, way=None, step=None):
        @pl.loop(0, 4)
        def _(i):
            t = 4 * h + i
            value = S0[e, t] + sibrecv[e, t].astype(F32)
            if step is not None:
                value += zrecv[way, step, t].astype(F32)
            dst[t] = value.astype(BF)

    def ring_send(way, step, h):
        send(
            half(zsend.at[way, step], h), half(zrecv.at[way, step], h), S_ZR + way * 8 + step * 2 + h,
            at(dz=1 if way == 0 else -1),
        )

    def terms(e):
        backward(e, 1, sibsend.at[e], put_bf16)
        send(sibsend.at[e], sibrecv.at[e], S_SIB + e, at(oc=1))
        backward(e, 0, S0.at[e], put_f32)

    terms(SLOT[4])
    arrived(sibrecv.at[SLOT[4]], S_SIB + SLOT[4])
    for way in range(2):
        combine(zsend.at[way, 0], SLOT[4], way)
        ring_send(way, 0, way)
    for step in range(1, 4):
        d = 4 - step
        ends = (SLOT[d], SLOT[-d])
        for e in ends:
            terms(e)
        for e in ends:
            arrived(sibrecv.at[e], S_SIB + e)
        for h in range(2):
            for way, e in enumerate(ends):
                came = step > 1 or h == way
                if came:
                    arrived(half(zrecv.at[way, step - 1], h), S_ZR + way * 8 + (step - 1) * 2 + h)
                combine(zsend.at[way, step], e, h, way, step - 1 if came else None)
                ring_send(way, step, h)
    terms(0)
    arrived(sibrecv.at[0], S_SIB + 0)

    for h in range(2):
        for way in range(2):
            arrived(half(zrecv.at[way, 3], h), S_ZR + way * 8 + 6 + h)

        @pl.loop(0, 4)
        def _(i, h=h):
            t = 4 * h + i
            value = S0[0, t] + sibrecv[0, t].astype(F32) + SL[t]
            value += zrecv[0, 3, t].astype(F32) + zrecv[1, 3, t].astype(F32)
            value = value.astype(BF).astype(F32)
            GAT[:, pl.ds(pl.multiple_of(t * B, B), B)] = value.astype(BF)
            GA[pl.ds(pl.multiple_of(t * B, B), B), :] = value.T.astype(BF)

    for dx in range(NX):
        part = dot(GAT[...], F[dx]).T
        for j in range(4):
            k = lax.rem(x + dx, NX) * 4 + j
            arsend[k, 0:32, :] = part[32 * j : 32 * j + 32]
    for k in range(16):
        arsend[k, 32:40, :] = bsum[...]
    me = z * NC + c
    for e in range(NZ):
        for oc in range(NC):
            if (e, oc) != (0, 0):
                k = lax.rem(z + DIST[e] + NZ, NZ) * NC + lax.rem(c + oc, NC)
                back = SLOT[-DIST[e]]
                send(arsend.at[k], arin.at[me], S_A1 + back * 2 + oc, at(dz=DIST[e], oc=oc))
    arin[me] = arsend[me]

    def terms_x(dx, h, dst, more=None):
        @pl.loop(0, 4)
        def _(b):
            r = pl.ds(pl.multiple_of(512 * h + b * B, B), B)
            value = dot_t(GA[r, :], w_rows(dx))
            if more is not None:
                value += more[pl.ds(pl.multiple_of(b * B, B), B), :].astype(F32)
            dst[r, :] = value.astype(dst.dtype)

    terms_x(2, 0, xsend2)
    send(xsend2.at[rows_of(0)], xrel.at[0], S_XR + 0, at(dx=1))
    terms_x(2, 1, xsend2)
    send(xsend2.at[rows_of(1)], xrel.at[1], S_XR + 1, at(dx=-1))
    terms_x(1, 1, xsend1)
    send(xsend1.at[rows_of(1)], xin.at[0, rows_of(1)], S_XI + 1, at(dx=1))
    terms_x(3, 0, xsend3)
    send(xsend3.at[rows_of(0)], xin.at[1, rows_of(0)], S_XI + 2, at(dx=-1))
    arrived(xrel.at[0], S_XR + 0)
    terms_x(1, 0, xsend1, xrel.at[0])
    send(xsend1.at[rows_of(0)], xin.at[0, rows_of(0)], S_XI + 0, at(dx=1))
    arrived(xrel.at[1], S_XR + 1)
    terms_x(3, 1, xsend3, xrel.at[1])
    send(xsend3.at[rows_of(1)], xin.at[1, rows_of(1)], S_XI + 3, at(dx=-1))
    for h in range(2):
        terms_x(0, h, PT)

    for e in range(NZ):
        for oc in range(NC):
            if (e, oc) != (0, 0):
                k = lax.rem(z + DIST[e] + NZ, NZ) * NC + lax.rem(c + oc, NC)
                arrived(arin.at[k], S_A1 + e * 2 + oc)
    total = arin[0]
    for k in range(1, 16):
        total += arin[k]
    red[...] = total
    for d in range(1, NY):
        send(red, ar2in.at[y], S_A2 + NY - d, at(dy=d))
    ar2in[y] = red[...]
    for d in range(1, NY):
        arrived(ar2in.at[lax.rem(y + d, NY)], S_A2 + d)
    total = ar2in[0] + ar2in[1] + ar2in[2] + ar2in[3]
    gb[...] = jnp.sum(total[32:40], 0, keepdims=True)
    gwall[me] = total[0:32]
    for e in range(NZ):
        for oc in range(NC):
            if (e, oc) != (0, 0):
                back = SLOT[-DIST[e]]
                send(gwall.at[me], gwall.at[me], S_A3 + back * 2 + oc, at(dz=DIST[e], oc=oc))

    for h in range(2):
        arrived(xin.at[0, rows_of(h)], S_XI + h)
        arrived(xin.at[1, rows_of(h)], S_XI + 2 + h)

        @pl.loop(0, 4)
        def _(b, h=h):
            r = pl.ds(pl.multiple_of(512 * h + b * B, B), B)
            gin[r, :] = (PT[r, :] + xin[0, r, :].astype(F32) + xin[1, r, :].astype(F32)).astype(BF)

    for e in range(NZ):
        for oc in range(NC):
            if (e, oc) != (0, 0):
                k = lax.rem(z + DIST[e] + NZ, NZ) * NC + lax.rem(c + oc, NC)
                arrived(gwall.at[k], S_A3 + e * 2 + oc)
    for k in range(16):
        gw[32 * k : 32 * k + 32, :] = gwall[k]

    for made in started:
        made.wait_send()


def shards(
    features, weight, bias, cotangent, tile_vals, tile_row, tile_src, send_blocks, send_count
):
    blocks = lambda *lead, dtype=BF: pltpu.VMEM((*lead, B, B), dtype)
    scratch = [
        pltpu.VMEM((NX, 1024, B), BF),
        blocks(NB),
        blocks(NB),
        *[blocks(NC, NB) for _ in range(NZ - 1)],
        blocks(NY, NZ, 4),
        blocks(2, 4, 4),
        blocks(NY, NB, dtype=F32),
        blocks(NB),
        blocks(NB),
        blocks(NB),
        blocks(2, 4),
        blocks(2, NB),
        *[blocks(NB + 1) for _ in range(NY)],
        blocks(8, dtype=F32),
        blocks(NZ, NB, dtype=F32),
        blocks(NB, dtype=F32),
        blocks(2, 4, NB),
        blocks(2, 4, NB),
        blocks(NZ, NB),
        blocks(NZ, NB),
        pltpu.VMEM((B, 1024), BF),
        pltpu.VMEM((1024, B), BF),
        pltpu.VMEM((1024, B), F32),
        pltpu.VMEM((1024, B), BF),
        pltpu.VMEM((1024, B), BF),
        pltpu.VMEM((1024, B), BF),
        pltpu.VMEM((2, 512, B), BF),
        pltpu.VMEM((2, 1024, B), BF),
        pltpu.VMEM((8, B), F32),
        pltpu.VMEM((16, 40, B), F32),
        pltpu.VMEM((16, 40, B), F32),
        pltpu.VMEM((NY, 40, B), F32),
        pltpu.VMEM((40, B), F32),
        pltpu.VMEM((16, 32, B), F32),
        pltpu.VMEM((NZ, NC, 1, 128), jnp.int32),
        pltpu.VMEM((NY, 1, 256), jnp.int32),
        pltpu.SMEM((NZ, NC, 1, 128), jnp.int32),
        pltpu.SMEM((NY, 1, 256), jnp.int32),
        pltpu.SemaphoreType.DMA((S_SEND,)),
        pltpu.SemaphoreType.DMA((S_RECV,)),
        pltpu.SemaphoreType.DMA((L_N + NZ,)),
    ]
    vmem = pl.BlockSpec(memory_space=pltpu.VMEM)
    smem = pl.BlockSpec(memory_space=pltpu.SMEM)
    out, gin, gw, gb = pl.pallas_call(
        kernel,
        out_shape=(
            jax.ShapeDtypeStruct((1024, B), BF),
            jax.ShapeDtypeStruct((1024, B), BF),
            jax.ShapeDtypeStruct((512, B), F32),
            jax.ShapeDtypeStruct((1, B), F32),
        ),
        in_specs=[vmem] * 4 + [pl.BlockSpec(memory_space=pl.ANY)] + [vmem] * 2 + [smem] * 2,
        out_specs=(vmem,) * 4,
        scratch_shapes=scratch,
        compiler_params=pltpu.CompilerParams(
            collective_id=0, has_side_effects=True, vmem_limit_bytes=56 * 2**20
        ),
    )(
        features,
        weight,
        bias.reshape(1, B),
        cotangent,
        tile_vals.reshape(10, 4, 4, B, B),
        send_blocks.reshape(1, 128),
        jnp.pad(tile_row, ((0, 0), (0, 96)), constant_values=NB),
        tile_row,
        tile_src,
    )
    return out, gin, gw, gb.reshape(B)


def solution(mesh):
    in_specs = (
        P("dom", "rep"),
        P(None, "rep"),
        P("rep"),
        P("dom", "rep"),
        P("dom", None, None, None),
        P("dom", None),
        P("dom", None),
        P("dom", None, None),
        P("dom", None),
    )
    out_specs = (P("dom", "rep"), P("dom", "rep"), P(None, "rep"), P("rep"))
    return jax.shard_map(shards, mesh=mesh, in_specs=in_specs, out_specs=out_specs, check_vma=False)
```

```python
import jax
import jax.numpy as jnp
from jax import lax
from jax.experimental import pallas as pl
from jax.experimental.pallas import tpu as pltpu
from jax.sharding import PartitionSpec as P

B = 128
NB = 8
CAP = 2
NX, NY, NZ, NC = 4, 4, 8, 2
MESH = pl.DeviceIdType.MESH
BF = jnp.bfloat16
F32 = jnp.float32

DIST = [0, 1, -1, 2, -2, 3, -3, 4]
SLOT = {d: e for e, d in enumerate(DIST)}
SLOT[-4] = SLOT[4]


def dot(a, b):
    return lax.dot_general(a, b, (((1,), (0,)), ((), ())), preferred_element_type=F32)


def dot_t(a, b):
    return lax.dot_general(a, b, (((1,), (1,)), ((), ())), preferred_element_type=F32)


class Semaphores:
    def __init__(self):
        self.n = 0

    def take(self, count):
        first = self.n
        self.n += count
        return first


S = Semaphores()
S_FEAT = S.take(4)
S_FREL = S.take(2)
S_SB = S.take(8)
S_ROW = S.take(4)
S_TY = S.take(16)
S_TQ = S.take(8)
S_HZ = S.take(16)
S_HC = S.take(16)
S_YR = S.take(2)
S_YI = S.take(4)
S_G = S.take(4)
S_GR = S.take(2)
S_SIB = S.take(8)
S_ZR = S.take(16)
S_XR = S.take(2)
S_XI = S.take(4)
S_SBC = S.take(1)
S_TR = S.take(1)
S_A0 = S.take(1)
S_A1 = S.take(8)
S_A2 = S.take(4)
S_A3 = S.take(8)
S_A4 = S.take(1)
S_RECV = S.n
S_TF = S.take(7)
S_SEND = S.n
L_LOC, L_SB, L_ROW, L_FEAT, L_W, L_COT, L_BIAS, L_OUT, L_GIN, L_GW, L_GB, L_N = 0, 1, 2, 3, 4, 5, 6, 7, 9, 11, 12, 13


def kernel(
    feat, weight, bias, cot, tiles, sendb, trow, row_own, src_own,
    out, gin, gw, gb,
    F, Hown, Hcore, H1, H2, H3, H4, H5, H6, H7, T, TL, trel, agg, ysend2, ysend1, ysend3, yrel, yin, G0, G1, G2, G3, D, S0, SL,
    zsend, zrecv, sibsend, sibrecv, GAT, GA, PT, xsend2, xsend1, xsend3, xrel, xin, bsum, gws, arc, arsend, arin, ar2in, red, gwall,
    wv, cv, bv, ov, giv, gbv, sbv, rowv, sbs, rows, ssem, rsem, lsem,
):
    H = [None, H1, H2, H3, H4, H5, H6, H7]
    G = [G0, G1, G2, G3]

    def hid(e, oc):
        return H[e].at[oc] if e else (Hown, Hcore)[oc]

    dom, x = lax.axis_index("dom"), lax.axis_index("rep")
    z = dom // (NY * NC)
    y = lax.rem(dom // NC, NY)
    c = lax.rem(dom, NC)

    def at(dx=0, dy=0, dz=0, oc=0):
        zz = lax.rem(z + dz + NZ, NZ)
        yy = lax.rem(y + dy + NY, NY)
        cc = lax.rem(c + oc, NC)
        return ((zz * NY + yy) * NC + cc, lax.rem(x + dx + NX, NX))

    started = []

    def copy(src, dst, sem, dev, recv=None):
        return pltpu.make_async_remote_copy(
            src_ref=src,
            dst_ref=dst,
            send_sem=ssem.at[sem],
            recv_sem=rsem.at[sem if recv is None else recv],
            device_id=dev,
            device_id_type=MESH,
        )

    def send(src, dst, sem, dev, recv=None):
        made = copy(src, dst, sem, dev, recv)
        made.start()
        started.append(made)

    here = (dom, x)

    def arrived(dst, sem):
        pltpu.make_async_remote_copy(
            src_ref=dst, dst_ref=dst, send_sem=ssem.at[0], recv_sem=rsem.at[sem], device_id=here, device_id_type=MESH
        ).wait_recv()

    half = lambda ref, h: ref.at[pl.ds(4 * h, 4)]

    def local(src, dst, sem):
        made = pltpu.make_async_copy(src, dst, lsem.at[sem])
        made.start()
        return made

    feat_in = local(feat, F.at[0], L_FEAT)
    weight_in = local(weight, wv, L_W)
    loc_tiles = local(tiles.at[pl.ds(0, 2)], TL, L_LOC)
    own_tiles = [
        local(tiles.at[2 + lax.rem(z + DIST[e] + NZ, NZ), y], T.at[0, e], L_N + e) for e in range(NZ)
    ]
    cot_in = local(cot, cv, L_COT)
    bias_in = local(bias, bv, L_BIAS)

    barrier = pltpu.get_barrier_semaphore()
    peers = [at(dz=DIST[e]) for e in range(1, NZ)] + [at(oc=1)]
    peers += [at(dy=d) for d in range(1, NY)] + [at(dx=d) for d in range(1, NX)]
    for dev in peers:
        pl.semaphore_signal(barrier, inc=1, device_id=dev, device_id_type=MESH)
    pl.semaphore_wait(barrier, len(peers))

    rows_of = lambda h: pl.ds(512 * h, 512)
    for h, g in ((0, 1), (1, 0)):
        send(feat.at[rows_of(h)], F.at[3, rows_of(h)], S_FEAT + h, at(dx=1))
        send(feat.at[rows_of(g)], F.at[1, rows_of(g)], S_FEAT + 2 + g, at(dx=-1))
    for e in range(1, NZ):
        back = SLOT[-DIST[e]]
        send(sendb, sbv.at[0, back], S_SB + back, at(dz=DIST[e]))
    for d in range(1, NY):
        send(trow, rowv.at[NY - d], S_ROW + NY - d, at(dy=d))
    sb_in = local(sendb, sbv.at[0, 0], L_SB)
    row_in = local(trow, rowv.at[0], L_ROW)

    def tile_slot(e):
        d = jnp.where(lax.rem(e, 2) == 1, (e + 1) // 2, NZ - e // 2)
        return 2 + lax.rem(z + d, NZ)

    far = lax.rem(y + 2, NY)
    send(tiles.at[tile_slot(x), far], T.at[2, x], S_TF + 6, at(dy=2), S_TQ + x)
    send(tiles.at[tile_slot(x + 4), far], trel, S_TR, at(dy=-1))
    for e in range(NZ):
        for dy, to, base in ((1, 3, 0), (-1, 1, 8)):
            send(
                tiles.at[2 + lax.rem(z + DIST[e] + NZ, NZ), lax.rem(y + dy + NY, NY)],
                T.at[to, e],
                S_TY + base + e,
                at(dy=dy),
            )

    for dy in range(NY):
        G[dy][NB] = jnp.zeros((B, B), BF)

    @pl.loop(0, NB)
    def _(i):
        for dy in range(NY):
            agg[dy, i] = jnp.zeros((B, B), F32)
        SL[i] = jnp.zeros((B, B), F32)

    arrived(F.at[3, rows_of(0)], S_FEAT + 0)
    send(F.at[3, rows_of(0)], F.at[2, rows_of(0)], S_FREL + 0, at(dx=1))
    arrived(F.at[1, rows_of(1)], S_FEAT + 3)
    send(F.at[1, rows_of(1)], F.at[2, rows_of(1)], S_FREL + 1, at(dx=-1))
    arrived(F.at[1, rows_of(0)], S_FEAT + 2)
    arrived(F.at[3, rows_of(1)], S_FEAT + 1)

    def w_rows(dx):
        return wv[pl.ds(pl.multiple_of(lax.rem(x + dx, NX) * B, B), B), :]

    def step_send(way, step, h):
        d = -step if way == 0 else step
        nd = d - 1 if way == 0 else d + 1
        send(
            half(hid(SLOT[d], 0), h), half(hid(SLOT[nd], 0), h), S_HZ + way * 8 + step * 2 + h,
            at(dz=1 if way == 0 else -1),
        )

    def core_send(e, h):
        send(half(hid(e, 0), h), half(hid(e, 1), h), S_HC + e * 2 + h, at(oc=1))

    feat_in.wait()
    weight_in.wait()
    for h in range(2):
        arrived(F.at[2, rows_of(h)], S_FREL + h)

        @pl.loop(0, 4)
        def _(b, h=h):
            r = pl.ds(pl.multiple_of(512 * h + b * B, B), B)
            acc = dot(F[0, r], w_rows(0))
            for dx in range(1, NX):
                acc += dot(F[dx, r], w_rows(dx))
            Hown[4 * h + b] = acc.astype(BF)

        step_send(0, 0, h)
        step_send(1, 0, h)
        core_send(0, h)

    sb_in.wait()
    row_in.wait()
    for e in range(1, NZ):
        arrived(sbv.at[0, e], S_SB + e)
    send(sbv.at[0], sbv.at[1], S_SBC, at(oc=1))
    for d in range(1, NY):
        arrived(rowv.at[d], S_ROW + d)

    arrived(trel, S_TR)
    send(trel, T.at[2, x + 4], S_TQ, at(dy=-1), S_TQ + x + 4)
    arrived(sbv.at[1], S_SBC)
    to_s = [local(sbv, sbs, L_SB), local(rowv, rows, L_ROW)]

    loc_tiles.wait()

    @pl.loop(0, 8)
    def _(i):
        k = i * 4
        prods = [dot(TL[i // 4, lax.rem(i, 4), j], Hown[src_own[0, k + j]]) for j in range(4)]
        tr = [row_own[0, k + j] for j in range(4)]
        for t in range(NB):
            add = jnp.where(tr[0] == t, prods[0], 0.0)
            for j in range(1, 4):
                add += jnp.where(tr[j] == t, prods[j], 0.0)
            agg[0, t] += add

    for made in to_s:
        made.wait()

    for k in range(2):
        e = x + 4 * k
        arrived(T.at[2, e], S_TQ + e)
        for i, dx in enumerate((1, -1, 2)):
            send(T.at[2, e], T.at[2, e], S_TF + k * 3 + i, at(dx=dx), S_TQ + e)
    for made in own_tiles:
        made.wait()

    def slot_row(dy, e, cc, cap):
        zz = lax.rem(z + DIST[e] + NZ, NZ)
        return rows[dy, 0, 32 + zz * 16 + y * 4 + cc * 2 + cap]

    def slot_block(dy, e, oc, cap):
        target = (z * NY + lax.rem(y + dy, NY)) * NC + c
        return sbs[oc, e, cap, target]

    def forward(e):
        for dy, base in ((3, 0), (1, 8)):
            arrived(T.at[dy, e], S_TY + base + e)

        @pl.when(x != e % 4)
        def _():
            arrived(T.at[2, e], S_TQ + e)

        for h in range(2):
            arrived(half(hid(e, 1), h), S_HC + e * 2 + h)

        def add(oc, dys=range(NY)):
            cc = lax.rem(c + oc, NC)
            for dy in dys:
                prods, tr = [], []
                for cap in range(CAP):
                    t, b = T[dy, e, cc * 2 + cap], slot_block(dy, e, oc, cap)
                    prods.append(dot(t, H[e][oc, b] if e else (Hown, Hcore)[oc][b]))
                    tr.append(slot_row(dy, e, cc, cap))
                for t in range(NB):
                    agg[dy, t] += jnp.where(tr[0] == t, prods[0], 0.0) + jnp.where(tr[1] == t, prods[1], 0.0)

        if e == SLOT[4]:
            return add
        if e:
            pl.loop(0, NC)(add)
        else:
            for oc in range(NC):
                add(oc)

    pending = [0]
    for step in range(4):
        halves = ((0, 0), (1, 0), (0, 1), (1, 1)) if step < 3 else ((0, 0), (1, 1))
        for way, h in halves:
            d = -(step + 1) if way == 0 else step + 1
            arrived(half(hid(SLOT[d], 0), h), S_HZ + way * 8 + step * 2 + h)
            if step < 2 or (step == 2 and h == way):
                step_send(way, step + 1, h)
            core_send(SLOT[d], h)
        for e in pending:
            forward(e)
        pending = [SLOT[step + 1], SLOT[-step - 1]] if step < 3 else [SLOT[4]]
    last = forward(SLOT[4])

    def to_bf16(dst, src, base, more=None):
        @pl.loop(0, 4)
        def _(i):
            value = src[base + i]
            if more is not None:
                value += more[i].astype(F32)
            dst[base + i] = value.astype(BF)

    for oc in range(NC):
        last(oc, (2,))
    to_bf16(ysend2, agg.at[2], 0)
    send(half(ysend2, 0), yrel.at[0], S_YR + 0, at(dy=1))
    to_bf16(ysend2, agg.at[2], 4)
    send(half(ysend2, 1), yrel.at[1], S_YR + 1, at(dy=-1))
    for oc in range(NC):
        last(oc, (1, 3))
    to_bf16(ysend1, agg.at[1], 4)
    send(half(ysend1, 1), half(yin.at[0], 1), S_YI + 1, at(dy=1))
    to_bf16(ysend3, agg.at[3], 0)
    send(half(ysend3, 0), half(yin.at[1], 0), S_YI + 2, at(dy=-1))
    arrived(yrel.at[0], S_YR + 0)
    to_bf16(ysend1, agg.at[1], 0, yrel.at[0])
    send(half(ysend1, 0), half(yin.at[0], 0), S_YI + 0, at(dy=1))
    arrived(yrel.at[1], S_YR + 1)
    to_bf16(ysend3, agg.at[3], 4, yrel.at[1])
    send(half(ysend3, 1), half(yin.at[1], 1), S_YI + 3, at(dy=-1))
    for oc in range(NC):
        last(oc, (0,))

    bsum[...] = jnp.zeros_like(bsum)
    cot_in.wait()
    bias_in.wait()
    leaving = []
    for h in range(2):
        arrived(half(yin.at[0], h), S_YI + h)
        arrived(half(yin.at[1], h), S_YI + 2 + h)

        @pl.loop(0, 4)
        def _(b, h=h):
            i = 4 * h + b
            r = pl.ds(pl.multiple_of(i * B, B), B)
            pre = agg[0, i] + yin[0, i].astype(F32) + yin[1, i].astype(F32) + bv[...].astype(F32)
            sig = jax.nn.sigmoid(pre)
            ov[r, :] = (pre * sig).astype(BF)
            g = (cv[r, :].astype(F32) * sig * (1.0 + pre * (1.0 - sig))).astype(BF).astype(F32)
            part = g[0:8]
            for j in range(1, 16):
                part += g[8 * j : 8 * j + 8]
            bsum[...] += part
            G[0][i] = g.T.astype(BF)

        send(half(G[0], h), half(G[3], h), S_G + h, at(dy=1))
        send(half(G[0], h), half(G[1], h), S_G + 2 + h, at(dy=-1))
        leaving.append(local(ov.at[rows_of(h)], out.at[rows_of(h)], L_OUT + h))

    def spread(n, base, dst, tail):
        @pl.loop(0, 8)
        def _(j):
            r = pl.ds(pl.multiple_of(j * 16, 16), 16)
            parts = [D[k, r, :] for k in range(n)]
            for t in range(NB):
                acc = jnp.where(base[0] == t, parts[0], 0.0)
                for k in range(1, n):
                    acc += jnp.where(base[k] == t, parts[k], 0.0)
                tail(dst, t, r, acc)

    def add_f32(dst, t, r, acc):
        dst[t, r, :] += acc

    def put_f32(dst, t, r, acc):
        dst[t, r, :] = acc

    def put_bf16(dst, t, r, acc):
        dst[t, r, :] = acc.astype(BF)

    @pl.loop(0, 4)
    def _(i):
        k0 = i * 8
        for j in range(8):
            D[j] = dot(G[0][row_own[0, k0 + j]], TL[i // 2, lax.rem(i, 2) * 2 + j // 4, j % 4])
        spread(8, [src_own[0, k0 + j] for j in range(8)], SL, add_f32)

    arrived(half(G[3], 0), S_G + 0)
    send(half(G[3], 0), half(G[2], 0), S_GR + 0, at(dy=1))
    arrived(half(G[1], 1), S_G + 3)
    send(half(G[1], 1), half(G[2], 1), S_GR + 1, at(dy=-1))
    arrived(half(G[1], 0), S_G + 2)
    arrived(half(G[3], 1), S_G + 1)
    for h in range(2):
        arrived(half(G[2], h), S_GR + h)

    def backward(e, oc, dst, tail):
        cc = lax.rem(c + oc, NC)
        blocks = []
        for dy in range(NY):
            for cap in range(CAP):
                D[dy * 2 + cap] = dot(G[dy][slot_row(dy, e, cc, cap)], T[dy, e, cc * 2 + cap])
                blocks.append(slot_block(dy, e, oc, cap))
        spread(8, blocks, dst, tail)

    def combine(dst, e, h, way=None, step=None):
        @pl.loop(0, 4)
        def _(i):
            t = 4 * h + i
            value = S0[e, t] + sibrecv[e, t].astype(F32)
            if step is not None:
                value += zrecv[way, step, t].astype(F32)
            dst[t] = value.astype(BF)

    def ring_send(way, step, h):
        send(
            half(zsend.at[way, step], h), half(zrecv.at[way, step], h), S_ZR + way * 8 + step * 2 + h,
            at(dz=1 if way == 0 else -1),
        )

    def terms(e):
        backward(e, 1, sibsend.at[e], put_bf16)
        send(sibsend.at[e], sibrecv.at[e], S_SIB + e, at(oc=1))
        backward(e, 0, S0.at[e], put_f32)

    terms(SLOT[4])
    arrived(sibrecv.at[SLOT[4]], S_SIB + SLOT[4])
    for way in range(2):
        combine(zsend.at[way, 0], SLOT[4], way)
        ring_send(way, 0, way)
    for step in range(1, 4):
        d = 4 - step
        ends = (SLOT[d], SLOT[-d])
        for e in ends:
            terms(e)
        for e in ends:
            arrived(sibrecv.at[e], S_SIB + e)
        order = ((1, 0), (0, 1), (0, 0), (1, 1)) if step == 1 else ((0, 0), (1, 0), (0, 1), (1, 1))
        for way, h in order:
            came = step > 1 or h == way
            if came:
                arrived(half(zrecv.at[way, step - 1], h), S_ZR + way * 8 + (step - 1) * 2 + h)
            combine(zsend.at[way, step], ends[way], h, way, step - 1 if came else None)
            ring_send(way, step, h)
    terms(0)
    arrived(sibrecv.at[0], S_SIB + 0)

    def terms_x(dx, h, dst, more=None):
        @pl.loop(0, 4)
        def _(b):
            r = pl.ds(pl.multiple_of(512 * h + b * B, B), B)
            value = dot_t(GA[r, :], w_rows(dx))
            if more is not None:
                value += more[pl.ds(pl.multiple_of(b * B, B), B), :].astype(F32)
            dst[r, :] = value.astype(dst.dtype)

    for h in range(2):
        for way in range(2):
            arrived(half(zrecv.at[way, 3], h), S_ZR + way * 8 + 6 + h)

        @pl.loop(0, 4)
        def _(i, h=h):
            t = 4 * h + i
            value = S0[0, t] + sibrecv[0, t].astype(F32) + SL[t]
            value += zrecv[0, 3, t].astype(F32) + zrecv[1, 3, t].astype(F32)
            value = value.astype(BF).astype(F32)
            GAT[:, pl.ds(pl.multiple_of(t * B, B), B)] = value.astype(BF)
            GA[pl.ds(pl.multiple_of(t * B, B), B), :] = value.T.astype(BF)

        if h == 0:
            terms_x(2, 0, xsend2)
            send(xsend2.at[rows_of(0)], xrel.at[0], S_XR + 0, at(dx=1))
            terms_x(3, 0, xsend3)
            send(xsend3.at[rows_of(0)], xin.at[1, rows_of(0)], S_XI + 2, at(dx=-1))

    for dx in range(NX):
        k = lax.rem(x + dx, NX)
        gws[k // 2, pl.ds(pl.multiple_of(lax.rem(k, 2) * B, B), B), :] = dot(GAT[...], F[dx]).T
    for k in range(NC):
        gws[k, 256:264, :] = bsum[...]
    send(gws.at[1 - c], arc, S_A0, at(oc=1))
    terms_x(2, 1, xsend2)
    send(xsend2.at[rows_of(1)], xrel.at[1], S_XR + 1, at(dx=-1))
    terms_x(1, 1, xsend1)
    send(xsend1.at[rows_of(1)], xin.at[0, rows_of(1)], S_XI + 1, at(dx=1))

    arrived(arc, S_A0)
    for k in range(NZ):
        arsend[k, 0:32, :] = gws[c, 32 * k : 32 * k + 32, :] + arc[32 * k : 32 * k + 32, :]
        arsend[k, 32:40, :] = gws[c, 256:264, :] + arc[256:264, :]
    for e in range(NZ - 1, 0, -1):
        send(arsend.at[lax.rem(z + DIST[e] + NZ, NZ)], arin.at[z], S_A1 + SLOT[-DIST[e]], at(dz=DIST[e]))
    arin[z] = arsend[z]

    arrived(xrel.at[0], S_XR + 0)
    terms_x(1, 0, xsend1, xrel.at[0])
    send(xsend1.at[rows_of(0)], xin.at[0, rows_of(0)], S_XI + 0, at(dx=1))
    arrived(xrel.at[1], S_XR + 1)
    terms_x(3, 1, xsend3, xrel.at[1])
    send(xsend3.at[rows_of(1)], xin.at[1, rows_of(1)], S_XI + 3, at(dx=-1))

    for e in range(1, NZ):
        arrived(arin.at[lax.rem(z + DIST[e] + NZ, NZ)], S_A1 + e)
    total = arin[0]
    for k in range(1, NZ):
        total += arin[k]
    red[...] = total
    for d in range(1, NY):
        send(red, ar2in.at[y], S_A2 + NY - d, at(dy=d))
    ar2in[y] = red[...]
    for h in range(2):
        terms_x(0, h, PT)
    for d in range(1, NY):
        arrived(ar2in.at[lax.rem(y + d, NY)], S_A2 + d)
    total = ar2in[0] + ar2in[1] + ar2in[2] + ar2in[3]
    gbv[...] = jnp.sum(total[32:40], 0, keepdims=True)
    leaving.append(local(gbv, gb, L_GB))
    gwall[c, z] = total[0:32]
    for e in range(NZ - 1, 0, -1):
        send(gwall.at[c, z], gwall.at[c, z], S_A3 + SLOT[-DIST[e]], at(dz=DIST[e]))

    for h in range(2):
        arrived(xin.at[0, rows_of(h)], S_XI + h)
        arrived(xin.at[1, rows_of(h)], S_XI + 2 + h)

        @pl.loop(0, 4)
        def _(b, h=h):
            r = pl.ds(pl.multiple_of(512 * h + b * B, B), B)
            giv[r, :] = (PT[r, :] + xin[0, r, :].astype(F32) + xin[1, r, :].astype(F32)).astype(BF)

        leaving.append(local(giv.at[rows_of(h)], gin.at[rows_of(h)], L_GIN + h))

    for e in range(1, NZ):
        arrived(gwall.at[c, lax.rem(z + DIST[e] + NZ, NZ)], S_A3 + e)
    send(gwall.at[c], gwall.at[c], S_A4, at(oc=1))
    arrived(gwall.at[1 - c], S_A4)
    leaving.append(local(gwall, gw, L_GW))
    for made in leaving:
        made.wait()
    for made in started:
        made.wait_send()


def hand_over(*refs):
    sem = refs[-1]
    copies = [pltpu.make_async_copy(refs[i], refs[4 + i], sem.at[i]) for i in range(4)]
    for made in copies:
        made.start()
    for made in copies:
        made.wait()


def shards(
    features, weight, bias, cotangent, tile_vals, tile_row, tile_src, send_blocks, send_count
):
    blocks = lambda *lead, dtype=BF: pltpu.VMEM((*lead, B, B), dtype)
    scratch = [
        pltpu.VMEM((NX, 1024, B), BF),
        blocks(NB),
        blocks(NB),
        *[blocks(NC, NB) for _ in range(NZ - 1)],
        blocks(NY, NZ, 4),
        blocks(2, 4, 4),
        blocks(4),
        blocks(NY, NB, dtype=F32),
        blocks(NB),
        blocks(NB),
        blocks(NB),
        blocks(2, 4),
        blocks(2, NB),
        *[blocks(NB + 1) for _ in range(NY)],
        blocks(8, dtype=F32),
        blocks(NZ, NB, dtype=F32),
        blocks(NB, dtype=F32),
        blocks(2, 4, NB),
        blocks(2, 4, NB),
        blocks(NZ, NB),
        blocks(NZ, NB),
        pltpu.VMEM((B, 1024), BF),
        pltpu.VMEM((1024, B), BF),
        pltpu.VMEM((1024, B), F32),
        pltpu.VMEM((1024, B), BF),
        pltpu.VMEM((1024, B), BF),
        pltpu.VMEM((1024, B), BF),
        pltpu.VMEM((2, 512, B), BF),
        pltpu.VMEM((2, 1024, B), BF),
        pltpu.VMEM((8, B), F32),
        pltpu.VMEM((NC, 264, B), F32),
        pltpu.VMEM((264, B), F32),
        pltpu.VMEM((NZ, 40, B), F32),
        pltpu.VMEM((NZ, 40, B), F32),
        pltpu.VMEM((NY, 40, B), F32),
        pltpu.VMEM((40, B), F32),
        pltpu.VMEM((NC, NZ, 32, B), F32),
        pltpu.VMEM((512, B), BF),
        pltpu.VMEM((1024, B), BF),
        pltpu.VMEM((1, B), BF),
        pltpu.VMEM((1024, B), BF),
        pltpu.VMEM((1024, B), BF),
        pltpu.VMEM((1, B), F32),
        pltpu.VMEM((NC, NZ, CAP, 64), jnp.int32),
        pltpu.VMEM((NY, 1, 160), jnp.int32),
        pltpu.SMEM((NC, NZ, CAP, 64), jnp.int32),
        pltpu.SMEM((NY, 1, 160), jnp.int32),
        pltpu.SemaphoreType.DMA((S_SEND,)),
        pltpu.SemaphoreType.DMA((S_RECV,)),
        pltpu.SemaphoreType.DMA((L_N + NZ,)),
    ]
    anywhere = pl.BlockSpec(memory_space=pl.ANY)
    smem = pl.BlockSpec(memory_space=pltpu.SMEM)
    shapes = (
        jax.ShapeDtypeStruct((1024, B), BF),
        jax.ShapeDtypeStruct((1024, B), BF),
        jax.ShapeDtypeStruct((NC, NZ, 32, B), F32),
        jax.ShapeDtypeStruct((1, B), F32),
    )
    results = pl.pallas_call(
        kernel,
        out_shape=shapes,
        in_specs=[anywhere] * 7 + [smem] * 2,
        out_specs=(anywhere,) * 4,
        scratch_shapes=scratch,
        compiler_params=pltpu.CompilerParams(
            collective_id=0, has_side_effects=True, vmem_limit_bytes=56 * 2**20
        ),
    )(
        features,
        weight,
        bias.reshape(1, B),
        cotangent,
        tile_vals.reshape(10, 4, 4, B, B),
        send_blocks.transpose(0, 2, 1).reshape(CAP, 64),
        tile_row,
        tile_row,
        tile_src,
    )
    out, gin, gw, gb = pl.pallas_call(
        hand_over,
        out_shape=shapes,
        in_specs=[anywhere] * 4,
        out_specs=(anywhere,) * 4,
        scratch_shapes=[pltpu.SemaphoreType.DMA((4,))],
    )(*results)
    return out, gin, gw.reshape(512, B), gb.reshape(B)


def solution(mesh):
    in_specs = (
        P("dom", "rep"),
        P(None, "rep"),
        P("rep"),
        P("dom", "rep"),
        P("dom", None, None, None),
        P("dom", None),
        P("dom", None),
        P("dom", None, None),
        P("dom", None),
    )
    out_specs = (P("dom", "rep"), P("dom", "rep"), P(None, "rep"), P("rep"))
    return jax.shard_map(shards, mesh=mesh, in_specs=in_specs, out_specs=out_specs, check_vma=False)
```

```python
import jax
import jax.numpy as jnp
from jax import lax
from jax.experimental import pallas as pl
from jax.experimental.pallas import tpu as pltpu
from jax.sharding import PartitionSpec as P

B = 128
NB = 8
CAP = 2
NX, NY, NZ, NC = 4, 4, 8, 2
MESH = pl.DeviceIdType.MESH
BF = jnp.bfloat16
F32 = jnp.float32

DIST = [0, 1, -1, 2, -2, 3, -3, 4]
SLOT = {d: e for e, d in enumerate(DIST)}
SLOT[-4] = SLOT[4]


def dot(a, b):
    return lax.dot_general(a, b, (((1,), (0,)), ((), ())), preferred_element_type=F32)


def dot_t(a, b):
    return lax.dot_general(a, b, (((1,), (1,)), ((), ())), preferred_element_type=F32)


class Semaphores:
    def __init__(self):
        self.n = 0

    def take(self, count):
        first = self.n
        self.n += count
        return first


S = Semaphores()
S_FEAT = S.take(4)
S_FREL = S.take(2)
S_SB = S.take(8)
S_ROW = S.take(4)
S_TY = S.take(16)
S_TQ = S.take(8)
S_HZ = S.take(16)
S_HC = S.take(16)
S_YR = S.take(2)
S_YI = S.take(4)
S_G = S.take(4)
S_GR = S.take(2)
S_SIB = S.take(8)
S_ZR = S.take(16)
S_XR = S.take(2)
S_XI = S.take(4)
S_SBC = S.take(1)
S_TR = S.take(1)
S_A0 = S.take(1)
S_A1 = S.take(8)
S_A2 = S.take(4)
S_A3 = S.take(8)
S_A4 = S.take(1)
S_RECV = S.n
S_TF = S.take(7)
S_SEND = S.n
L_LOC, L_SB, L_ROW, L_FEAT, L_W, L_COT, L_BIAS, L_OUT, L_GIN, L_GW, L_GB, L_N = 0, 1, 2, 3, 4, 5, 6, 7, 9, 11, 12, 13


def kernel(
    feat, weight, bias, cot, tiles, sendb, trow, row_own, src_own,
    out, gin, gw, gb,
    F, Hown, Hcore, H1, H2, H3, H4, H5, H6, H7, T, TL, trel, agg, ysend2, ysend1, ysend3, yrel, yin, G0, G1, G2, G3, D, S0, SL,
    zsend, zrecv, sibsend, sibrecv, GAT, GA, PT, xsend2, xsend1, xsend3, xrel, xin, bsum, gws, arc, arsend, arin, ar2in, red, gwall,
    wv, cv, bv, ov, giv, gbv, sbv, rowv, sbs, rows, ssem, rsem, lsem,
):
    H = [None, H1, H2, H3, H4, H5, H6, H7]
    G = [G0, G1, G2, G3]

    def hid(e, oc):
        return H[e].at[oc] if e else (Hown, Hcore)[oc]

    dom, x = lax.axis_index("dom"), lax.axis_index("rep")
    z = dom // (NY * NC)
    y = lax.rem(dom // NC, NY)
    c = lax.rem(dom, NC)

    def at(dx=0, dy=0, dz=0, oc=0):
        zz = lax.rem(z + dz + NZ, NZ)
        yy = lax.rem(y + dy + NY, NY)
        cc = lax.rem(c + oc, NC)
        return ((zz * NY + yy) * NC + cc, lax.rem(x + dx + NX, NX))

    started = []

    def copy(src, dst, sem, dev, recv=None):
        return pltpu.make_async_remote_copy(
            src_ref=src,
            dst_ref=dst,
            send_sem=ssem.at[sem],
            recv_sem=rsem.at[sem if recv is None else recv],
            device_id=dev,
            device_id_type=MESH,
        )

    def send(src, dst, sem, dev, recv=None):
        made = copy(src, dst, sem, dev, recv)
        made.start()
        started.append(made)

    here = (dom, x)

    def arrived(dst, sem):
        pltpu.make_async_remote_copy(
            src_ref=dst, dst_ref=dst, send_sem=ssem.at[0], recv_sem=rsem.at[sem], device_id=here, device_id_type=MESH
        ).wait_recv()

    half = lambda ref, h: ref.at[pl.ds(4 * h, 4)]

    def local(src, dst, sem):
        made = pltpu.make_async_copy(src, dst, lsem.at[sem])
        made.start()
        return made

    feat_in = local(feat, F.at[0], L_FEAT)
    weight_in = local(weight, wv, L_W)
    loc_tiles = local(tiles.at[pl.ds(0, 2)], TL, L_LOC)
    own_tiles = [
        local(tiles.at[2 + lax.rem(z + DIST[e] + NZ, NZ), y], T.at[0, e], L_N + e) for e in range(NZ)
    ]
    cot_in = local(cot, cv, L_COT)
    bias_in = local(bias, bv, L_BIAS)

    barrier = pltpu.get_barrier_semaphore()
    peers = [at(dz=DIST[e]) for e in range(1, NZ)] + [at(oc=1)]
    peers += [at(dy=d) for d in range(1, NY)] + [at(dx=d) for d in range(1, NX)]
    for dev in peers:
        pl.semaphore_signal(barrier, inc=1, device_id=dev, device_id_type=MESH)
    pl.semaphore_wait(barrier, len(peers))

    rows_of = lambda h: pl.ds(512 * h, 512)
    for h, g in ((0, 1), (1, 0)):
        send(feat.at[rows_of(h)], F.at[3, rows_of(h)], S_FEAT + h, at(dx=1))
        send(feat.at[rows_of(g)], F.at[1, rows_of(g)], S_FEAT + 2 + g, at(dx=-1))
    for e in range(1, NZ):
        back = SLOT[-DIST[e]]
        send(sendb, sbv.at[0, back], S_SB + back, at(dz=DIST[e]))
    for d in range(1, NY):
        send(trow, rowv.at[NY - d], S_ROW + NY - d, at(dy=d))
    sb_in = local(sendb, sbv.at[0, 0], L_SB)
    row_in = local(trow, rowv.at[0], L_ROW)

    def tile_slot(e):
        d = jnp.where(lax.rem(e, 2) == 1, (e + 1) // 2, NZ - e // 2)
        return 2 + lax.rem(z + d, NZ)

    far = lax.rem(y + 2, NY)
    send(tiles.at[tile_slot(x), far], T.at[2, x], S_TF + 6, at(dy=2), S_TQ + x)
    send(tiles.at[tile_slot(x + 4), far], trel, S_TR, at(dy=-1))

    def near_tiles(slots):
        for e in slots:
            for dy, to, base in ((1, 3, 0), (-1, 1, 8)):
                send(
                    tiles.at[2 + lax.rem(z + DIST[e] + NZ, NZ), lax.rem(y + dy + NY, NY)],
                    T.at[to, e],
                    S_TY + base + e,
                    at(dy=dy),
                )

    near_tiles(range(2))

    for dy in range(NY):
        G[dy][NB] = jnp.zeros((B, B), BF)

    @pl.loop(0, NB)
    def _(i):
        for dy in range(NY):
            agg[dy, i] = jnp.zeros((B, B), F32)
        SL[i] = jnp.zeros((B, B), F32)

    arrived(F.at[3, rows_of(0)], S_FEAT + 0)
    send(F.at[3, rows_of(0)], F.at[2, rows_of(0)], S_FREL + 0, at(dx=1))
    arrived(F.at[1, rows_of(1)], S_FEAT + 3)
    send(F.at[1, rows_of(1)], F.at[2, rows_of(1)], S_FREL + 1, at(dx=-1))
    arrived(F.at[1, rows_of(0)], S_FEAT + 2)
    arrived(F.at[3, rows_of(1)], S_FEAT + 1)

    def w_rows(dx):
        return wv[pl.ds(pl.multiple_of(lax.rem(x + dx, NX) * B, B), B), :]

    arrived(trel, S_TR)
    send(trel, T.at[2, x + 4], S_TQ, at(dy=-1), S_TQ + x + 4)
    near_tiles(range(2, NZ))

    def step_send(way, step, h):
        d = -step if way == 0 else step
        nd = d - 1 if way == 0 else d + 1
        send(
            half(hid(SLOT[d], 0), h), half(hid(SLOT[nd], 0), h), S_HZ + way * 8 + step * 2 + h,
            at(dz=1 if way == 0 else -1),
        )

    def core_send(e, h):
        send(half(hid(e, 0), h), half(hid(e, 1), h), S_HC + e * 2 + h, at(oc=1))

    feat_in.wait()
    weight_in.wait()
    for h in range(2):
        arrived(F.at[2, rows_of(h)], S_FREL + h)

        @pl.loop(0, 4, unroll=True)
        def _(b, h=h):
            r = pl.ds(pl.multiple_of(512 * h + b * B, B), B)
            acc = dot(F[0, r], w_rows(0))
            for dx in range(1, NX):
                acc += dot(F[dx, r], w_rows(dx))
            Hown[4 * h + b] = acc.astype(BF)

        step_send(0, 0, h)
        step_send(1, 0, h)
        core_send(0, h)

    def far_tiles(k):
        e = x + 4 * k
        arrived(T.at[2, e], S_TQ + e)
        for i, dx in enumerate((1, -1, 2)):
            send(T.at[2, e], T.at[2, e], S_TF + k * 3 + i, at(dx=dx), S_TQ + e)

    far_tiles(0)

    sb_in.wait()
    row_in.wait()
    for e in range(1, NZ):
        arrived(sbv.at[0, e], S_SB + e)
    send(sbv.at[0], sbv.at[1], S_SBC, at(oc=1))
    for d in range(1, NY):
        arrived(rowv.at[d], S_ROW + d)

    arrived(sbv.at[1], S_SBC)
    to_s = [local(sbv, sbs, L_SB), local(rowv, rows, L_ROW)]

    loc_tiles.wait()

    @pl.loop(0, 8)
    def _(i):
        k = i * 4
        prods = [dot(TL[i // 4, lax.rem(i, 4), j], Hown[src_own[0, k + j]]) for j in range(4)]
        tr = [row_own[0, k + j] for j in range(4)]
        for t in range(NB):
            add = jnp.where(tr[0] == t, prods[0], 0.0)
            for j in range(1, 4):
                add += jnp.where(tr[j] == t, prods[j], 0.0)
            agg[0, t] += add

    far_tiles(1)
    for made in to_s:
        made.wait()

    for made in own_tiles:
        made.wait()

    def slot_row(dy, e, cc, cap):
        zz = lax.rem(z + DIST[e] + NZ, NZ)
        return rows[dy, 0, 32 + zz * 16 + y * 4 + cc * 2 + cap]

    def slot_block(dy, e, oc, cap):
        target = (z * NY + lax.rem(y + dy, NY)) * NC + c
        return sbs[oc, e, cap, target]

    def forward(e):
        for dy, base in ((3, 0), (1, 8)):
            arrived(T.at[dy, e], S_TY + base + e)

        @pl.when(x != e % 4)
        def _():
            arrived(T.at[2, e], S_TQ + e)

        for h in range(2):
            arrived(half(hid(e, 1), h), S_HC + e * 2 + h)

        def add(oc, dys=range(NY)):
            cc = lax.rem(c + oc, NC)
            for dy in dys:
                prods, tr = [], []
                for cap in range(CAP):
                    t, b = T[dy, e, cc * 2 + cap], slot_block(dy, e, oc, cap)
                    prods.append(dot(t, H[e][oc, b] if e else (Hown, Hcore)[oc][b]))
                    tr.append(slot_row(dy, e, cc, cap))
                for t in range(NB):
                    agg[dy, t] += jnp.where(tr[0] == t, prods[0], 0.0) + jnp.where(tr[1] == t, prods[1], 0.0)

        if e == SLOT[4]:
            return add
        if e:
            pl.loop(0, NC)(add)
        else:
            for oc in range(NC):
                add(oc)

    pending = [0]
    for step in range(4):
        halves = ((0, 0), (1, 0), (0, 1), (1, 1)) if step < 3 else ((0, 0), (1, 1))
        for way, h in halves:
            d = -(step + 1) if way == 0 else step + 1
            arrived(half(hid(SLOT[d], 0), h), S_HZ + way * 8 + step * 2 + h)
            if step < 2 or (step == 2 and h == way):
                step_send(way, step + 1, h)
            core_send(SLOT[d], h)
        for e in pending:
            forward(e)
        pending = [SLOT[step + 1], SLOT[-step - 1]] if step < 3 else [SLOT[4]]
    last = forward(SLOT[4])

    def to_bf16(dst, src, base, more=None):
        @pl.loop(0, 4)
        def _(i):
            value = src[base + i]
            if more is not None:
                value += more[i].astype(F32)
            dst[base + i] = value.astype(BF)

    for oc in range(NC):
        last(oc, (2,))
    to_bf16(ysend2, agg.at[2], 0)
    send(half(ysend2, 0), yrel.at[0], S_YR + 0, at(dy=1))
    to_bf16(ysend2, agg.at[2], 4)
    send(half(ysend2, 1), yrel.at[1], S_YR + 1, at(dy=-1))
    for oc in range(NC):
        last(oc, (1, 3))
    to_bf16(ysend1, agg.at[1], 4)
    send(half(ysend1, 1), half(yin.at[0], 1), S_YI + 1, at(dy=1))
    to_bf16(ysend3, agg.at[3], 0)
    send(half(ysend3, 0), half(yin.at[1], 0), S_YI + 2, at(dy=-1))
    arrived(yrel.at[0], S_YR + 0)
    to_bf16(ysend1, agg.at[1], 0, yrel.at[0])
    send(half(ysend1, 0), half(yin.at[0], 0), S_YI + 0, at(dy=1))
    arrived(yrel.at[1], S_YR + 1)
    to_bf16(ysend3, agg.at[3], 4, yrel.at[1])
    send(half(ysend3, 1), half(yin.at[1], 1), S_YI + 3, at(dy=-1))
    for oc in range(NC):
        last(oc, (0,))

    bsum[...] = jnp.zeros_like(bsum)
    cot_in.wait()
    bias_in.wait()
    leaving = []
    for h in range(2):
        arrived(half(yin.at[0], h), S_YI + h)
        arrived(half(yin.at[1], h), S_YI + 2 + h)

        @pl.loop(0, 4)
        def _(b, h=h):
            i = 4 * h + b
            r = pl.ds(pl.multiple_of(i * B, B), B)
            pre = agg[0, i] + yin[0, i].astype(F32) + yin[1, i].astype(F32) + bv[...].astype(F32)
            sig = jax.nn.sigmoid(pre)
            ov[r, :] = (pre * sig).astype(BF)
            g = (cv[r, :].astype(F32) * sig * (1.0 + pre * (1.0 - sig))).astype(BF).astype(F32)
            part = g[0:8]
            for j in range(1, 16):
                part += g[8 * j : 8 * j + 8]
            bsum[...] += part
            G[0][i] = g.T.astype(BF)

        send(half(G[0], h), half(G[3], h), S_G + h, at(dy=1))
        send(half(G[0], h), half(G[1], h), S_G + 2 + h, at(dy=-1))
        leaving.append(local(ov.at[rows_of(h)], out.at[rows_of(h)], L_OUT + h))

    def spread(n, base, dst, tail):
        @pl.loop(0, 8)
        def _(j):
            r = pl.ds(pl.multiple_of(j * 16, 16), 16)
            parts = [D[k, r, :] for k in range(n)]
            for t in range(NB):
                acc = jnp.where(base[0] == t, parts[0], 0.0)
                for k in range(1, n):
                    acc += jnp.where(base[k] == t, parts[k], 0.0)
                tail(dst, t, r, acc)

    def add_f32(dst, t, r, acc):
        dst[t, r, :] += acc

    def put_f32(dst, t, r, acc):
        dst[t, r, :] = acc

    def put_bf16(dst, t, r, acc):
        dst[t, r, :] = acc.astype(BF)

    @pl.loop(0, 4)
    def _(i):
        k0 = i * 8
        for j in range(8):
            D[j] = dot(G[0][row_own[0, k0 + j]], TL[i // 2, lax.rem(i, 2) * 2 + j // 4, j % 4])
        spread(8, [src_own[0, k0 + j] for j in range(8)], SL, add_f32)

    arrived(half(G[3], 0), S_G + 0)
    send(half(G[3], 0), half(G[2], 0), S_GR + 0, at(dy=1))
    arrived(half(G[1], 1), S_G + 3)
    send(half(G[1], 1), half(G[2], 1), S_GR + 1, at(dy=-1))
    arrived(half(G[1], 0), S_G + 2)
    arrived(half(G[3], 1), S_G + 1)
    for h in range(2):
        arrived(half(G[2], h), S_GR + h)

    def backward(e, oc, dst, tail):
        cc = lax.rem(c + oc, NC)
        blocks = []
        for dy in range(NY):
            for cap in range(CAP):
                D[dy * 2 + cap] = dot(G[dy][slot_row(dy, e, cc, cap)], T[dy, e, cc * 2 + cap])
                blocks.append(slot_block(dy, e, oc, cap))
        spread(8, blocks, dst, tail)

    def combine(dst, e, h, way=None, step=None):
        @pl.loop(0, 4)
        def _(i):
            t = 4 * h + i
            value = S0[e, t] + sibrecv[e, t].astype(F32)
            if step is not None:
                value += zrecv[way, step, t].astype(F32)
            dst[t] = value.astype(BF)

    def ring_send(way, step, h):
        send(
            half(zsend.at[way, step], h), half(zrecv.at[way, step], h), S_ZR + way * 8 + step * 2 + h,
            at(dz=1 if way == 0 else -1),
        )

    def terms(e):
        backward(e, 1, sibsend.at[e], put_bf16)
        send(sibsend.at[e], sibrecv.at[e], S_SIB + e, at(oc=1))
        backward(e, 0, S0.at[e], put_f32)

    terms(SLOT[4])
    arrived(sibrecv.at[SLOT[4]], S_SIB + SLOT[4])
    for way in range(2):
        combine(zsend.at[way, 0], SLOT[4], way)
        ring_send(way, 0, way)
    for step in range(1, 4):
        d = 4 - step
        ends = (SLOT[d], SLOT[-d])
        for e in ends:
            terms(e)
        for e in ends:
            arrived(sibrecv.at[e], S_SIB + e)
        order = ((1, 0), (0, 1), (0, 0), (1, 1)) if step == 1 else ((0, 0), (1, 0), (0, 1), (1, 1))
        for way, h in order:
            came = step > 1 or h == way
            if came:
                arrived(half(zrecv.at[way, step - 1], h), S_ZR + way * 8 + (step - 1) * 2 + h)
            combine(zsend.at[way, step], ends[way], h, way, step - 1 if came else None)
            ring_send(way, step, h)
    terms(0)
    arrived(sibrecv.at[0], S_SIB + 0)

    def terms_x(dx, h, dst, more=None):
        @pl.loop(0, 4, unroll=True)
        def _(b):
            r = pl.ds(pl.multiple_of(512 * h + b * B, B), B)
            value = dot_t(GA[r, :], w_rows(dx))
            if more is not None:
                value += more[pl.ds(pl.multiple_of(b * B, B), B), :].astype(F32)
            dst[r, :] = value.astype(dst.dtype)

    for h in range(2):
        for way in range(2):
            arrived(half(zrecv.at[way, 3], h), S_ZR + way * 8 + 6 + h)

        @pl.loop(0, 4, unroll=True)
        def _(i, h=h):
            t = 4 * h + i
            value = S0[0, t] + sibrecv[0, t].astype(F32) + SL[t]
            value += zrecv[0, 3, t].astype(F32) + zrecv[1, 3, t].astype(F32)
            value = value.astype(BF).astype(F32)
            GAT[:, pl.ds(pl.multiple_of(t * B, B), B)] = value.astype(BF)
            GA[pl.ds(pl.multiple_of(t * B, B), B), :] = value.T.astype(BF)

        if h == 0:
            terms_x(2, 0, xsend2)
            send(xsend2.at[rows_of(0)], xrel.at[0], S_XR + 0, at(dx=1))
            terms_x(3, 0, xsend3)
            send(xsend3.at[rows_of(0)], xin.at[1, rows_of(0)], S_XI + 2, at(dx=-1))

    for dx in range(NX):
        k = lax.rem(x + dx, NX)
        gws[k // 2, pl.ds(pl.multiple_of(lax.rem(k, 2) * B, B), B), :] = dot(GAT[...], F[dx]).T
    for k in range(NC):
        gws[k, 256:264, :] = bsum[...]
    send(gws.at[1 - c], arc, S_A0, at(oc=1))
    terms_x(2, 1, xsend2)
    send(xsend2.at[rows_of(1)], xrel.at[1], S_XR + 1, at(dx=-1))
    terms_x(1, 1, xsend1)
    send(xsend1.at[rows_of(1)], xin.at[0, rows_of(1)], S_XI + 1, at(dx=1))

    arrived(arc, S_A0)
    for k in range(NZ):
        arsend[k, 0:32, :] = gws[c, 32 * k : 32 * k + 32, :] + arc[32 * k : 32 * k + 32, :]
        arsend[k, 32:40, :] = gws[c, 256:264, :] + arc[256:264, :]
    for e in range(NZ - 1, 0, -1):
        send(arsend.at[lax.rem(z + DIST[e] + NZ, NZ)], arin.at[z], S_A1 + SLOT[-DIST[e]], at(dz=DIST[e]))
    arin[z] = arsend[z]

    arrived(xrel.at[0], S_XR + 0)
    terms_x(1, 0, xsend1, xrel.at[0])
    send(xsend1.at[rows_of(0)], xin.at[0, rows_of(0)], S_XI + 0, at(dx=1))
    arrived(xrel.at[1], S_XR + 1)
    terms_x(3, 1, xsend3, xrel.at[1])
    send(xsend3.at[rows_of(1)], xin.at[1, rows_of(1)], S_XI + 3, at(dx=-1))

    for e in range(1, NZ):
        arrived(arin.at[lax.rem(z + DIST[e] + NZ, NZ)], S_A1 + e)
    total = arin[0]
    for k in range(1, NZ):
        total += arin[k]
    red[...] = total
    for d in range(1, NY):
        send(red, ar2in.at[y], S_A2 + NY - d, at(dy=d))
    ar2in[y] = red[...]
    for h in range(2):
        terms_x(0, h, PT)
    for d in range(1, NY):
        arrived(ar2in.at[lax.rem(y + d, NY)], S_A2 + d)
    total = ar2in[0] + ar2in[1] + ar2in[2] + ar2in[3]
    gbv[...] = jnp.sum(total[32:40], 0, keepdims=True)
    leaving.append(local(gbv, gb, L_GB))
    gwall[c, z] = total[0:32]
    for e in range(NZ - 1, 0, -1):
        send(gwall.at[c, z], gwall.at[c, z], S_A3 + SLOT[-DIST[e]], at(dz=DIST[e]))

    for h in range(2):
        arrived(xin.at[0, rows_of(h)], S_XI + h)
        arrived(xin.at[1, rows_of(h)], S_XI + 2 + h)

        @pl.loop(0, 4)
        def _(b, h=h):
            r = pl.ds(pl.multiple_of(512 * h + b * B, B), B)
            giv[r, :] = (PT[r, :] + xin[0, r, :].astype(F32) + xin[1, r, :].astype(F32)).astype(BF)

        leaving.append(local(giv.at[rows_of(h)], gin.at[rows_of(h)], L_GIN + h))

    for e in range(1, NZ):
        arrived(gwall.at[c, lax.rem(z + DIST[e] + NZ, NZ)], S_A3 + e)
    send(gwall.at[c], gwall.at[c], S_A4, at(oc=1))
    arrived(gwall.at[1 - c], S_A4)
    leaving.append(local(gwall, gw, L_GW))
    for made in leaving:
        made.wait()
    for made in started:
        made.wait_send()


def hand_over(*refs):
    for k in range(4):
        refs[4 + k][...] = refs[k][...]


def shards(
    features, weight, bias, cotangent, tile_vals, tile_row, tile_src, send_blocks, send_count
):
    blocks = lambda *lead, dtype=BF: pltpu.VMEM((*lead, B, B), dtype)
    scratch = [
        pltpu.VMEM((NX, 1024, B), BF),
        blocks(NB),
        blocks(NB),
        *[blocks(NC, NB) for _ in range(NZ - 1)],
        blocks(NY, NZ, 4),
        blocks(2, 4, 4),
        blocks(4),
        blocks(NY, NB, dtype=F32),
        blocks(NB),
        blocks(NB),
        blocks(NB),
        blocks(2, 4),
        blocks(2, NB),
        *[blocks(NB + 1) for _ in range(NY)],
        blocks(8, dtype=F32),
        blocks(NZ, NB, dtype=F32),
        blocks(NB, dtype=F32),
        blocks(2, 4, NB),
        blocks(2, 4, NB),
        blocks(NZ, NB),
        blocks(NZ, NB),
        pltpu.VMEM((B, 1024), BF),
        pltpu.VMEM((1024, B), BF),
        pltpu.VMEM((1024, B), F32),
        pltpu.VMEM((1024, B), BF),
        pltpu.VMEM((1024, B), BF),
        pltpu.VMEM((1024, B), BF),
        pltpu.VMEM((2, 512, B), BF),
        pltpu.VMEM((2, 1024, B), BF),
        pltpu.VMEM((8, B), F32),
        pltpu.VMEM((NC, 264, B), F32),
        pltpu.VMEM((264, B), F32),
        pltpu.VMEM((NZ, 40, B), F32),
        pltpu.VMEM((NZ, 40, B), F32),
        pltpu.VMEM((NY, 40, B), F32),
        pltpu.VMEM((40, B), F32),
        pltpu.VMEM((NC, NZ, 32, B), F32),
        pltpu.VMEM((512, B), BF),
        pltpu.VMEM((1024, B), BF),
        pltpu.VMEM((1, B), BF),
        pltpu.VMEM((1024, B), BF),
        pltpu.VMEM((1024, B), BF),
        pltpu.VMEM((1, B), F32),
        pltpu.VMEM((NC, NZ, CAP, 64), jnp.int32),
        pltpu.VMEM((NY, 1, 160), jnp.int32),
        pltpu.SMEM((NC, NZ, CAP, 64), jnp.int32),
        pltpu.SMEM((NY, 1, 160), jnp.int32),
        pltpu.SemaphoreType.DMA((S_SEND,)),
        pltpu.SemaphoreType.DMA((S_RECV,)),
        pltpu.SemaphoreType.DMA((L_N + NZ,)),
    ]
    anywhere = pl.BlockSpec(memory_space=pl.ANY)
    smem = pl.BlockSpec(memory_space=pltpu.SMEM)
    vmem = pl.BlockSpec(memory_space=pltpu.VMEM)
    shapes = (
        jax.ShapeDtypeStruct((1024, B), BF),
        jax.ShapeDtypeStruct((1024, B), BF),
        jax.ShapeDtypeStruct((NC, NZ, 32, B), F32),
        jax.ShapeDtypeStruct((1, B), F32),
    )
    results = pl.pallas_call(
        kernel,
        out_shape=shapes,
        in_specs=[anywhere] * 7 + [smem] * 2,
        out_specs=(anywhere,) * 4,
        scratch_shapes=scratch,
        compiler_params=pltpu.CompilerParams(
            collective_id=0, has_side_effects=True, vmem_limit_bytes=56 * 2**20
        ),
    )(
        features,
        weight,
        bias.reshape(1, B),
        cotangent,
        tile_vals.reshape(10, 4, 4, B, B),
        send_blocks.transpose(0, 2, 1).reshape(CAP, 64),
        tile_row,
        tile_row,
        tile_src,
    )
    out, gin, gw, gb = pl.pallas_call(
        hand_over,
        out_shape=shapes,
        in_specs=[vmem] * 4,
        out_specs=(vmem,) * 4,
        compiler_params=pltpu.CompilerParams(vmem_limit_bytes=8 * 2**20),
    )(*results)
    return out, gin, gw.reshape(512, B), gb.reshape(B)


def solution(mesh):
    in_specs = (
        P("dom", "rep"),
        P(None, "rep"),
        P("rep"),
        P("dom", "rep"),
        P("dom", None, None, None),
        P("dom", None),
        P("dom", None),
        P("dom", None, None),
        P("dom", None),
    )
    out_specs = (P("dom", "rep"), P("dom", "rep"), P(None, "rep"), P("rep"))
    return jax.shard_map(shards, mesh=mesh, in_specs=in_specs, out_specs=out_specs, check_vma=False)
```

```python
import jax
import jax.numpy as jnp
from jax import lax
from jax.experimental import pallas as pl
from jax.experimental.pallas import tpu as pltpu
from jax.sharding import PartitionSpec as P

B = 128
NB = 8
CAP = 2
NX, NY, NZ, NC = 4, 4, 8, 2
MESH = pl.DeviceIdType.MESH
BF = jnp.bfloat16
F32 = jnp.float32

DIST = [0, 1, -1, 2, -2, 3, -3, 4]
SLOT = {d: e for e, d in enumerate(DIST)}
SLOT[-4] = SLOT[4]


def dot(a, b):
    return lax.dot_general(a, b, (((1,), (0,)), ((), ())), preferred_element_type=F32)


def dot_t(a, b):
    return lax.dot_general(a, b, (((1,), (1,)), ((), ())), preferred_element_type=F32)


class Semaphores:
    def __init__(self):
        self.n = 0

    def take(self, count):
        first = self.n
        self.n += count
        return first


S = Semaphores()
S_FEAT = S.take(8)
S_FREL = S.take(4)
S_SB = S.take(8)
S_ROW = S.take(4)
S_TY = S.take(16)
S_TQ = S.take(8)
S_HZ = S.take(16)
S_HC = S.take(16)
S_YR = S.take(2)
S_YI = S.take(4)
S_G = S.take(4)
S_GR = S.take(2)
S_SIB = S.take(8)
S_ZR = S.take(16)
S_XR = S.take(2)
S_XI = S.take(4)
S_SBC = S.take(1)
S_TR = S.take(1)
S_B0 = S.take(1)
S_B1 = S.take(8)
S_B2 = S.take(4)
S_A0 = S.take(1)
S_A1 = S.take(8)
S_A2 = S.take(4)
S_A3 = S.take(8)
S_A4 = S.take(1)
S_RECV = S.n
S_TF = S.take(7)
S_SEND = S.n
L_LOC, L_SB, L_ROW, L_FEAT, L_W, L_COT, L_BIAS, L_OUT, L_GIN, L_GW, L_GB, L_N = 0, 1, 2, 3, 4, 5, 6, 7, 9, 11, 12, 13


def kernel(
    feat, weight, bias, cot, tiles, sendb, trow, row_own, src_own,
    out, gin, gw, gb,
    F, Hown, Hcore, H1, H2, H3, H4, H5, H6, Hlast, Hlastcore, T, TL, trel, agg, ysend2, ysend1, ysend3, yrel, yin, G0, G1, G2, G3, D, S0, SL,
    zsend, zrecv, sibsend, sibrecv, GAT, GA, PT, xsend2, xsend1, xsend3, xrel, xin, bsum, bcore, bz, by, gws, arc, arown, arsend, arin, ar2in, gwall, gwf,
    wv, cv, bv, ov, giv, gbv, sbv, rowv, sbs, rows, ssem, rsem, lsem,
):
    H = [(Hown, Hcore), H1, H2, H3, H4, H5, H6, (Hlast, Hlastcore)]
    G = [G0, G1, G2, G3]

    def hid(e, oc):
        return H[e][oc] if isinstance(H[e], tuple) else H[e].at[oc]

    dom, x = lax.axis_index("dom"), lax.axis_index("rep")
    z = dom // (NY * NC)
    y = lax.rem(dom // NC, NY)
    c = lax.rem(dom, NC)

    def at(dx=0, dy=0, dz=0, oc=0):
        zz = lax.rem(z + dz + NZ, NZ)
        yy = lax.rem(y + dy + NY, NY)
        cc = lax.rem(c + oc, NC)
        return ((zz * NY + yy) * NC + cc, lax.rem(x + dx + NX, NX))

    started = []

    def copy(src, dst, sem, dev, recv=None):
        return pltpu.make_async_remote_copy(
            src_ref=src,
            dst_ref=dst,
            send_sem=ssem.at[sem],
            recv_sem=rsem.at[sem if recv is None else recv],
            device_id=dev,
            device_id_type=MESH,
        )

    def send(src, dst, sem, dev, recv=None):
        made = copy(src, dst, sem, dev, recv)
        made.start()
        started.append(made)

    here = (dom, x)

    def arrived(dst, sem):
        pltpu.make_async_remote_copy(
            src_ref=dst, dst_ref=dst, send_sem=ssem.at[0], recv_sem=rsem.at[sem], device_id=here, device_id_type=MESH
        ).wait_recv()

    half = lambda ref, h: ref.at[pl.ds(4 * h, 4)]

    def local(src, dst, sem):
        made = pltpu.make_async_copy(src, dst, lsem.at[sem])
        made.start()
        return made

    feat_in = local(feat, F.at[0], L_FEAT)
    weight_in = local(weight, wv, L_W)
    loc_tiles = local(tiles.at[pl.ds(0, 2)], TL, L_LOC)
    own_tiles = [
        local(tiles.at[2 + lax.rem(z + DIST[e] + NZ, NZ), y], T.at[0, e], L_N + e) for e in range(NZ)
    ]
    cot_in = local(cot, cv, L_COT)
    bias_in = local(bias, bv, L_BIAS)

    barrier = pltpu.get_barrier_semaphore()
    peers = [at(dz=DIST[e]) for e in range(1, NZ)] + [at(oc=1)]
    peers += [at(dy=d) for d in range(1, NY)] + [at(dx=d) for d in range(1, NX)]
    for dev in peers:
        pl.semaphore_signal(barrier, inc=1, device_id=dev, device_id_type=MESH)
    pl.semaphore_wait(barrier, len(peers))

    rows_of = lambda h: pl.ds(512 * h, 512)
    quarter = lambda q: pl.ds(256 * q, 256)

    def feat_send(q):
        send(feat.at[quarter(q)], F.at[3, quarter(q)], S_FEAT + q, at(dx=1))
        send(feat.at[quarter(q)], F.at[1, quarter(q)], S_FEAT + 4 + q, at(dx=-1))

    def feat_pass(q):
        up = q % 2 == 0
        came, sem = (F.at[3, quarter(q)], S_FEAT + q) if up else (F.at[1, quarter(q)], S_FEAT + 4 + q)
        arrived(came, sem)
        send(came, F.at[2, quarter(q)], S_FREL + q, at(dx=1 if up else -1))

    def feat_rest(q):
        up = q % 2 == 0
        came, sem = (F.at[1, quarter(q)], S_FEAT + 4 + q) if up else (F.at[3, quarter(q)], S_FEAT + q)
        arrived(came, sem)
        arrived(F.at[2, quarter(q)], S_FREL + q)

    feat_send(0)
    feat_send(1)

    for e in range(1, NZ):
        back = SLOT[-DIST[e]]
        send(sendb, sbv.at[0, back], S_SB + back, at(dz=DIST[e]))
    for d in range(1, NY):
        send(trow, rowv.at[NY - d], S_ROW + NY - d, at(dy=d))
    sb_in = local(sendb, sbv.at[0, 0], L_SB)
    row_in = local(trow, rowv.at[0], L_ROW)

    def tile_slot(e):
        d = jnp.where(lax.rem(e, 2) == 1, (e + 1) // 2, NZ - e // 2)
        return 2 + lax.rem(z + d, NZ)

    far = lax.rem(y + 2, NY)
    send(tiles.at[tile_slot(x), far], T.at[2, x], S_TF + 6, at(dy=2), S_TQ + x)
    send(tiles.at[tile_slot(x + 4), far], trel, S_TR, at(dy=-1))

    def near_tiles(slots):
        for e in slots:
            for dy, to, base in ((1, 3, 0), (-1, 1, 8)):
                send(
                    tiles.at[2 + lax.rem(z + DIST[e] + NZ, NZ), lax.rem(y + dy + NY, NY)],
                    T.at[to, e],
                    S_TY + base + e,
                    at(dy=dy),
                )

    near_tiles(range(2))

    for dy in range(NY):
        G[dy][NB] = jnp.zeros((B, B), BF)

    @pl.loop(0, NB)
    def _(i):
        for dy in range(NY):
            agg[dy, i] = jnp.zeros((B, B), F32)
        SL[i] = jnp.zeros((B, B), F32)

    for q in range(2):
        feat_pass(q)
    for q in range(2, 4):
        feat_send(q)

    def w_rows(dx):
        return wv[pl.ds(pl.multiple_of(lax.rem(x + dx, NX) * B, B), B), :]

    def step_send(way, step, h):
        d = -step if way == 0 else step
        nd = d - 1 if way == 0 else d + 1
        send(
            half(hid(SLOT[d], 0), h), half(hid(SLOT[nd], 0), h), S_HZ + way * 8 + step * 2 + h,
            at(dz=1 if way == 0 else -1),
        )

    def core_send(e, h):
        send(half(hid(e, 0), h), half(hid(e, 1), h), S_HC + e * 2 + h, at(oc=1))

    feat_in.wait()
    weight_in.wait()
    for h in range(2):
        for q in (2 * h, 2 * h + 1):
            feat_rest(q)

        @pl.loop(0, 4, unroll=True)
        def _(b, h=h):
            r = pl.ds(pl.multiple_of(512 * h + b * B, B), B)
            acc = dot(F[0, r], w_rows(0))
            for dx in range(1, NX):
                acc += dot(F[dx, r], w_rows(dx))
            Hown[4 * h + b] = acc.astype(BF)

        step_send(0, 0, h)
        step_send(1, 0, h)
        core_send(0, h)
        if h == 0:
            for q in range(2, 4):
                feat_pass(q)
            arrived(trel, S_TR)
            send(trel, T.at[2, x + 4], S_TQ, at(dy=-1), S_TQ + x + 4)
            near_tiles(range(2, NZ))

    def far_tiles(k):
        e = x + 4 * k
        arrived(T.at[2, e], S_TQ + e)
        for i, dx in enumerate((1, -1, 2)):
            send(T.at[2, e], T.at[2, e], S_TF + k * 3 + i, at(dx=dx), S_TQ + e)

    far_tiles(0)

    sb_in.wait()
    row_in.wait()
    for e in range(1, NZ):
        arrived(sbv.at[0, e], S_SB + e)
    send(sbv.at[0], sbv.at[1], S_SBC, at(oc=1))
    for d in range(1, NY):
        arrived(rowv.at[d], S_ROW + d)

    arrived(sbv.at[1], S_SBC)
    to_s = [local(sbv, sbs, L_SB), local(rowv, rows, L_ROW)]

    loc_tiles.wait()

    @pl.loop(0, 8)
    def _(i):
        k = i * 4
        prods = [dot(TL[i // 4, lax.rem(i, 4), j], Hown[src_own[0, k + j]]) for j in range(4)]
        tr = [row_own[0, k + j] for j in range(4)]
        for t in range(NB):
            add = jnp.where(tr[0] == t, prods[0], 0.0)
            for j in range(1, 4):
                add += jnp.where(tr[j] == t, prods[j], 0.0)
            agg[0, t] += add

    far_tiles(1)
    for made in to_s:
        made.wait()

    for made in own_tiles:
        made.wait()

    def slot_row(dy, e, cc, cap):
        zz = lax.rem(z + DIST[e] + NZ, NZ)
        return rows[dy, 0, 32 + zz * 16 + y * 4 + cc * 2 + cap]

    def slot_block(dy, e, oc, cap):
        target = (z * NY + lax.rem(y + dy, NY)) * NC + c
        return sbs[oc, e, cap, target]

    def core_arrived(e):
        for h in range(2):
            arrived(half(hid(e, 1), h), S_HC + e * 2 + h)

    def forward(e):
        for dy, base in ((3, 0), (1, 8)):
            arrived(T.at[dy, e], S_TY + base + e)

        @pl.when(x != e % 4)
        def _():
            arrived(T.at[2, e], S_TQ + e)

        def add(oc, dys=range(NY)):
            cc = lax.rem(c + oc, NC)
            for dy in dys:
                prods, tr = [], []
                for cap in range(CAP):
                    t, b = T[dy, e, cc * 2 + cap], slot_block(dy, e, oc, cap)
                    prods.append(dot(t, H[e][oc][b] if isinstance(H[e], tuple) else H[e][oc, b]))
                    tr.append(slot_row(dy, e, cc, cap))
                for t in range(NB):
                    agg[dy, t] += jnp.where(tr[0] == t, prods[0], 0.0) + jnp.where(tr[1] == t, prods[1], 0.0)

        if e == SLOT[4]:
            return add
        core_arrived(e)
        if e:
            pl.loop(0, NC)(add)
        else:
            for oc in range(NC):
                add(oc)

    pending = [0]
    for step in range(4):
        halves = ((0, 0), (1, 0), (0, 1), (1, 1)) if step < 3 else ((0, 0), (1, 1))
        if step == 3:
            for e in pending:
                forward(e)
            pending = []
        for way, h in halves:
            d = -(step + 1) if way == 0 else step + 1
            arrived(half(hid(SLOT[d], 0), h), S_HZ + way * 8 + step * 2 + h)
            if step < 2 or (step == 2 and h == way):
                step_send(way, step + 1, h)
            core_send(SLOT[d], h)
        for e in pending:
            forward(e)
        pending = [SLOT[step + 1], SLOT[-step - 1]] if step < 3 else [SLOT[4]]
    last = forward(SLOT[4])

    def to_bf16(dst, src, base, more=None):
        @pl.loop(0, 4)
        def _(i):
            value = src[base + i]
            if more is not None:
                value += more[i].astype(F32)
            dst[base + i] = value.astype(BF)

    last(0, (2,))
    core_arrived(SLOT[4])
    last(1, (2,))
    to_bf16(ysend2, agg.at[2], 0)
    send(half(ysend2, 0), yrel.at[0], S_YR + 0, at(dy=1))
    to_bf16(ysend2, agg.at[2], 4)
    send(half(ysend2, 1), yrel.at[1], S_YR + 1, at(dy=-1))
    for oc in range(NC):
        last(oc, (1, 3))
    to_bf16(ysend1, agg.at[1], 4)
    send(half(ysend1, 1), half(yin.at[0], 1), S_YI + 1, at(dy=1))
    to_bf16(ysend3, agg.at[3], 0)
    send(half(ysend3, 0), half(yin.at[1], 0), S_YI + 2, at(dy=-1))
    arrived(yrel.at[0], S_YR + 0)
    to_bf16(ysend1, agg.at[1], 0, yrel.at[0])
    send(half(ysend1, 0), half(yin.at[0], 0), S_YI + 0, at(dy=1))
    arrived(yrel.at[1], S_YR + 1)
    to_bf16(ysend3, agg.at[3], 4, yrel.at[1])
    send(half(ysend3, 1), half(yin.at[1], 1), S_YI + 3, at(dy=-1))
    for oc in range(NC):
        last(oc, (0,))

    bsum[...] = jnp.zeros_like(bsum)
    cot_in.wait()
    bias_in.wait()
    leaving = []
    for h in range(2):
        arrived(half(yin.at[0], h), S_YI + h)
        arrived(half(yin.at[1], h), S_YI + 2 + h)

        @pl.loop(0, 4)
        def _(b, h=h):
            i = 4 * h + b
            r = pl.ds(pl.multiple_of(i * B, B), B)
            pre = agg[0, i] + yin[0, i].astype(F32) + yin[1, i].astype(F32) + bv[...].astype(F32)
            sig = jax.nn.sigmoid(pre)
            ov[r, :] = (pre * sig).astype(BF)
            g = (cv[r, :].astype(F32) * sig * (1.0 + pre * (1.0 - sig))).astype(BF).astype(F32)
            part = g[0:8]
            for j in range(1, 16):
                part += g[8 * j : 8 * j + 8]
            bsum[...] += part
            G[0][i] = g.T.astype(BF)

        send(half(G[0], h), half(G[3], h), S_G + h, at(dy=1))
        send(half(G[0], h), half(G[1], h), S_G + 2 + h, at(dy=-1))
        leaving.append(local(ov.at[rows_of(h)], out.at[rows_of(h)], L_OUT + h))

    def spread(n, base, dst, tail):
        @pl.loop(0, 8)
        def _(j):
            r = pl.ds(pl.multiple_of(j * 16, 16), 16)
            parts = [D[k, r, :] for k in range(n)]
            for t in range(NB):
                acc = jnp.where(base[0] == t, parts[0], 0.0)
                for k in range(1, n):
                    acc += jnp.where(base[k] == t, parts[k], 0.0)
                tail(dst, t, r, acc)

    def add_f32(dst, t, r, acc):
        dst[t, r, :] += acc

    def put_f32(dst, t, r, acc):
        dst[t, r, :] = acc

    def put_bf16(dst, t, r, acc):
        dst[t, r, :] = acc.astype(BF)

    send(bsum, bcore, S_B0, at(oc=1))

    @pl.loop(0, 4)
    def _(i):
        k0 = i * 8
        for j in range(8):
            D[j] = dot(G[0][row_own[0, k0 + j]], TL[i // 2, lax.rem(i, 2) * 2 + j // 4, j % 4])
        spread(8, [src_own[0, k0 + j] for j in range(8)], SL, add_f32)

    arrived(bcore, S_B0)
    bz[z] = bsum[...] + bcore[...]
    for e in range(1, NZ):
        send(bz.at[z], bz.at[z], S_B1 + SLOT[-DIST[e]], at(dz=DIST[e]))

    arrived(half(G[3], 0), S_G + 0)
    send(half(G[3], 0), half(G[2], 0), S_GR + 0, at(dy=1))
    arrived(half(G[1], 1), S_G + 3)
    send(half(G[1], 1), half(G[2], 1), S_GR + 1, at(dy=-1))
    arrived(half(G[1], 0), S_G + 2)
    arrived(half(G[3], 1), S_G + 1)
    for h in range(2):
        arrived(half(G[2], h), S_GR + h)

    def backward(e, oc, dst, tail):
        cc = lax.rem(c + oc, NC)
        blocks = []
        for dy in range(NY):
            for cap in range(CAP):
                D[dy * 2 + cap] = dot(G[dy][slot_row(dy, e, cc, cap)], T[dy, e, cc * 2 + cap])
                blocks.append(slot_block(dy, e, oc, cap))
        spread(8, blocks, dst, tail)

    def combine(dst, e, h, way=None, step=None):
        @pl.loop(0, 4)
        def _(i):
            t = 4 * h + i
            value = S0[e, t] + sibrecv[e, t].astype(F32)
            if step is not None:
                value += zrecv[way, step, t].astype(F32)
            dst[t] = value.astype(BF)

    def ring_send(way, step, h):
        send(
            half(zsend.at[way, step], h), half(zrecv.at[way, step], h), S_ZR + way * 8 + step * 2 + h,
            at(dz=1 if way == 0 else -1),
        )

    def terms(e):
        backward(e, 1, sibsend.at[e], put_bf16)
        send(sibsend.at[e], sibrecv.at[e], S_SIB + e, at(oc=1))
        backward(e, 0, S0.at[e], put_f32)

    def bias_step(step):
        if step == 2:
            for e in range(1, NZ):
                arrived(bz.at[lax.rem(z + DIST[e] + NZ, NZ)], S_B1 + e)
            total = bz[0]
            for k in range(1, NZ):
                total += bz[k]
            by[y] = total
            for d in range(1, NY):
                send(by.at[y], by.at[y], S_B2 + NY - d, at(dy=d))
        elif step == 3:
            for d in range(1, NY):
                arrived(by.at[lax.rem(y + d, NY)], S_B2 + d)
            gbv[...] = jnp.sum(by[0] + by[1] + by[2] + by[3], 0, keepdims=True)
            leaving.append(local(gbv, gb, L_GB))

    terms(SLOT[4])
    arrived(sibrecv.at[SLOT[4]], S_SIB + SLOT[4])
    for way in range(2):
        combine(zsend.at[way, 0], SLOT[4], way)
        ring_send(way, 0, way)
    for step in range(1, 4):
        d = 4 - step
        ends = (SLOT[d], SLOT[-d])
        for e in ends:
            terms(e)
        for e in ends:
            arrived(sibrecv.at[e], S_SIB + e)
        order = ((1, 0), (0, 1), (0, 0), (1, 1)) if step == 1 else ((0, 0), (1, 0), (0, 1), (1, 1))
        for way, h in order:
            came = step > 1 or h == way
            if came:
                arrived(half(zrecv.at[way, step - 1], h), S_ZR + way * 8 + (step - 1) * 2 + h)
            combine(zsend.at[way, step], ends[way], h, way, step - 1 if came else None)
            ring_send(way, step, h)
        bias_step(step)
    terms(0)
    arrived(sibrecv.at[0], S_SIB + 0)

    def terms_x(dx, h, dst, more=None):
        @pl.loop(0, 4, unroll=True)
        def _(b):
            r = pl.ds(pl.multiple_of(512 * h + b * B, B), B)
            value = dot_t(GA[r, :], w_rows(dx))
            if more is not None:
                value += more[pl.ds(pl.multiple_of(b * B, B), B), :].astype(F32)
            dst[r, :] = value.astype(dst.dtype)

    for h in range(2):
        for way in range(2):
            arrived(half(zrecv.at[way, 3], h), S_ZR + way * 8 + 6 + h)

        @pl.loop(0, 4, unroll=True)
        def _(i, h=h):
            t = 4 * h + i
            value = S0[0, t] + sibrecv[0, t].astype(F32) + SL[t]
            value += zrecv[0, 3, t].astype(F32) + zrecv[1, 3, t].astype(F32)
            value = value.astype(BF).astype(F32)
            GAT[:, pl.ds(pl.multiple_of(t * B, B), B)] = value.astype(BF)
            GA[pl.ds(pl.multiple_of(t * B, B), B), :] = value.T.astype(BF)

        if h == 0:
            terms_x(2, 0, xsend2)
            send(xsend2.at[rows_of(0)], xrel.at[0], S_XR + 0, at(dx=1))
            terms_x(3, 0, xsend3)
            send(xsend3.at[rows_of(0)], xin.at[1, rows_of(0)], S_XI + 2, at(dx=-1))

    def weight_terms(core):
        for i in range(2):
            dx = lax.rem(core * 2 + i - x + NX, NX)
            gws[core, B * i : B * i + B, :] = dot(GAT[...], F[dx]).T

    weight_terms(1 - c)
    send(gws.at[1 - c], arc, S_A0, at(oc=1))
    weight_terms(c)
    terms_x(2, 1, xsend2)
    send(xsend2.at[rows_of(1)], xrel.at[1], S_XR + 1, at(dx=-1))

    arrived(arc, S_A0)
    for k in range(NZ):
        value = gws[c, 32 * k : 32 * k + 32, :] + arc[32 * k : 32 * k + 32, :]
        arown[k] = value
        arsend[k] = value.astype(BF)
    for e in range(NZ - 1, 0, -1):
        send(arsend.at[lax.rem(z + DIST[e] + NZ, NZ)], arin.at[z], S_A1 + SLOT[-DIST[e]], at(dz=DIST[e]))
    terms_x(1, 1, xsend1)
    send(xsend1.at[rows_of(1)], xin.at[0, rows_of(1)], S_XI + 1, at(dx=1))

    arrived(xrel.at[0], S_XR + 0)
    terms_x(1, 0, xsend1, xrel.at[0])
    send(xsend1.at[rows_of(0)], xin.at[0, rows_of(0)], S_XI + 0, at(dx=1))
    terms_x(0, 0, PT)
    arrived(xrel.at[1], S_XR + 1)
    terms_x(3, 1, xsend3, xrel.at[1])
    send(xsend3.at[rows_of(1)], xin.at[1, rows_of(1)], S_XI + 3, at(dx=-1))

    total = arown[z]
    for e in range(1, NZ):
        k = lax.rem(z + DIST[e] + NZ, NZ)
        arrived(arin.at[k], S_A1 + e)
        total += arin[k].astype(F32)
    ar2in[y] = total
    for d in range(1, NY):
        send(ar2in.at[y], ar2in.at[y], S_A2 + NY - d, at(dy=d))
    terms_x(0, 1, PT)
    for d in range(1, NY):
        arrived(ar2in.at[lax.rem(y + d, NY)], S_A2 + d)
    gwall[c, z] = (ar2in[0] + ar2in[1] + ar2in[2] + ar2in[3]).astype(BF)
    for e in range(NZ - 1, 0, -1):
        send(gwall.at[c, z], gwall.at[c, z], S_A3 + SLOT[-DIST[e]], at(dz=DIST[e]))

    def input_gradient(h):
        arrived(xin.at[0, rows_of(h)], S_XI + h)
        arrived(xin.at[1, rows_of(h)], S_XI + 2 + h)

        @pl.loop(0, 4, unroll=True)
        def _(b):
            r = pl.ds(pl.multiple_of(512 * h + b * B, B), B)
            giv[r, :] = (PT[r, :] + xin[0, r, :].astype(F32) + xin[1, r, :].astype(F32)).astype(BF)

        leaving.append(local(giv.at[rows_of(h)], gin.at[rows_of(h)], L_GIN + h))

    input_gradient(0)
    input_gradient(1)
    for e in range(1, NZ):
        arrived(gwall.at[c, lax.rem(z + DIST[e] + NZ, NZ)], S_A3 + e)
    send(gwall.at[c], gwall.at[c], S_A4, at(oc=1))
    arrived(gwall.at[1 - c], S_A4)
    for k in range(NC):
        gwf[k] = gwall[k].astype(F32)
    leaving.append(local(gwf, gw, L_GW))
    for made in leaving:
        made.wait()
    for made in started:
        made.wait_send()


def hand_over(*refs):
    given, result, held, sem = refs[0:4], refs[4:8], refs[8:12], refs[12]
    reads = [pltpu.make_async_copy(given[k], held[k], sem.at[k]) for k in range(4)]
    writes = [pltpu.make_async_copy(held[k], result[k], sem.at[4 + k]) for k in range(4)]
    for made in reads:
        made.start()
    for k in range(4):
        reads[k].wait()
        writes[k].start()
    for made in writes:
        made.wait()


def shards(
    features, weight, bias, cotangent, tile_vals, tile_row, tile_src, send_blocks, send_count
):
    blocks = lambda *lead, dtype=BF: pltpu.VMEM((*lead, B, B), dtype)
    scratch = [
        pltpu.VMEM((NX, 1024, B), BF),
        blocks(NB),
        blocks(NB),
        *[blocks(NC, NB) for _ in range(NZ - 2)],
        blocks(NB),
        blocks(NB),
        blocks(NY, NZ, 4),
        blocks(2, 4, 4),
        blocks(4),
        blocks(NY, NB, dtype=F32),
        blocks(NB),
        blocks(NB),
        blocks(NB),
        blocks(2, 4),
        blocks(2, NB),
        *[blocks(NB + 1) for _ in range(NY)],
        blocks(8, dtype=F32),
        blocks(NZ, NB, dtype=F32),
        blocks(NB, dtype=F32),
        blocks(2, 4, NB),
        blocks(2, 4, NB),
        blocks(NZ, NB),
        blocks(NZ, NB),
        pltpu.VMEM((B, 1024), BF),
        pltpu.VMEM((1024, B), BF),
        pltpu.VMEM((1024, B), F32),
        pltpu.VMEM((1024, B), BF),
        pltpu.VMEM((1024, B), BF),
        pltpu.VMEM((1024, B), BF),
        pltpu.VMEM((2, 512, B), BF),
        pltpu.VMEM((2, 1024, B), BF),
        pltpu.VMEM((8, B), F32),
        pltpu.VMEM((8, B), F32),
        pltpu.VMEM((NZ, 8, B), F32),
        pltpu.VMEM((NY, 8, B), F32),
        pltpu.VMEM((NC, 256, B), F32),
        pltpu.VMEM((256, B), F32),
        pltpu.VMEM((NZ, 32, B), F32),
        pltpu.VMEM((NZ, 32, B), BF),
        pltpu.VMEM((NZ, 32, B), BF),
        pltpu.VMEM((NY, 32, B), F32),
        pltpu.VMEM((NC, NZ, 32, B), BF),
        pltpu.VMEM((NC, NZ, 32, B), F32),
        pltpu.VMEM((512, B), BF),
        pltpu.VMEM((1024, B), BF),
        pltpu.VMEM((1, B), BF),
        pltpu.VMEM((1024, B), BF),
        pltpu.VMEM((1024, B), BF),
        pltpu.VMEM((1, B), F32),
        pltpu.VMEM((NC, NZ, CAP, 64), jnp.int32),
        pltpu.VMEM((NY, 1, 160), jnp.int32),
        pltpu.SMEM((NC, NZ, CAP, 64), jnp.int32),
        pltpu.SMEM((NY, 1, 160), jnp.int32),
        pltpu.SemaphoreType.DMA((S_SEND,)),
        pltpu.SemaphoreType.DMA((S_RECV,)),
        pltpu.SemaphoreType.DMA((L_N + NZ,)),
    ]
    anywhere = pl.BlockSpec(memory_space=pl.ANY)
    smem = pl.BlockSpec(memory_space=pltpu.SMEM)
    shapes = (
        jax.ShapeDtypeStruct((1024, B), BF),
        jax.ShapeDtypeStruct((1024, B), BF),
        jax.ShapeDtypeStruct((NC, NZ, 32, B), F32),
        jax.ShapeDtypeStruct((1, B), F32),
    )
    results = pl.pallas_call(
        kernel,
        out_shape=shapes,
        in_specs=[anywhere] * 7 + [smem] * 2,
        out_specs=(anywhere,) * 4,
        scratch_shapes=scratch,
        compiler_params=pltpu.CompilerParams(
            collective_id=0, has_side_effects=True, vmem_limit_bytes=56 * 2**20
        ),
    )(
        features,
        weight,
        bias.reshape(1, B),
        cotangent,
        tile_vals.reshape(10, 4, 4, B, B),
        send_blocks.transpose(0, 2, 1).reshape(CAP, 64),
        tile_row,
        tile_row,
        tile_src,
    )
    out, gin, gw, gb = pl.pallas_call(
        hand_over,
        out_shape=shapes,
        in_specs=[anywhere] * 4,
        out_specs=(anywhere,) * 4,
        scratch_shapes=[pltpu.VMEM(a.shape, a.dtype) for a in shapes] + [pltpu.SemaphoreType.DMA((8,))],
        compiler_params=pltpu.CompilerParams(vmem_limit_bytes=60 * 2**20),
    )(*results)
    return out, gin, gw.reshape(512, B), gb.reshape(B)


def solution(mesh):
    in_specs = (
        P("dom", "rep"),
        P(None, "rep"),
        P("rep"),
        P("dom", "rep"),
        P("dom", None, None, None),
        P("dom", None),
        P("dom", None),
        P("dom", None, None),
        P("dom", None),
    )
    out_specs = (P("dom", "rep"), P("dom", "rep"), P(None, "rep"), P("rep"))
    return jax.shard_map(shards, mesh=mesh, in_specs=in_specs, out_specs=out_specs, check_vma=False)
```

```python
import jax
import jax.numpy as jnp
from jax import lax
from jax.experimental import pallas as pl
from jax.experimental.pallas import tpu as pltpu
from jax.sharding import PartitionSpec as P

B = 128
NB = 8
CAP = 2
NX, NY, NZ, NC = 4, 4, 8, 2
MESH = pl.DeviceIdType.MESH
BF = jnp.bfloat16
F32 = jnp.float32

DIST = [0, 1, -1, 2, -2, 3, -3, 4]
SLOT = {d: e for e, d in enumerate(DIST)}
SLOT[-4] = SLOT[4]


def dot(a, b):
    return lax.dot_general(a, b, (((1,), (0,)), ((), ())), preferred_element_type=F32)


def dot_t(a, b):
    return lax.dot_general(a, b, (((1,), (1,)), ((), ())), preferred_element_type=F32)


class Semaphores:
    def __init__(self):
        self.n = 0

    def take(self, count):
        first = self.n
        self.n += count
        return first


S = Semaphores()
S_FEAT = S.take(4)
S_FREL = S.take(2)
S_SB = S.take(8)
S_ROW = S.take(4)
S_TY = S.take(16)
S_TQ = S.take(8)
S_HZ = S.take(16)
S_HC = S.take(16)
S_YR = S.take(2)
S_YI = S.take(4)
S_G = S.take(4)
S_GR = S.take(2)
S_SIB = S.take(8)
S_ZR = S.take(16)
S_XR = S.take(2)
S_XI = S.take(4)
S_SBC = S.take(1)
S_TR = S.take(1)
S_B0 = S.take(1)
S_B1 = S.take(8)
S_B2 = S.take(4)
S_A0 = S.take(1)
S_A1 = S.take(8)
S_A2 = S.take(4)
S_A3 = S.take(8)
S_A4 = S.take(1)
S_RECV = S.n
S_TF = S_RECV
S_SEND = 64
L_LOC, L_SB, L_ROW, L_FEAT, L_W, L_COT, L_BIAS, L_OUT, L_GIN, L_GW, L_GB, L_N = 0, 1, 2, 3, 4, 5, 6, 7, 9, 11, 12, 13


def kernel(
    feat, weight, bias, cot, tiles, sendb, trow, row_own, src_own,
    out, gin, gw, gb,
    F, Hown, Hcore, H1, H2, H3, H4, H5, H6, Hlast, Hlastcore, T, TL, trel, agg, ysend2, ysend1, ysend3, yrel, yin, G0, G1, G2, G3, D, S0, SL,
    zsend, zrecv, sibsend, sibrecv, GAT, GA, PT, xsend2, xsend1, xsend3, xrel, xin, bsum, bcore, bz, by, gws, arc, arown, arsend, arin, ar2in, gwall, gwf,
    wv, cv, bv, ov, giv, gbv, sbv, rowv, sbs, rows, ssem, rsem, lsem,
):
    H = [(Hown, Hcore), H1, H2, H3, H4, H5, H6, (Hlast, Hlastcore)]
    G = [G0, G1, G2, G3]

    def hid(e, oc):
        return H[e][oc] if isinstance(H[e], tuple) else H[e].at[oc]

    dom, x = lax.axis_index("dom"), lax.axis_index("rep")
    z = dom // (NY * NC)
    y = lax.rem(dom // NC, NY)
    c = lax.rem(dom, NC)

    def at(dx=0, dy=0, dz=0, oc=0):
        zz = lax.rem(z + dz + NZ, NZ)
        yy = lax.rem(y + dy + NY, NY)
        cc = lax.rem(c + oc, NC)
        return ((zz * NY + yy) * NC + cc, lax.rem(x + dx + NX, NX))

    started = []

    def copy(src, dst, sem, dev, recv=None):
        return pltpu.make_async_remote_copy(
            src_ref=src,
            dst_ref=dst,
            send_sem=ssem.at[len(started) % S_SEND],
            recv_sem=rsem.at[sem if recv is None else recv],
            device_id=dev,
            device_id_type=MESH,
        )

    def send(src, dst, sem, dev, recv=None):
        if len(started) >= S_SEND:
            started[len(started) - S_SEND].wait_send()
        made = copy(src, dst, sem, dev, recv)
        made.start()
        started.append(made)

    here = (dom, x)

    def arrived(dst, sem):
        pltpu.make_async_remote_copy(
            src_ref=dst, dst_ref=dst, send_sem=ssem.at[0], recv_sem=rsem.at[sem], device_id=here, device_id_type=MESH
        ).wait_recv()

    half = lambda ref, h: ref.at[pl.ds(4 * h, 4)]

    def local(src, dst, sem):
        made = pltpu.make_async_copy(src, dst, lsem.at[sem])
        made.start()
        return made

    feat_in = local(feat, F.at[0], L_FEAT)
    weight_in = local(weight, wv, L_W)
    loc_tiles = local(tiles.at[pl.ds(0, 2)], TL, L_LOC)
    own_tiles = [
        local(tiles.at[2 + lax.rem(z + DIST[e] + NZ, NZ), y], T.at[0, e], L_N + e) for e in range(NZ)
    ]
    cot_in = local(cot, cv, L_COT)
    bias_in = local(bias, bv, L_BIAS)

    barrier = pltpu.get_barrier_semaphore()
    peers = [at(dz=DIST[e]) for e in range(1, NZ)] + [at(oc=1)]
    peers += [at(dy=d) for d in range(1, NY)] + [at(dx=d) for d in range(1, NX)]
    for dev in peers:
        pl.semaphore_signal(barrier, inc=1, device_id=dev, device_id_type=MESH)
    pl.semaphore_wait(barrier, len(peers))

    rows_of = lambda h: pl.ds(512 * h, 512)
    feat_in.wait()
    for h, g in ((0, 1), (1, 0)):
        send(F.at[0, rows_of(h)], F.at[3, rows_of(h)], S_FEAT + h, at(dx=1))
        send(F.at[0, rows_of(g)], F.at[1, rows_of(g)], S_FEAT + 2 + g, at(dx=-1))

    for e in range(1, NZ):
        back = SLOT[-DIST[e]]
        send(sendb, sbv.at[0, back], S_SB + back, at(dz=DIST[e]))
    for d in range(1, NY):
        send(trow, rowv.at[NY - d], S_ROW + NY - d, at(dy=d))
    sb_in = local(sendb, sbv.at[0, 0], L_SB)
    row_in = local(trow, rowv.at[0], L_ROW)

    def tile_slot(e):
        d = jnp.where(lax.rem(e, 2) == 1, (e + 1) // 2, NZ - e // 2)
        return 2 + lax.rem(z + d, NZ)

    far = lax.rem(y + 2, NY)
    send(tiles.at[tile_slot(x), far], T.at[2, x], S_TF + 6, at(dy=2), S_TQ + x)
    send(tiles.at[tile_slot(x + 4), far], trel, S_TR, at(dy=-1))

    def near_tiles(slots):
        for e in slots:
            for dy, to, base in ((1, 3, 0), (-1, 1, 8)):
                send(
                    tiles.at[2 + lax.rem(z + DIST[e] + NZ, NZ), lax.rem(y + dy + NY, NY)],
                    T.at[to, e],
                    S_TY + base + e,
                    at(dy=dy),
                )

    near_tiles(range(2))

    for dy in range(NY):
        G[dy][NB] = jnp.zeros((B, B), BF)

    @pl.loop(0, NB)
    def _(i):
        for dy in range(NY):
            agg[dy, i] = jnp.zeros((B, B), F32)
        SL[i] = jnp.zeros((B, B), F32)

    arrived(F.at[3, rows_of(0)], S_FEAT + 0)
    send(F.at[3, rows_of(0)], F.at[2, rows_of(0)], S_FREL + 0, at(dx=1))
    arrived(F.at[1, rows_of(1)], S_FEAT + 3)
    send(F.at[1, rows_of(1)], F.at[2, rows_of(1)], S_FREL + 1, at(dx=-1))
    arrived(F.at[1, rows_of(0)], S_FEAT + 2)
    arrived(F.at[3, rows_of(1)], S_FEAT + 1)

    def w_rows(dx):
        return wv[pl.ds(pl.multiple_of(lax.rem(x + dx, NX) * B, B), B), :]

    def step_send(way, step, h):
        d = -step if way == 0 else step
        nd = d - 1 if way == 0 else d + 1
        send(
            half(hid(SLOT[d], 0), h), half(hid(SLOT[nd], 0), h), S_HZ + way * 8 + step * 2 + h,
            at(dz=1 if way == 0 else -1),
        )

    def core_send(e, h):
        send(half(hid(e, 0), h), half(hid(e, 1), h), S_HC + e * 2 + h, at(oc=1))

    weight_in.wait()

    @pl.loop(0, 4)
    def _(k):
        for i in range(2):
            r = pl.ds(pl.multiple_of((2 * k + i) * B, B), B)
            PT[r, :] = dot(F[0, r], w_rows(0)) + dot(F[1, r], w_rows(1)) + dot(F[3, r], w_rows(3))

    for h in range(2):
        arrived(F.at[2, rows_of(h)], S_FREL + h)
        for b in range(4 * h, 4 * h + 4):
            r = pl.ds(b * B, B)
            Hown[b] = (PT[r, :] + dot(F[2, r], w_rows(2))).astype(BF)

        step_send(0, 0, h)
        step_send(1, 0, h)
        core_send(0, h)

    arrived(trel, S_TR)
    send(trel, T.at[2, x + 4], S_TQ, at(dy=-1), S_TQ + x + 4)
    near_tiles(range(2, NZ))

    def far_tiles(k):
        e = x + 4 * k
        arrived(T.at[2, e], S_TQ + e)
        for i, dx in enumerate((1, -1, 2)):
            send(T.at[2, e], T.at[2, e], S_TF + k * 3 + i, at(dx=dx), S_TQ + e)

    far_tiles(0)

    sb_in.wait()
    row_in.wait()
    for e in range(1, NZ):
        arrived(sbv.at[0, e], S_SB + e)
    send(sbv.at[0], sbv.at[1], S_SBC, at(oc=1))
    for d in range(1, NY):
        arrived(rowv.at[d], S_ROW + d)

    arrived(sbv.at[1], S_SBC)
    to_s = [local(sbv, sbs, L_SB), local(rowv, rows, L_ROW)]

    loc_tiles.wait()

    @pl.loop(0, 8)
    def _(i):
        k = i * 4
        prods = [dot(TL[i // 4, lax.rem(i, 4), j], Hown[src_own[0, k + j]]) for j in range(4)]
        tr = [row_own[0, k + j] for j in range(4)]
        for t in range(NB):
            add = jnp.where(tr[0] == t, prods[0], 0.0)
            for j in range(1, 4):
                add += jnp.where(tr[j] == t, prods[j], 0.0)
            agg[0, t] += add

    far_tiles(1)
    for made in to_s:
        made.wait()

    for made in own_tiles:
        made.wait()

    def slot_row(dy, e, cc, cap):
        zz = lax.rem(z + DIST[e] + NZ, NZ)
        return rows[dy, 0, 32 + zz * 16 + y * 4 + cc * 2 + cap]

    def slot_block(dy, e, oc, cap):
        target = (z * NY + lax.rem(y + dy, NY)) * NC + c
        return sbs[oc, e, cap, target]

    def core_arrived(e):
        for h in range(2):
            arrived(half(hid(e, 1), h), S_HC + e * 2 + h)

    def forward(e):
        for dy, base in ((3, 0), (1, 8)):
            arrived(T.at[dy, e], S_TY + base + e)

        @pl.when(x != e % 4)
        def _():
            arrived(T.at[2, e], S_TQ + e)

        def add(oc, dys=range(NY)):
            cc = lax.rem(c + oc, NC)
            for dy in dys:
                prods, tr = [], []
                for cap in range(CAP):
                    t, b = T[dy, e, cc * 2 + cap], slot_block(dy, e, oc, cap)
                    prods.append(dot(t, H[e][oc][b] if isinstance(H[e], tuple) else H[e][oc, b]))
                    tr.append(slot_row(dy, e, cc, cap))
                for t in range(NB):
                    agg[dy, t] += jnp.where(tr[0] == t, prods[0], 0.0) + jnp.where(tr[1] == t, prods[1], 0.0)

        if e == SLOT[4]:
            return add
        core_arrived(e)
        if e:
            pl.loop(0, NC)(add)
        else:
            for oc in range(NC):
                add(oc)

    pending = [0]
    for step in range(4):
        halves = ((0, 0), (1, 0), (0, 1), (1, 1)) if step < 3 else ((0, 0), (1, 1))
        if step == 3:
            for e in pending:
                forward(e)
            pending = []
        for way, h in halves:
            d = -(step + 1) if way == 0 else step + 1
            arrived(half(hid(SLOT[d], 0), h), S_HZ + way * 8 + step * 2 + h)
            if step < 2 or (step == 2 and h == way):
                step_send(way, step + 1, h)
            core_send(SLOT[d], h)
        for e in pending:
            forward(e)
        pending = [SLOT[step + 1], SLOT[-step - 1]] if step < 3 else [SLOT[4]]
    last = forward(SLOT[4])

    def to_bf16(dst, src, base, more=None):
        @pl.loop(0, 4)
        def _(i):
            value = src[base + i]
            if more is not None:
                value += more[i].astype(F32)
            dst[base + i] = value.astype(BF)

    last(0, (2,))
    core_arrived(SLOT[4])
    last(1, (2,))
    to_bf16(ysend2, agg.at[2], 0)
    send(half(ysend2, 0), yrel.at[0], S_YR + 0, at(dy=1))
    to_bf16(ysend2, agg.at[2], 4)
    send(half(ysend2, 1), yrel.at[1], S_YR + 1, at(dy=-1))
    for oc in range(NC):
        last(oc, (1, 3))
    to_bf16(ysend1, agg.at[1], 4)
    send(half(ysend1, 1), half(yin.at[0], 1), S_YI + 1, at(dy=1))
    to_bf16(ysend3, agg.at[3], 0)
    send(half(ysend3, 0), half(yin.at[1], 0), S_YI + 2, at(dy=-1))
    arrived(yrel.at[0], S_YR + 0)
    to_bf16(ysend1, agg.at[1], 0, yrel.at[0])
    send(half(ysend1, 0), half(yin.at[0], 0), S_YI + 0, at(dy=1))
    arrived(yrel.at[1], S_YR + 1)
    to_bf16(ysend3, agg.at[3], 4, yrel.at[1])
    send(half(ysend3, 1), half(yin.at[1], 1), S_YI + 3, at(dy=-1))
    for oc in range(NC):
        last(oc, (0,))

    bsum[...] = jnp.zeros_like(bsum)
    cot_in.wait()
    bias_in.wait()
    leaving = []
    for h in range(2):
        arrived(half(yin.at[0], h), S_YI + h)
        arrived(half(yin.at[1], h), S_YI + 2 + h)

        @pl.loop(0, 4)
        def _(b, h=h):
            i = 4 * h + b
            r = pl.ds(pl.multiple_of(i * B, B), B)
            pre = agg[0, i] + yin[0, i].astype(F32) + yin[1, i].astype(F32) + bv[...].astype(F32)
            sig = jax.nn.sigmoid(pre)
            ov[r, :] = (pre * sig).astype(BF)
            g = (cv[r, :].astype(F32) * sig * (1.0 + pre * (1.0 - sig))).astype(BF).astype(F32)
            part = g[0:8]
            for j in range(1, 16):
                part += g[8 * j : 8 * j + 8]
            bsum[...] += part
            G[0][i] = g.T.astype(BF)

        send(half(G[0], h), half(G[3], h), S_G + h, at(dy=1))
        send(half(G[0], h), half(G[1], h), S_G + 2 + h, at(dy=-1))
        leaving.append(local(ov.at[rows_of(h)], out.at[rows_of(h)], L_OUT + h))

    def spread(n, base, dst, tail):
        @pl.loop(0, 8)
        def _(j):
            r = pl.ds(pl.multiple_of(j * 16, 16), 16)
            parts = [D[k, r, :] for k in range(n)]
            for t in range(NB):
                acc = jnp.where(base[0] == t, parts[0], 0.0)
                for k in range(1, n):
                    acc += jnp.where(base[k] == t, parts[k], 0.0)
                tail(dst, t, r, acc)

    def add_f32(dst, t, r, acc):
        dst[t, r, :] += acc

    def put_f32(dst, t, r, acc):
        dst[t, r, :] = acc

    def put_bf16(dst, t, r, acc):
        dst[t, r, :] = acc.astype(BF)

    send(bsum, bcore, S_B0, at(oc=1))

    @pl.loop(0, 4)
    def _(i):
        k0 = i * 8
        for j in range(8):
            D[j] = dot(G[0][row_own[0, k0 + j]], TL[i // 2, lax.rem(i, 2) * 2 + j // 4, j % 4])
        spread(8, [src_own[0, k0 + j] for j in range(8)], SL, add_f32)

    arrived(bcore, S_B0)
    bz[z] = bsum[...] + bcore[...]
    for e in range(1, NZ):
        send(bz.at[z], bz.at[z], S_B1 + SLOT[-DIST[e]], at(dz=DIST[e]))

    arrived(half(G[3], 0), S_G + 0)
    send(half(G[3], 0), half(G[2], 0), S_GR + 0, at(dy=1))
    arrived(half(G[1], 1), S_G + 3)
    send(half(G[1], 1), half(G[2], 1), S_GR + 1, at(dy=-1))
    arrived(half(G[1], 0), S_G + 2)
    arrived(half(G[3], 1), S_G + 1)
    for h in range(2):
        arrived(half(G[2], h), S_GR + h)

    def backward(e, oc, dst, tail):
        cc = lax.rem(c + oc, NC)
        blocks = []
        for dy in range(NY):
            for cap in range(CAP):
                D[dy * 2 + cap] = dot(G[dy][slot_row(dy, e, cc, cap)], T[dy, e, cc * 2 + cap])
                blocks.append(slot_block(dy, e, oc, cap))
        spread(8, blocks, dst, tail)

    def combine(dst, e, h, way=None, step=None):
        @pl.loop(0, 4)
        def _(i):
            t = 4 * h + i
            value = S0[e, t] + sibrecv[e, t].astype(F32)
            if step is not None:
                value += zrecv[way, step, t].astype(F32)
            dst[t] = value.astype(BF)

    def ring_send(way, step, h):
        send(
            half(zsend.at[way, step], h), half(zrecv.at[way, step], h), S_ZR + way * 8 + step * 2 + h,
            at(dz=1 if way == 0 else -1),
        )

    def terms(e):
        backward(e, 1, sibsend.at[e], put_bf16)
        send(sibsend.at[e], sibrecv.at[e], S_SIB + e, at(oc=1))
        backward(e, 0, S0.at[e], put_f32)

    def bias_step(step):
        if step == 2:
            for e in range(1, NZ):
                arrived(bz.at[lax.rem(z + DIST[e] + NZ, NZ)], S_B1 + e)
            total = bz[0]
            for k in range(1, NZ):
                total += bz[k]
            by[y] = total
            for d in range(1, NY):
                send(by.at[y], by.at[y], S_B2 + NY - d, at(dy=d))
        elif step == 3:
            for d in range(1, NY):
                arrived(by.at[lax.rem(y + d, NY)], S_B2 + d)
            gbv[...] = jnp.sum(by[0] + by[1] + by[2] + by[3], 0, keepdims=True)
            leaving.append(local(gbv, gb, L_GB))

    terms(SLOT[4])
    arrived(sibrecv.at[SLOT[4]], S_SIB + SLOT[4])
    for way in range(2):
        combine(zsend.at[way, 0], SLOT[4], way)
        ring_send(way, 0, way)
    for step in range(1, 4):
        d = 4 - step
        ends = (SLOT[d], SLOT[-d])
        for e in ends:
            terms(e)
        for e in ends:
            arrived(sibrecv.at[e], S_SIB + e)
        order = ((1, 0), (0, 1), (0, 0), (1, 1)) if step == 1 else ((0, 0), (1, 0), (0, 1), (1, 1))
        for way, h in order:
            came = step > 1 or h == way
            if came:
                arrived(half(zrecv.at[way, step - 1], h), S_ZR + way * 8 + (step - 1) * 2 + h)
            combine(zsend.at[way, step], ends[way], h, way, step - 1 if came else None)
            ring_send(way, step, h)
        bias_step(step)
    terms(0)
    arrived(sibrecv.at[0], S_SIB + 0)

    def terms_x(dx, h, dst, more=None):
        @pl.loop(0, 4, unroll=True)
        def _(b):
            r = pl.ds(pl.multiple_of(512 * h + b * B, B), B)
            value = dot_t(GA[r, :], w_rows(dx))
            if more is not None:
                value += more[pl.ds(pl.multiple_of(b * B, B), B), :].astype(F32)
            dst[r, :] = value.astype(dst.dtype)

    for h in range(2):
        for way in range(2):
            arrived(half(zrecv.at[way, 3], h), S_ZR + way * 8 + 6 + h)

        @pl.loop(0, 4, unroll=True)
        def _(i, h=h):
            t = 4 * h + i
            value = S0[0, t] + sibrecv[0, t].astype(F32) + SL[t]
            value += zrecv[0, 3, t].astype(F32) + zrecv[1, 3, t].astype(F32)
            value = value.astype(BF).astype(F32)
            GAT[:, pl.ds(pl.multiple_of(t * B, B), B)] = value.astype(BF)
            GA[pl.ds(pl.multiple_of(t * B, B), B), :] = value.T.astype(BF)

        if h == 0:
            terms_x(2, 0, xsend2)
            send(xsend2.at[rows_of(0)], xrel.at[0], S_XR + 0, at(dx=1))
            terms_x(3, 0, xsend3)
            send(xsend3.at[rows_of(0)], xin.at[1, rows_of(0)], S_XI + 2, at(dx=-1))

    def weight_terms(core):
        for i in range(2):
            dx = lax.rem(core * 2 + i - x + NX, NX)
            gws[core, B * i : B * i + B, :] = dot(GAT[...], F[dx]).T

    weight_terms(1 - c)
    send(gws.at[1 - c], arc, S_A0, at(oc=1))
    weight_terms(c)
    terms_x(2, 1, xsend2)
    send(xsend2.at[rows_of(1)], xrel.at[1], S_XR + 1, at(dx=-1))

    arrived(arc, S_A0)
    for k in range(NZ):
        value = gws[c, 32 * k : 32 * k + 32, :] + arc[32 * k : 32 * k + 32, :]
        arown[k] = value
        arsend[k] = value.astype(BF)
    for e in range(NZ - 1, 0, -1):
        send(arsend.at[lax.rem(z + DIST[e] + NZ, NZ)], arin.at[z], S_A1 + SLOT[-DIST[e]], at(dz=DIST[e]))
    terms_x(1, 1, xsend1)
    send(xsend1.at[rows_of(1)], xin.at[0, rows_of(1)], S_XI + 1, at(dx=1))

    arrived(xrel.at[0], S_XR + 0)
    terms_x(1, 0, xsend1, xrel.at[0])
    send(xsend1.at[rows_of(0)], xin.at[0, rows_of(0)], S_XI + 0, at(dx=1))
    terms_x(0, 0, PT)
    arrived(xrel.at[1], S_XR + 1)
    terms_x(3, 1, xsend3, xrel.at[1])
    send(xsend3.at[rows_of(1)], xin.at[1, rows_of(1)], S_XI + 3, at(dx=-1))

    total = arown[z]
    for e in range(1, NZ):
        k = lax.rem(z + DIST[e] + NZ, NZ)
        arrived(arin.at[k], S_A1 + e)
        total += arin[k].astype(F32)
    ar2in[y] = total
    for d in range(1, NY):
        send(ar2in.at[y], ar2in.at[y], S_A2 + NY - d, at(dy=d))
    terms_x(0, 1, PT)
    for d in range(1, NY):
        arrived(ar2in.at[lax.rem(y + d, NY)], S_A2 + d)
    gwall[c, z] = (ar2in[0] + ar2in[1] + ar2in[2] + ar2in[3]).astype(BF)
    for e in range(NZ - 1, 0, -1):
        send(gwall.at[c, z], gwall.at[c, z], S_A3 + SLOT[-DIST[e]], at(dz=DIST[e]))

    def input_gradient(h):
        arrived(xin.at[0, rows_of(h)], S_XI + h)
        arrived(xin.at[1, rows_of(h)], S_XI + 2 + h)

        @pl.loop(0, 4, unroll=True)
        def _(b):
            r = pl.ds(pl.multiple_of(512 * h + b * B, B), B)
            giv[r, :] = (PT[r, :] + xin[0, r, :].astype(F32) + xin[1, r, :].astype(F32)).astype(BF)

        leaving.append(local(giv.at[rows_of(h)], gin.at[rows_of(h)], L_GIN + h))

    input_gradient(0)
    input_gradient(1)
    for e in range(1, NZ):
        arrived(gwall.at[c, lax.rem(z + DIST[e] + NZ, NZ)], S_A3 + e)
    send(gwall.at[c], gwall.at[c], S_A4, at(oc=1))
    arrived(gwall.at[1 - c], S_A4)
    for k in range(NC):
        gwf[k] = gwall[k].astype(F32)
    leaving.append(local(gwf, gw, L_GW))
    for made in leaving:
        made.wait()
    for made in started[-S_SEND:]:
        made.wait_send()


def hand_over(*refs):
    given, result, held, sem = refs[0:4], refs[4:8], refs[8:12], refs[12]
    reads = [pltpu.make_async_copy(given[k], held[k], sem.at[k]) for k in range(4)]
    writes = [pltpu.make_async_copy(held[k], result[k], sem.at[4 + k]) for k in range(4)]
    for made in reads:
        made.start()
    for k in range(4):
        reads[k].wait()
        writes[k].start()
    for made in writes:
        made.wait()


def shards(
    features, weight, bias, cotangent, tile_vals, tile_row, tile_src, send_blocks, send_count
):
    blocks = lambda *lead, dtype=BF: pltpu.VMEM((*lead, B, B), dtype)
    scratch = [
        pltpu.VMEM((NX, 1024, B), BF),
        blocks(NB),
        blocks(NB),
        *[blocks(NC, NB) for _ in range(NZ - 2)],
        blocks(NB),
        blocks(NB),
        blocks(NY, NZ, 4),
        blocks(2, 4, 4),
        blocks(4),
        blocks(NY, NB, dtype=F32),
        blocks(NB),
        blocks(NB),
        blocks(NB),
        blocks(2, 4),
        blocks(2, NB),
        *[blocks(NB + 1) for _ in range(NY)],
        blocks(8, dtype=F32),
        blocks(NZ, NB, dtype=F32),
        blocks(NB, dtype=F32),
        blocks(2, 4, NB),
        blocks(2, 4, NB),
        blocks(NZ, NB),
        blocks(NZ, NB),
        pltpu.VMEM((B, 1024), BF),
        pltpu.VMEM((1024, B), BF),
        pltpu.VMEM((1024, B), F32),
        pltpu.VMEM((1024, B), BF),
        pltpu.VMEM((1024, B), BF),
        pltpu.VMEM((1024, B), BF),
        pltpu.VMEM((2, 512, B), BF),
        pltpu.VMEM((2, 1024, B), BF),
        pltpu.VMEM((8, B), F32),
        pltpu.VMEM((8, B), F32),
        pltpu.VMEM((NZ, 8, B), F32),
        pltpu.VMEM((NY, 8, B), F32),
        pltpu.VMEM((NC, 256, B), F32),
        pltpu.VMEM((256, B), F32),
        pltpu.VMEM((NZ, 32, B), F32),
        pltpu.VMEM((NZ, 32, B), BF),
        pltpu.VMEM((NZ, 32, B), BF),
        pltpu.VMEM((NY, 32, B), F32),
        pltpu.VMEM((NC, NZ, 32, B), BF),
        pltpu.VMEM((NC, NZ, 32, B), F32),
        pltpu.VMEM((512, B), BF),
        pltpu.VMEM((1024, B), BF),
        pltpu.VMEM((1, B), BF),
        pltpu.VMEM((1024, B), BF),
        pltpu.VMEM((1024, B), BF),
        pltpu.VMEM((1, B), F32),
        pltpu.VMEM((NC, NZ, CAP, 64), jnp.int32),
        pltpu.VMEM((NY, 1, 160), jnp.int32),
        pltpu.SMEM((NC, NZ, CAP, 64), jnp.int32),
        pltpu.SMEM((NY, 1, 160), jnp.int32),
        pltpu.SemaphoreType.DMA((S_SEND,)),
        pltpu.SemaphoreType.DMA((S_RECV,)),
        pltpu.SemaphoreType.DMA((L_N + NZ,)),
    ]
    anywhere = pl.BlockSpec(memory_space=pl.ANY)
    smem = pl.BlockSpec(memory_space=pltpu.SMEM)
    shapes = (
        jax.ShapeDtypeStruct((1024, B), BF),
        jax.ShapeDtypeStruct((1024, B), BF),
        jax.ShapeDtypeStruct((NC, NZ, 32, B), F32),
        jax.ShapeDtypeStruct((1, B), F32),
    )
    results = pl.pallas_call(
        kernel,
        out_shape=shapes,
        in_specs=[anywhere] * 7 + [smem] * 2,
        out_specs=(anywhere,) * 4,
        scratch_shapes=scratch,
        compiler_params=pltpu.CompilerParams(
            collective_id=0, has_side_effects=True, vmem_limit_bytes=56 * 2**20
        ),
    )(
        features,
        weight,
        bias.reshape(1, B),
        cotangent,
        tile_vals.reshape(10, 4, 4, B, B),
        send_blocks.transpose(0, 2, 1).reshape(CAP, 64),
        tile_row,
        tile_row,
        tile_src,
    )
    out, gin, gw, gb = pl.pallas_call(
        hand_over,
        out_shape=shapes,
        in_specs=[anywhere] * 4,
        out_specs=(anywhere,) * 4,
        scratch_shapes=[pltpu.VMEM(a.shape, a.dtype) for a in shapes] + [pltpu.SemaphoreType.DMA((8,))],
        compiler_params=pltpu.CompilerParams(vmem_limit_bytes=60 * 2**20),
    )(*results)
    return out, gin, gw.reshape(512, B), gb.reshape(B)


def solution(mesh):
    in_specs = (
        P("dom", "rep"),
        P(None, "rep"),
        P("rep"),
        P("dom", "rep"),
        P("dom", None, None, None),
        P("dom", None),
        P("dom", None),
        P("dom", None, None),
        P("dom", None),
    )
    out_specs = (P("dom", "rep"), P("dom", "rep"), P(None, "rep"), P("rep"))
    return jax.shard_map(shards, mesh=mesh, in_specs=in_specs, out_specs=out_specs, check_vma=False)
```

```python
import jax
import jax.numpy as jnp
from jax import lax
from jax.experimental import pallas as pl
from jax.experimental.pallas import tpu as pltpu
from jax.sharding import PartitionSpec as P

B = 128
NB = 8
CAP = 2
NX, NY, NZ, NC = 4, 4, 8, 2
MESH = pl.DeviceIdType.MESH
BF = jnp.bfloat16
F32 = jnp.float32

DIST = [0, 1, -1, 2, -2, 3, -3, 4]
SLOT = {d: e for e, d in enumerate(DIST)}
SLOT[-4] = SLOT[4]


def dot(a, b):
    return lax.dot_general(a, b, (((1,), (0,)), ((), ())), preferred_element_type=F32)


def dot_t(a, b):
    return lax.dot_general(a, b, (((1,), (1,)), ((), ())), preferred_element_type=F32)


class Semaphores:
    def __init__(self):
        self.n = 0

    def take(self, count):
        first = self.n
        self.n += count
        return first


S = Semaphores()
S_FEAT = S.take(4)
S_FREL = S.take(2)
S_SB = S.take(8)
S_ROW = S.take(4)
S_TY = S.take(16)
S_TQ = S.take(8)
S_HZ = S.take(16)
S_HC = S.take(16)
S_YR = S.take(2)
S_YI = S.take(4)
S_G = S.take(4)
S_GR = S.take(2)
S_SIB = S.take(8)
S_ZR = S.take(16)
S_XR = S.take(2)
S_XI = S.take(4)
S_SBC = S.take(1)
S_TR = S.take(1)
S_B0 = S.take(1)
S_B1 = S.take(8)
S_B2 = S.take(4)
S_A0 = S.take(1)
S_A1 = S.take(8)
S_A2 = S.take(4)
S_A3 = S.take(8)
S_A4 = S.take(1)
S_RECV = S.n
S_TF = S_RECV
S_SEND = 40
L_LOC, L_SB, L_ROW, L_FEAT, L_W, L_COT, L_BIAS, L_OUT, L_GIN, L_GW, L_GB, L_N = 0, 1, 2, 3, 4, 5, 6, 7, 9, 11, 12, 13


def kernel(
    feat, weight, bias, cot, tiles, sendb, trow, row_own, src_own,
    out, gin, gw, gb,
    F, Hown, Hcore, H1, H2, H3, H4, H5, H6, Hlast, Hlastcore, T, TL, trel, agg, ysend2, ysend1, ysend3, yrel, yin, G0, G1, G2, G3, D, S0, SL,
    zsend, zrecv, sibsend, sibrecv, GAT, GA, PT, xsend2, xsend1, xsend3, xrel, xin, bsum, bcore, bz, by, gws, arc, arown, arsend, arin, ar2in, gwall, gwf,
    wv, cv, bv, ov, giv, gbv, sbv, rowv, sbs, rows, ssem, rsem, lsem,
):
    H = [(Hown, Hcore), H1, H2, H3, H4, H5, H6, (Hlast, Hlastcore)]
    G = [G0, G1, G2, G3]

    def hid(e, oc):
        return H[e][oc] if isinstance(H[e], tuple) else H[e].at[oc]

    dom, x = lax.axis_index("dom"), lax.axis_index("rep")
    z = dom // (NY * NC)
    y = lax.rem(dom // NC, NY)
    c = lax.rem(dom, NC)

    def at(dx=0, dy=0, dz=0, oc=0):
        zz = lax.rem(z + dz + NZ, NZ)
        yy = lax.rem(y + dy + NY, NY)
        cc = lax.rem(c + oc, NC)
        return ((zz * NY + yy) * NC + cc, lax.rem(x + dx + NX, NX))

    started = []

    def copy(src, dst, sem, dev, recv=None):
        return pltpu.make_async_remote_copy(
            src_ref=src,
            dst_ref=dst,
            send_sem=ssem.at[len(started) % S_SEND],
            recv_sem=rsem.at[sem if recv is None else recv],
            device_id=dev,
            device_id_type=MESH,
        )

    def send(src, dst, sem, dev, recv=None):
        if len(started) >= S_SEND:
            started[len(started) - S_SEND].wait_send()
        made = copy(src, dst, sem, dev, recv)
        made.start()
        started.append(made)

    here = (dom, x)

    def arrived(dst, sem):
        pltpu.make_async_remote_copy(
            src_ref=dst, dst_ref=dst, send_sem=ssem.at[0], recv_sem=rsem.at[sem], device_id=here, device_id_type=MESH
        ).wait_recv()

    half = lambda ref, h: ref.at[pl.ds(4 * h, 4)]

    def local(src, dst, sem):
        made = pltpu.make_async_copy(src, dst, lsem.at[sem])
        made.start()
        return made

    feat_in = local(feat, F.at[0], L_FEAT)
    weight_in = local(weight, wv, L_W)
    loc_tiles = local(tiles.at[pl.ds(0, 2)], TL, L_LOC)
    own_tiles = [
        local(tiles.at[2 + lax.rem(z + DIST[e] + NZ, NZ), y], T.at[0, e], L_N + e) for e in range(NZ)
    ]
    cot_in = local(cot, cv, L_COT)
    bias_in = local(bias, bv, L_BIAS)

    barrier = pltpu.get_barrier_semaphore()
    peers = [at(dz=DIST[e]) for e in range(1, NZ)] + [at(oc=1)]
    peers += [at(dy=d) for d in range(1, NY)] + [at(dx=d) for d in range(1, NX)]
    for dev in peers:
        pl.semaphore_signal(barrier, inc=1, device_id=dev, device_id_type=MESH)
    pl.semaphore_wait(barrier, len(peers))

    rows_of = lambda h: pl.ds(512 * h, 512)
    feat_in.wait()
    for h, g in ((0, 1), (1, 0)):
        send(F.at[0, rows_of(h)], F.at[3, rows_of(h)], S_FEAT + h, at(dx=1))
        send(F.at[0, rows_of(g)], F.at[1, rows_of(g)], S_FEAT + 2 + g, at(dx=-1))

    for e in range(1, NZ):
        back = SLOT[-DIST[e]]
        send(sendb, sbv.at[0, back], S_SB + back, at(dz=DIST[e]))
    for d in range(1, NY):
        send(trow, rowv.at[NY - d], S_ROW + NY - d, at(dy=d))
    sb_in = local(sendb, sbv.at[0, 0], L_SB)
    row_in = local(trow, rowv.at[0], L_ROW)

    def tile_slot(e):
        d = jnp.where(lax.rem(e, 2) == 1, (e + 1) // 2, NZ - e // 2)
        return 2 + lax.rem(z + d, NZ)

    far = lax.rem(y + 2, NY)
    send(tiles.at[tile_slot(x), far], T.at[2, x], S_TF + 6, at(dy=2), S_TQ + x)
    send(tiles.at[tile_slot(x + 4), far], trel, S_TR, at(dy=-1))

    def near_tiles(slots):
        for e in slots:
            for dy, to, base in ((1, 3, 0), (-1, 1, 8)):
                send(
                    tiles.at[2 + lax.rem(z + DIST[e] + NZ, NZ), lax.rem(y + dy + NY, NY)],
                    T.at[to, e],
                    S_TY + base + e,
                    at(dy=dy),
                )

    near_tiles(range(2))

    for dy in range(NY):
        G[dy][NB] = jnp.zeros((B, B), BF)

    @pl.loop(0, NB)
    def _(i):
        for dy in range(NY):
            agg[dy, i] = jnp.zeros((B, B), F32)
        SL[i] = jnp.zeros((B, B), F32)

    arrived(F.at[3, rows_of(0)], S_FEAT + 0)
    send(F.at[3, rows_of(0)], F.at[2, rows_of(0)], S_FREL + 0, at(dx=1))
    arrived(F.at[1, rows_of(1)], S_FEAT + 3)
    send(F.at[1, rows_of(1)], F.at[2, rows_of(1)], S_FREL + 1, at(dx=-1))
    arrived(F.at[1, rows_of(0)], S_FEAT + 2)
    arrived(F.at[3, rows_of(1)], S_FEAT + 1)

    def w_rows(dx):
        return wv[pl.ds(pl.multiple_of(lax.rem(x + dx, NX) * B, B), B), :]

    def step_send(way, step, h):
        d = -step if way == 0 else step
        nd = d - 1 if way == 0 else d + 1
        send(
            half(hid(SLOT[d], 0), h), half(hid(SLOT[nd], 0), h), S_HZ + way * 8 + step * 2 + h,
            at(dz=1 if way == 0 else -1),
        )

    def core_send(e, h):
        send(half(hid(e, 0), h), half(hid(e, 1), h), S_HC + e * 2 + h, at(oc=1))

    weight_in.wait()

    @pl.loop(0, 4)
    def _(k):
        for i in range(2):
            r = pl.ds(pl.multiple_of((2 * k + i) * B, B), B)
            PT[r, :] = dot(F[0, r], w_rows(0)) + dot(F[1, r], w_rows(1)) + dot(F[3, r], w_rows(3))

    for h in range(2):
        arrived(F.at[2, rows_of(h)], S_FREL + h)
        for b in range(4 * h, 4 * h + 4):
            r = pl.ds(b * B, B)
            Hown[b] = (PT[r, :] + dot(F[2, r], w_rows(2))).astype(BF)

        step_send(0, 0, h)
        step_send(1, 0, h)
        core_send(0, h)

    arrived(trel, S_TR)
    send(trel, T.at[2, x + 4], S_TQ, at(dy=-1), S_TQ + x + 4)
    near_tiles(range(2, NZ))

    def far_tiles(k):
        e = x + 4 * k
        arrived(T.at[2, e], S_TQ + e)
        for i, dx in enumerate((1, -1, 2)):
            send(T.at[2, e], T.at[2, e], S_TF + k * 3 + i, at(dx=dx), S_TQ + e)

    far_tiles(0)

    sb_in.wait()
    row_in.wait()
    for e in range(1, NZ):
        arrived(sbv.at[0, e], S_SB + e)
    send(sbv.at[0], sbv.at[1], S_SBC, at(oc=1))
    for d in range(1, NY):
        arrived(rowv.at[d], S_ROW + d)

    arrived(sbv.at[1], S_SBC)
    to_s = [local(sbv, sbs, L_SB), local(rowv, rows, L_ROW)]

    loc_tiles.wait()

    @pl.loop(0, 8)
    def _(i):
        k = i * 4
        prods = [dot(TL[i // 4, lax.rem(i, 4), j], Hown[src_own[0, k + j]]) for j in range(4)]
        tr = [row_own[0, k + j] for j in range(4)]
        for t in range(NB):
            add = jnp.where(tr[0] == t, prods[0], 0.0)
            for j in range(1, 4):
                add += jnp.where(tr[j] == t, prods[j], 0.0)
            agg[0, t] += add

    far_tiles(1)
    for made in to_s:
        made.wait()

    for made in own_tiles:
        made.wait()

    def slot_row(dy, e, cc, cap):
        zz = lax.rem(z + DIST[e] + NZ, NZ)
        return rows[dy, 0, 32 + zz * 16 + y * 4 + cc * 2 + cap]

    def slot_block(dy, e, oc, cap):
        target = (z * NY + lax.rem(y + dy, NY)) * NC + c
        return sbs[oc, e, cap, target]

    def core_arrived(e):
        for h in range(2):
            arrived(half(hid(e, 1), h), S_HC + e * 2 + h)

    def forward(e):
        for dy, base in ((3, 0), (1, 8)):
            arrived(T.at[dy, e], S_TY + base + e)

        @pl.when(x != e % 4)
        def _():
            arrived(T.at[2, e], S_TQ + e)

        def add(oc, dys=range(NY)):
            cc = lax.rem(c + oc, NC)
            for dy in dys:
                prods, tr = [], []
                for cap in range(CAP):
                    t, b = T[dy, e, cc * 2 + cap], slot_block(dy, e, oc, cap)
                    prods.append(dot(t, H[e][oc][b] if isinstance(H[e], tuple) else H[e][oc, b]))
                    tr.append(slot_row(dy, e, cc, cap))
                for t in range(NB):
                    agg[dy, t] += jnp.where(tr[0] == t, prods[0], 0.0) + jnp.where(tr[1] == t, prods[1], 0.0)

        if e == SLOT[4]:
            return add
        core_arrived(e)
        if e:
            pl.loop(0, NC)(add)
        else:
            for oc in range(NC):
                add(oc)

    pending = [0]
    for step in range(4):
        halves = ((0, 0), (1, 0), (0, 1), (1, 1)) if step < 3 else ((0, 0), (1, 1))
        if step == 3:
            for e in pending:
                forward(e)
            pending = []
        for way, h in halves:
            d = -(step + 1) if way == 0 else step + 1
            arrived(half(hid(SLOT[d], 0), h), S_HZ + way * 8 + step * 2 + h)
            if step < 2 or (step == 2 and h == way):
                step_send(way, step + 1, h)
            core_send(SLOT[d], h)
        for e in pending:
            forward(e)
        pending = [SLOT[step + 1], SLOT[-step - 1]] if step < 3 else [SLOT[4]]
    last = forward(SLOT[4])

    def to_bf16(dst, src, base, more=None):
        @pl.loop(0, 4, unroll=True)
        def _(i):
            value = src[base + i]
            if more is not None:
                value += more[i].astype(F32)
            dst[base + i] = value.astype(BF)

    last(0, (2,))
    core_arrived(SLOT[4])
    last(1, (2,))
    to_bf16(ysend2, agg.at[2], 0)
    send(half(ysend2, 0), yrel.at[0], S_YR + 0, at(dy=1))
    to_bf16(ysend2, agg.at[2], 4)
    send(half(ysend2, 1), yrel.at[1], S_YR + 1, at(dy=-1))
    for oc in range(NC):
        last(oc, (1, 3))
    to_bf16(ysend1, agg.at[1], 4)
    send(half(ysend1, 1), half(yin.at[0], 1), S_YI + 1, at(dy=1))
    to_bf16(ysend3, agg.at[3], 0)
    send(half(ysend3, 0), half(yin.at[1], 0), S_YI + 2, at(dy=-1))
    arrived(yrel.at[0], S_YR + 0)
    to_bf16(ysend1, agg.at[1], 0, yrel.at[0])
    send(half(ysend1, 0), half(yin.at[0], 0), S_YI + 0, at(dy=1))
    arrived(yrel.at[1], S_YR + 1)
    to_bf16(ysend3, agg.at[3], 4, yrel.at[1])
    send(half(ysend3, 1), half(yin.at[1], 1), S_YI + 3, at(dy=-1))
    for oc in range(NC):
        last(oc, (0,))

    bsum[...] = jnp.zeros_like(bsum)
    cot_in.wait()
    bias_in.wait()
    leaving = []
    for h in range(2):
        arrived(half(yin.at[0], h), S_YI + h)
        arrived(half(yin.at[1], h), S_YI + 2 + h)

        @pl.loop(0, 4, unroll=True)
        def _(b, h=h):
            i = 4 * h + b
            r = pl.ds(pl.multiple_of(i * B, B), B)
            pre = agg[0, i] + yin[0, i].astype(F32) + yin[1, i].astype(F32) + bv[...].astype(F32)
            sig = jax.nn.sigmoid(pre)
            ov[r, :] = (pre * sig).astype(BF)
            g = (cv[r, :].astype(F32) * sig * (1.0 + pre * (1.0 - sig))).astype(BF).astype(F32)
            part = g[0:8]
            for j in range(1, 16):
                part += g[8 * j : 8 * j + 8]
            bsum[...] += part
            G[0][i] = g.T.astype(BF)

        send(half(G[0], h), half(G[3], h), S_G + h, at(dy=1))
        send(half(G[0], h), half(G[1], h), S_G + 2 + h, at(dy=-1))
        leaving.append(local(ov.at[rows_of(h)], out.at[rows_of(h)], L_OUT + h))

    def spread(n, base, dst, tail):
        @pl.loop(0, 8)
        def _(j):
            r = pl.ds(pl.multiple_of(j * 16, 16), 16)
            parts = [D[k, r, :] for k in range(n)]
            for t in range(NB):
                acc = jnp.where(base[0] == t, parts[0], 0.0)
                for k in range(1, n):
                    acc += jnp.where(base[k] == t, parts[k], 0.0)
                tail(dst, t, r, acc)

    def add_f32(dst, t, r, acc):
        dst[t, r, :] += acc

    def put_f32(dst, t, r, acc):
        dst[t, r, :] = acc

    def put_bf16(dst, t, r, acc):
        dst[t, r, :] = acc.astype(BF)

    send(bsum, bcore, S_B0, at(oc=1))

    @pl.loop(0, 4)
    def _(i):
        k0 = i * 8
        for j in range(8):
            D[j] = dot(G[0][row_own[0, k0 + j]], TL[i // 2, lax.rem(i, 2) * 2 + j // 4, j % 4])
        spread(8, [src_own[0, k0 + j] for j in range(8)], SL, add_f32)

    arrived(bcore, S_B0)
    bz[z] = bsum[...] + bcore[...]
    for e in range(1, NZ):
        send(bz.at[z], bz.at[z], S_B1 + SLOT[-DIST[e]], at(dz=DIST[e]))

    arrived(half(G[3], 0), S_G + 0)
    send(half(G[3], 0), half(G[2], 0), S_GR + 0, at(dy=1))
    arrived(half(G[1], 1), S_G + 3)
    send(half(G[1], 1), half(G[2], 1), S_GR + 1, at(dy=-1))
    arrived(half(G[1], 0), S_G + 2)
    arrived(half(G[3], 1), S_G + 1)
    for h in range(2):
        arrived(half(G[2], h), S_GR + h)

    def backward(e, oc, dst, tail):
        cc = lax.rem(c + oc, NC)
        blocks = []
        for dy in range(NY):
            for cap in range(CAP):
                D[dy * 2 + cap] = dot(G[dy][slot_row(dy, e, cc, cap)], T[dy, e, cc * 2 + cap])
                blocks.append(slot_block(dy, e, oc, cap))
        spread(8, blocks, dst, tail)

    def combine(dst, e, h, way=None, step=None):
        @pl.loop(0, 4, unroll=True)
        def _(i):
            t = 4 * h + i
            value = S0[e, t] + sibrecv[e, t].astype(F32)
            if step is not None:
                value += zrecv[way, step, t].astype(F32)
            dst[t] = value.astype(BF)

    def ring_send(way, step, h):
        send(
            half(zsend.at[way, step], h), half(zrecv.at[way, step], h), S_ZR + way * 8 + step * 2 + h,
            at(dz=1 if way == 0 else -1),
        )

    def terms(e):
        backward(e, 1, sibsend.at[e], put_bf16)
        send(sibsend.at[e], sibrecv.at[e], S_SIB + e, at(oc=1))
        backward(e, 0, S0.at[e], put_f32)

    def bias_step(step):
        if step == 2:
            for e in range(1, NZ):
                arrived(bz.at[lax.rem(z + DIST[e] + NZ, NZ)], S_B1 + e)
            total = bz[0]
            for k in range(1, NZ):
                total += bz[k]
            by[y] = total
            for d in range(1, NY):
                send(by.at[y], by.at[y], S_B2 + NY - d, at(dy=d))
        elif step == 3:
            for d in range(1, NY):
                arrived(by.at[lax.rem(y + d, NY)], S_B2 + d)
            gbv[...] = jnp.sum(by[0] + by[1] + by[2] + by[3], 0, keepdims=True)
            leaving.append(local(gbv, gb, L_GB))

    terms(SLOT[4])
    arrived(sibrecv.at[SLOT[4]], S_SIB + SLOT[4])
    for way in range(2):
        combine(zsend.at[way, 0], SLOT[4], way)
        ring_send(way, 0, way)
    for step in range(1, 4):
        d = 4 - step
        ends = (SLOT[d], SLOT[-d])
        for e in ends:
            terms(e)
        for e in ends:
            arrived(sibrecv.at[e], S_SIB + e)
        order = ((1, 0), (0, 1), (0, 0), (1, 1)) if step == 1 else ((0, 0), (1, 0), (0, 1), (1, 1))
        for way, h in order:
            came = step > 1 or h == way
            if came:
                arrived(half(zrecv.at[way, step - 1], h), S_ZR + way * 8 + (step - 1) * 2 + h)
            combine(zsend.at[way, step], ends[way], h, way, step - 1 if came else None)
            ring_send(way, step, h)
        bias_step(step)
    terms(0)
    arrived(sibrecv.at[0], S_SIB + 0)

    def terms_x(dx, h, dst, more=None):
        @pl.loop(0, 4, unroll=True)
        def _(b):
            r = pl.ds(pl.multiple_of(512 * h + b * B, B), B)
            value = dot_t(GA[r, :], w_rows(dx))
            if more is not None:
                value += more[pl.ds(pl.multiple_of(b * B, B), B), :].astype(F32)
            dst[r, :] = value.astype(dst.dtype)

    for h in range(2):
        for way in range(2):
            arrived(half(zrecv.at[way, 3], h), S_ZR + way * 8 + 6 + h)

        @pl.loop(0, 4, unroll=True)
        def _(i, h=h):
            t = 4 * h + i
            value = S0[0, t] + sibrecv[0, t].astype(F32) + SL[t]
            value += zrecv[0, 3, t].astype(F32) + zrecv[1, 3, t].astype(F32)
            value = value.astype(BF).astype(F32)
            GAT[:, pl.ds(pl.multiple_of(t * B, B), B)] = value.astype(BF)
            GA[pl.ds(pl.multiple_of(t * B, B), B), :] = value.T.astype(BF)

        if h == 0:
            terms_x(2, 0, xsend2)
            send(xsend2.at[rows_of(0)], xrel.at[0], S_XR + 0, at(dx=1))
            terms_x(3, 0, xsend3)
            send(xsend3.at[rows_of(0)], xin.at[1, rows_of(0)], S_XI + 2, at(dx=-1))

    def weight_terms(core):
        for i in range(2):
            dx = lax.rem(core * 2 + i - x + NX, NX)
            gws[core, B * i : B * i + B, :] = dot(GAT[...], F[dx]).T

    weight_terms(1 - c)
    send(gws.at[1 - c], arc, S_A0, at(oc=1))
    weight_terms(c)
    terms_x(2, 1, xsend2)
    send(xsend2.at[rows_of(1)], xrel.at[1], S_XR + 1, at(dx=-1))

    arrived(arc, S_A0)
    for k in range(NZ):
        value = gws[c, 32 * k : 32 * k + 32, :] + arc[32 * k : 32 * k + 32, :]
        arown[k] = value
        arsend[k] = value.astype(BF)
    for e in range(NZ - 1, 0, -1):
        send(arsend.at[lax.rem(z + DIST[e] + NZ, NZ)], arin.at[z], S_A1 + SLOT[-DIST[e]], at(dz=DIST[e]))
    terms_x(1, 1, xsend1)
    send(xsend1.at[rows_of(1)], xin.at[0, rows_of(1)], S_XI + 1, at(dx=1))

    arrived(xrel.at[0], S_XR + 0)
    terms_x(1, 0, xsend1, xrel.at[0])
    send(xsend1.at[rows_of(0)], xin.at[0, rows_of(0)], S_XI + 0, at(dx=1))
    terms_x(0, 0, PT)
    arrived(xrel.at[1], S_XR + 1)
    terms_x(3, 1, xsend3, xrel.at[1])
    send(xsend3.at[rows_of(1)], xin.at[1, rows_of(1)], S_XI + 3, at(dx=-1))

    total = arown[z]
    for e in range(1, NZ):
        k = lax.rem(z + DIST[e] + NZ, NZ)
        arrived(arin.at[k], S_A1 + e)
        total += arin[k].astype(F32)
    ar2in[y] = total
    for d in range(1, NY):
        send(ar2in.at[y], ar2in.at[y], S_A2 + NY - d, at(dy=d))
    terms_x(0, 1, PT)
    for d in range(1, NY):
        arrived(ar2in.at[lax.rem(y + d, NY)], S_A2 + d)
    gwall[c, z] = (ar2in[0] + ar2in[1] + ar2in[2] + ar2in[3]).astype(BF)
    for e in range(NZ - 1, 0, -1):
        send(gwall.at[c, z], gwall.at[c, z], S_A3 + SLOT[-DIST[e]], at(dz=DIST[e]))

    def input_gradient(h):
        arrived(xin.at[0, rows_of(h)], S_XI + h)
        arrived(xin.at[1, rows_of(h)], S_XI + 2 + h)

        @pl.loop(0, 4, unroll=True)
        def _(b):
            r = pl.ds(pl.multiple_of(512 * h + b * B, B), B)
            giv[r, :] = (PT[r, :] + xin[0, r, :].astype(F32) + xin[1, r, :].astype(F32)).astype(BF)

        leaving.append(local(giv.at[rows_of(h)], gin.at[rows_of(h)], L_GIN + h))

    input_gradient(0)
    input_gradient(1)
    for e in range(1, NZ):
        arrived(gwall.at[c, lax.rem(z + DIST[e] + NZ, NZ)], S_A3 + e)
    send(gwall.at[c], gwall.at[c], S_A4, at(oc=1))
    arrived(gwall.at[1 - c], S_A4)
    for k in range(NC):
        gwf[k] = gwall[k].astype(F32)
    leaving.append(local(gwf, gw, L_GW))
    for made in leaving:
        made.wait()
    for made in started[-S_SEND:]:
        made.wait_send()


def hand_over(*refs):
    given, result, held, sem = refs[0:4], refs[4:8], refs[8:12], refs[12]
    reads = [pltpu.make_async_copy(given[k], held[k], sem.at[k]) for k in range(4)]
    writes = [pltpu.make_async_copy(held[k], result[k], sem.at[4 + k]) for k in range(4)]
    for made in reads:
        made.start()
    for k in range(4):
        reads[k].wait()
        writes[k].start()
    for made in writes:
        made.wait()


def shards(
    features, weight, bias, cotangent, tile_vals, tile_row, tile_src, send_blocks, send_count
):
    blocks = lambda *lead, dtype=BF: pltpu.VMEM((*lead, B, B), dtype)
    scratch = [
        pltpu.VMEM((NX, 1024, B), BF),
        blocks(NB),
        blocks(NB),
        *[blocks(NC, NB) for _ in range(NZ - 2)],
        blocks(NB),
        blocks(NB),
        blocks(NY, NZ, 4),
        blocks(2, 4, 4),
        blocks(4),
        blocks(NY, NB, dtype=F32),
        blocks(NB),
        blocks(NB),
        blocks(NB),
        blocks(2, 4),
        blocks(2, NB),
        *[blocks(NB + 1) for _ in range(NY)],
        blocks(8, dtype=F32),
        blocks(NZ, NB, dtype=F32),
        blocks(NB, dtype=F32),
        blocks(2, 4, NB),
        blocks(2, 4, NB),
        blocks(NZ, NB),
        blocks(NZ, NB),
        pltpu.VMEM((B, 1024), BF),
        pltpu.VMEM((1024, B), BF),
        pltpu.VMEM((1024, B), F32),
        pltpu.VMEM((1024, B), BF),
        pltpu.VMEM((1024, B), BF),
        pltpu.VMEM((1024, B), BF),
        pltpu.VMEM((2, 512, B), BF),
        pltpu.VMEM((2, 1024, B), BF),
        pltpu.VMEM((8, B), F32),
        pltpu.VMEM((8, B), F32),
        pltpu.VMEM((NZ, 8, B), F32),
        pltpu.VMEM((NY, 8, B), F32),
        pltpu.VMEM((NC, 256, B), F32),
        pltpu.VMEM((256, B), F32),
        pltpu.VMEM((NZ, 32, B), F32),
        pltpu.VMEM((NZ, 32, B), BF),
        pltpu.VMEM((NZ, 32, B), BF),
        pltpu.VMEM((NY, 32, B), F32),
        pltpu.VMEM((NC, NZ, 32, B), BF),
        pltpu.VMEM((NC, NZ, 32, B), F32),
        pltpu.VMEM((512, B), BF),
        pltpu.VMEM((1024, B), BF),
        pltpu.VMEM((1, B), BF),
        pltpu.VMEM((1024, B), BF),
        pltpu.VMEM((1024, B), BF),
        pltpu.VMEM((1, B), F32),
        pltpu.VMEM((NC, NZ, CAP, 64), jnp.int32),
        pltpu.VMEM((NY, 1, 160), jnp.int32),
        pltpu.SMEM((NC, NZ, CAP, 64), jnp.int32),
        pltpu.SMEM((NY, 1, 160), jnp.int32),
        pltpu.SemaphoreType.DMA((S_SEND,)),
        pltpu.SemaphoreType.DMA((S_RECV,)),
        pltpu.SemaphoreType.DMA((L_N + NZ,)),
    ]
    anywhere = pl.BlockSpec(memory_space=pl.ANY)
    smem = pl.BlockSpec(memory_space=pltpu.SMEM)
    shapes = (
        jax.ShapeDtypeStruct((1024, B), BF),
        jax.ShapeDtypeStruct((1024, B), BF),
        jax.ShapeDtypeStruct((NC, NZ, 32, B), F32),
        jax.ShapeDtypeStruct((1, B), F32),
    )
    results = pl.pallas_call(
        kernel,
        out_shape=shapes,
        in_specs=[anywhere] * 7 + [smem] * 2,
        out_specs=(anywhere,) * 4,
        scratch_shapes=scratch,
        compiler_params=pltpu.CompilerParams(
            collective_id=0, has_side_effects=True, vmem_limit_bytes=56 * 2**20
        ),
    )(
        features,
        weight,
        bias.reshape(1, B),
        cotangent,
        tile_vals.reshape(10, 4, 4, B, B),
        send_blocks.transpose(0, 2, 1).reshape(CAP, 64),
        tile_row,
        tile_row,
        tile_src,
    )
    out, gin, gw, gb = pl.pallas_call(
        hand_over,
        out_shape=shapes,
        in_specs=[anywhere] * 4,
        out_specs=(anywhere,) * 4,
        scratch_shapes=[pltpu.VMEM(a.shape, a.dtype) for a in shapes] + [pltpu.SemaphoreType.DMA((8,))],
        compiler_params=pltpu.CompilerParams(vmem_limit_bytes=60 * 2**20),
    )(*results)
    return out, gin, gw.reshape(512, B), gb.reshape(B)


def solution(mesh):
    in_specs = (
        P("dom", "rep"),
        P(None, "rep"),
        P("rep"),
        P("dom", "rep"),
        P("dom", None, None, None),
        P("dom", None),
        P("dom", None),
        P("dom", None, None),
        P("dom", None),
    )
    out_specs = (P("dom", "rep"), P("dom", "rep"), P(None, "rep"), P("rep"))
    return jax.shard_map(shards, mesh=mesh, in_specs=in_specs, out_specs=out_specs, check_vma=False)
```

```python
import jax
import jax.numpy as jnp
from jax import lax
from jax.experimental import pallas as pl
from jax.experimental.pallas import tpu as pltpu
from jax.sharding import PartitionSpec as P

B = 128
NB = 8
CAP = 2
NX, NY, NZ, NC = 4, 4, 8, 2
MESH = pl.DeviceIdType.MESH
BF = jnp.bfloat16
F32 = jnp.float32

DIST = [0, 1, -1, 2, -2, 3, -3, 4]
SLOT = {d: e for e, d in enumerate(DIST)}
SLOT[-4] = SLOT[4]


def dot(a, b):
    return lax.dot_general(a, b, (((1,), (0,)), ((), ())), preferred_element_type=F32)


def dot_t(a, b):
    return lax.dot_general(a, b, (((1,), (1,)), ((), ())), preferred_element_type=F32)


class Semaphores:
    def __init__(self):
        self.n = 0

    def take(self, count):
        first = self.n
        self.n += count
        return first


S = Semaphores()
S_FEAT = S.take(4)
S_FREL = S.take(2)
S_SB = S.take(8)
S_ROW = S.take(4)
S_TY = S.take(16)
S_TQ = S.take(8)
S_HZ = S.take(16)
S_HC = S.take(16)
S_YR = S.take(2)
S_YI = S.take(4)
S_G = S.take(4)
S_GR = S.take(2)
S_SIB = S.take(8)
S_ZR = S.take(16)
S_XR = S.take(2)
S_XI = S.take(4)
S_SBC = S.take(1)
S_TR = S.take(1)
S_B0 = S.take(1)
S_B1 = S.take(8)
S_B2 = S.take(4)
S_A0 = S.take(1)
S_A1 = S.take(8)
S_A2 = S.take(4)
S_A3 = S.take(8)
S_A4 = S.take(1)
S_RECV = S.n
S_TF = S_RECV
S_SEND = 40
L_LOC, L_SB, L_ROW, L_FEAT, L_W, L_COT, L_BIAS, L_OUT, L_GIN, L_GW, L_GB, L_N = 0, 1, 2, 3, 4, 5, 6, 7, 9, 11, 12, 13


def kernel(
    feat, weight, bias, cot, tiles, sendb, trow, row_own, src_own,
    out, gin, gw, gb,
    F, Hown, Hcore, H1, H2, H3, H4, H5, H6, Hlast, Hlastcore, T, TL, trel, agg, ysend2, ysend1, ysend3, yrel, yin, G0, G1, G2, G3, D, S0, SL,
    zsend, zrecv, sibsend, sibrecv, GAT, GA, PT, xsend2, xsend1, xsend3, xrel, xin, bsum, bcore, bz, by, gws, arc, arown, arsend, arin, ar2in, gwall, gwf,
    wv, cv, bv, ov, giv, gbv, sbv, rowv, sbs, rows, ssem, rsem, lsem,
):
    H = [(Hown, Hcore), H1, H2, H3, H4, H5, H6, (Hlast, Hlastcore)]
    G = [G0, G1, G2, G3]

    def hid(e, oc):
        return H[e][oc] if isinstance(H[e], tuple) else H[e].at[oc]

    dom, x = lax.axis_index("dom"), lax.axis_index("rep")
    z = dom // (NY * NC)
    y = lax.rem(dom // NC, NY)
    c = lax.rem(dom, NC)

    def at(dx=0, dy=0, dz=0, oc=0):
        zz = lax.rem(z + dz + NZ, NZ)
        yy = lax.rem(y + dy + NY, NY)
        cc = lax.rem(c + oc, NC)
        return ((zz * NY + yy) * NC + cc, lax.rem(x + dx + NX, NX))

    started = []

    def copy(src, dst, sem, dev, recv=None):
        return pltpu.make_async_remote_copy(
            src_ref=src,
            dst_ref=dst,
            send_sem=ssem.at[len(started) % S_SEND],
            recv_sem=rsem.at[sem if recv is None else recv],
            device_id=dev,
            device_id_type=MESH,
        )

    def send(src, dst, sem, dev, recv=None):
        if len(started) >= S_SEND:
            started[len(started) - S_SEND].wait_send()
        made = copy(src, dst, sem, dev, recv)
        made.start()
        started.append(made)

    here = (dom, x)

    def arrived(dst, sem):
        pltpu.make_async_remote_copy(
            src_ref=dst, dst_ref=dst, send_sem=ssem.at[0], recv_sem=rsem.at[sem], device_id=here, device_id_type=MESH
        ).wait_recv()

    half = lambda ref, h: ref.at[pl.ds(4 * h, 4)]

    def local(src, dst, sem):
        made = pltpu.make_async_copy(src, dst, lsem.at[sem])
        made.start()
        return made

    feat_in = local(feat, F.at[0], L_FEAT)
    weight_in = local(weight, wv, L_W)
    loc_tiles = local(tiles.at[pl.ds(0, 2)], TL, L_LOC)
    own_tiles = [
        local(tiles.at[2 + lax.rem(z + DIST[e] + NZ, NZ), y], T.at[0, e], L_N + e) for e in range(NZ)
    ]
    cot_in = local(cot, cv, L_COT)
    bias_in = local(bias, bv, L_BIAS)

    barrier = pltpu.get_barrier_semaphore()
    peers = [at(dz=DIST[e]) for e in range(1, NZ)] + [at(oc=1)]
    peers += [at(dy=d) for d in range(1, NY)] + [at(dx=d) for d in range(1, NX)]
    for dev in peers:
        pl.semaphore_signal(barrier, inc=1, device_id=dev, device_id_type=MESH)
    pl.semaphore_wait(barrier, len(peers))

    rows_of = lambda h: pl.ds(512 * h, 512)
    feat_in.wait()
    for h, g in ((0, 1), (1, 0)):
        send(F.at[0, rows_of(h)], F.at[3, rows_of(h)], S_FEAT + h, at(dx=1))
        send(F.at[0, rows_of(g)], F.at[1, rows_of(g)], S_FEAT + 2 + g, at(dx=-1))

    for e in range(1, NZ):
        back = SLOT[-DIST[e]]
        send(sendb, sbv.at[0, back], S_SB + back, at(dz=DIST[e]))
    for d in range(1, NY):
        send(trow, rowv.at[NY - d], S_ROW + NY - d, at(dy=d))
    sb_in = local(sendb, sbv.at[0, 0], L_SB)
    row_in = local(trow, rowv.at[0], L_ROW)

    def tile_slot(e):
        d = jnp.where(lax.rem(e, 2) == 1, (e + 1) // 2, NZ - e // 2)
        return 2 + lax.rem(z + d, NZ)

    far = lax.rem(y + 2, NY)
    send(tiles.at[tile_slot(x), far], T.at[2, x], S_TF + 6, at(dy=2), S_TQ + x)
    send(tiles.at[tile_slot(x + 4), far], trel, S_TR, at(dy=-1))

    def near_tiles(slots):
        for e in slots:
            for dy, to, base in ((1, 3, 0), (-1, 1, 8)):
                send(
                    tiles.at[2 + lax.rem(z + DIST[e] + NZ, NZ), lax.rem(y + dy + NY, NY)],
                    T.at[to, e],
                    S_TY + base + e,
                    at(dy=dy),
                )

    near_tiles(range(2))

    for dy in range(NY):
        G[dy][NB] = jnp.zeros((B, B), BF)

    @pl.loop(0, NB)
    def _(i):
        for dy in range(NY):
            agg[dy, i] = jnp.zeros((B, B), F32)
        SL[i] = jnp.zeros((B, B), F32)

    arrived(F.at[3, rows_of(0)], S_FEAT + 0)
    send(F.at[3, rows_of(0)], F.at[2, rows_of(0)], S_FREL + 0, at(dx=1))
    arrived(F.at[1, rows_of(1)], S_FEAT + 3)
    send(F.at[1, rows_of(1)], F.at[2, rows_of(1)], S_FREL + 1, at(dx=-1))
    arrived(F.at[1, rows_of(0)], S_FEAT + 2)
    arrived(F.at[3, rows_of(1)], S_FEAT + 1)

    def w_rows(dx):
        return wv[pl.ds(pl.multiple_of(lax.rem(x + dx, NX) * B, B), B), :]

    def step_send(way, step, h):
        d = -step if way == 0 else step
        nd = d - 1 if way == 0 else d + 1
        send(
            half(hid(SLOT[d], 0), h), half(hid(SLOT[nd], 0), h), S_HZ + way * 8 + step * 2 + h,
            at(dz=1 if way == 0 else -1),
        )

    def core_send(e, h):
        send(half(hid(e, 0), h), half(hid(e, 1), h), S_HC + e * 2 + h, at(oc=1))

    weight_in.wait()

    @pl.loop(0, 4)
    def _(k):
        for i in range(2):
            r = pl.ds(pl.multiple_of((2 * k + i) * B, B), B)
            PT[r, :] = dot(F[0, r], w_rows(0)) + dot(F[1, r], w_rows(1)) + dot(F[3, r], w_rows(3))

    for h in range(2):
        arrived(F.at[2, rows_of(h)], S_FREL + h)
        for b in range(4 * h, 4 * h + 4):
            r = pl.ds(b * B, B)
            Hown[b] = (PT[r, :] + dot(F[2, r], w_rows(2))).astype(BF)

        step_send(0, 0, h)
        step_send(1, 0, h)
        core_send(0, h)

    arrived(trel, S_TR)
    send(trel, T.at[2, x + 4], S_TQ, at(dy=-1), S_TQ + x + 4)
    near_tiles(range(2, NZ))

    def far_tiles(k):
        e = x + 4 * k
        arrived(T.at[2, e], S_TQ + e)
        for i, dx in enumerate((1, -1, 2)):
            send(T.at[2, e], T.at[2, e], S_TF + k * 3 + i, at(dx=dx), S_TQ + e)

    far_tiles(0)

    sb_in.wait()
    row_in.wait()
    for e in range(1, NZ):
        arrived(sbv.at[0, e], S_SB + e)
    send(sbv.at[0], sbv.at[1], S_SBC, at(oc=1))
    for d in range(1, NY):
        arrived(rowv.at[d], S_ROW + d)

    arrived(sbv.at[1], S_SBC)
    to_s = [local(sbv, sbs, L_SB), local(rowv, rows, L_ROW)]

    loc_tiles.wait()

    @pl.loop(0, 8)
    def _(i):
        k = i * 4
        prods = [dot(TL[i // 4, lax.rem(i, 4), j], Hown[src_own[0, k + j]]) for j in range(4)]
        tr = [row_own[0, k + j] for j in range(4)]
        for t in range(NB):
            add = jnp.where(tr[0] == t, prods[0], 0.0)
            for j in range(1, 4):
                add += jnp.where(tr[j] == t, prods[j], 0.0)
            agg[0, t] += add

    far_tiles(1)
    for made in to_s:
        made.wait()

    for made in own_tiles:
        made.wait()

    def slot_row(dy, e, cc, cap):
        zz = lax.rem(z + DIST[e] + NZ, NZ)
        return rows[dy, 0, 32 + zz * 16 + y * 4 + cc * 2 + cap]

    def slot_block(dy, e, oc, cap):
        target = (z * NY + lax.rem(y + dy, NY)) * NC + c
        return sbs[oc, e, cap, target]

    def core_arrived(e):
        for h in range(2):
            arrived(half(hid(e, 1), h), S_HC + e * 2 + h)

    def forward(e):
        for dy, base in ((3, 0), (1, 8)):
            arrived(T.at[dy, e], S_TY + base + e)

        @pl.when(x != e % 4)
        def _():
            arrived(T.at[2, e], S_TQ + e)

        def add(oc, dys=range(NY)):
            cc = lax.rem(c + oc, NC)
            for dy in dys:
                prods, tr = [], []
                for cap in range(CAP):
                    t, b = T[dy, e, cc * 2 + cap], slot_block(dy, e, oc, cap)
                    prods.append(dot(t, H[e][oc][b] if isinstance(H[e], tuple) else H[e][oc, b]))
                    tr.append(slot_row(dy, e, cc, cap))
                for t in range(NB):
                    agg[dy, t] += jnp.where(tr[0] == t, prods[0], 0.0) + jnp.where(tr[1] == t, prods[1], 0.0)

        if e == SLOT[4]:
            return add
        core_arrived(e)
        if e:
            pl.loop(0, NC)(add)
        else:
            for oc in range(NC):
                add(oc)

    pending = [0]
    for step in range(4):
        halves = ((0, 0), (1, 0), (0, 1), (1, 1)) if step < 3 else ((0, 0), (1, 1))
        if step == 3:
            for e in pending:
                forward(e)
            pending = []
        for way, h in halves:
            d = -(step + 1) if way == 0 else step + 1
            arrived(half(hid(SLOT[d], 0), h), S_HZ + way * 8 + step * 2 + h)
            if step < 2 or (step == 2 and h == way):
                step_send(way, step + 1, h)
            core_send(SLOT[d], h)
        for e in pending:
            forward(e)
        pending = [SLOT[step + 1], SLOT[-step - 1]] if step < 3 else [SLOT[4]]
    last = forward(SLOT[4])

    def to_bf16(dst, src, base, more=None):
        @pl.loop(0, 4, unroll=True)
        def _(i):
            value = src[base + i]
            if more is not None:
                value += more[i].astype(F32)
            dst[base + i] = value.astype(BF)

    last(0, (2,))
    core_arrived(SLOT[4])
    last(1, (2,))
    to_bf16(ysend2, agg.at[2], 0)
    send(half(ysend2, 0), yrel.at[0], S_YR + 0, at(dy=1))
    to_bf16(ysend2, agg.at[2], 4)
    send(half(ysend2, 1), yrel.at[1], S_YR + 1, at(dy=-1))
    for oc in range(NC):
        last(oc, (1, 3))
    to_bf16(ysend1, agg.at[1], 4)
    send(half(ysend1, 1), half(yin.at[0], 1), S_YI + 1, at(dy=1))
    to_bf16(ysend3, agg.at[3], 0)
    send(half(ysend3, 0), half(yin.at[1], 0), S_YI + 2, at(dy=-1))
    arrived(yrel.at[0], S_YR + 0)
    to_bf16(ysend1, agg.at[1], 0, yrel.at[0])
    send(half(ysend1, 0), half(yin.at[0], 0), S_YI + 0, at(dy=1))
    arrived(yrel.at[1], S_YR + 1)
    to_bf16(ysend3, agg.at[3], 4, yrel.at[1])
    send(half(ysend3, 1), half(yin.at[1], 1), S_YI + 3, at(dy=-1))
    for oc in range(NC):
        last(oc, (0,))

    bsum[...] = jnp.zeros_like(bsum)
    cot_in.wait()
    bias_in.wait()
    leaving = []
    for h in range(2):
        arrived(half(yin.at[0], h), S_YI + h)
        arrived(half(yin.at[1], h), S_YI + 2 + h)

        @pl.loop(0, 4, unroll=True)
        def _(b, h=h):
            i = 4 * h + b
            r = pl.ds(pl.multiple_of(i * B, B), B)
            pre = agg[0, i] + yin[0, i].astype(F32) + yin[1, i].astype(F32) + bv[...].astype(F32)
            sig = jax.nn.sigmoid(pre)
            ov[r, :] = (pre * sig).astype(BF)
            g = (cv[r, :].astype(F32) * sig * (1.0 + pre * (1.0 - sig))).astype(BF).astype(F32)
            part = g[0:8]
            for j in range(1, 16):
                part += g[8 * j : 8 * j + 8]
            bsum[...] += part
            G[0][i] = g.T.astype(BF)

        send(half(G[0], h), half(G[3], h), S_G + h, at(dy=1))
        send(half(G[0], h), half(G[1], h), S_G + 2 + h, at(dy=-1))
        leaving.append(local(ov.at[rows_of(h)], out.at[rows_of(h)], L_OUT + h))

    def spread(n, base, dst, tail):
        @pl.loop(0, 8)
        def _(j):
            r = pl.ds(pl.multiple_of(j * 16, 16), 16)
            parts = [D[k, r, :] for k in range(n)]
            for t in range(NB):
                acc = jnp.where(base[0] == t, parts[0], 0.0)
                for k in range(1, n):
                    acc += jnp.where(base[k] == t, parts[k], 0.0)
                tail(dst, t, r, acc)

    def add_f32(dst, t, r, acc):
        dst[t, r, :] += acc

    def put_f32(dst, t, r, acc):
        dst[t, r, :] = acc

    def put_bf16(dst, t, r, acc):
        dst[t, r, :] = acc.astype(BF)

    send(bsum, bcore, S_B0, at(oc=1))

    @pl.loop(0, 4)
    def _(i):
        k0 = i * 8
        for j in range(8):
            D[j] = dot(G[0][row_own[0, k0 + j]], TL[i // 2, lax.rem(i, 2) * 2 + j // 4, j % 4])
        spread(8, [src_own[0, k0 + j] for j in range(8)], SL, add_f32)

    arrived(bcore, S_B0)
    bz[z] = bsum[...] + bcore[...]
    for e in range(1, NZ):
        send(bz.at[z], bz.at[z], S_B1 + SLOT[-DIST[e]], at(dz=DIST[e]))

    arrived(half(G[3], 0), S_G + 0)
    send(half(G[3], 0), half(G[2], 0), S_GR + 0, at(dy=1))
    arrived(half(G[1], 1), S_G + 3)
    send(half(G[1], 1), half(G[2], 1), S_GR + 1, at(dy=-1))
    arrived(half(G[1], 0), S_G + 2)
    arrived(half(G[3], 1), S_G + 1)
    for h in range(2):
        arrived(half(G[2], h), S_GR + h)

    def backward(e, oc, dst, tail):
        cc = lax.rem(c + oc, NC)
        blocks = []
        for dy in range(NY):
            for cap in range(CAP):
                D[dy * 2 + cap] = dot(G[dy][slot_row(dy, e, cc, cap)], T[dy, e, cc * 2 + cap])
                blocks.append(slot_block(dy, e, oc, cap))
        spread(8, blocks, dst, tail)

    def combine(dst, e, h, way=None, step=None):
        @pl.loop(0, 4, unroll=True)
        def _(i):
            t = 4 * h + i
            value = S0[e, t] + sibrecv[e, t].astype(F32)
            if step is not None:
                value += zrecv[way, step, t].astype(F32)
            dst[t] = value.astype(BF)

    def ring_send(way, step, h):
        send(
            half(zsend.at[way, step], h), half(zrecv.at[way, step], h), S_ZR + way * 8 + step * 2 + h,
            at(dz=1 if way == 0 else -1),
        )

    def terms(e):
        backward(e, 1, sibsend.at[e], put_bf16)
        send(sibsend.at[e], sibrecv.at[e], S_SIB + e, at(oc=1))
        backward(e, 0, S0.at[e], put_f32)

    def bias_step(step):
        if step == 2:
            for e in range(1, NZ):
                arrived(bz.at[lax.rem(z + DIST[e] + NZ, NZ)], S_B1 + e)
            total = bz[0]
            for k in range(1, NZ):
                total += bz[k]
            by[y] = total
            for d in range(1, NY):
                send(by.at[y], by.at[y], S_B2 + NY - d, at(dy=d))
        elif step == 3:
            for d in range(1, NY):
                arrived(by.at[lax.rem(y + d, NY)], S_B2 + d)
            gbv[...] = jnp.sum(by[0] + by[1] + by[2] + by[3], 0, keepdims=True)
            leaving.append(local(gbv, gb, L_GB))

    terms(SLOT[4])
    arrived(sibrecv.at[SLOT[4]], S_SIB + SLOT[4])
    for way in range(2):
        combine(zsend.at[way, 0], SLOT[4], way)
        ring_send(way, 0, way)
    for step in range(1, 4):
        d = 4 - step
        ends = (SLOT[d], SLOT[-d])
        for e in ends:
            terms(e)
        for e in ends:
            arrived(sibrecv.at[e], S_SIB + e)
        order = ((1, 0), (0, 1), (0, 0), (1, 1)) if step == 1 else ((0, 0), (1, 0), (0, 1), (1, 1))
        for way, h in order:
            came = step > 1 or h == way
            if came:
                arrived(half(zrecv.at[way, step - 1], h), S_ZR + way * 8 + (step - 1) * 2 + h)
            combine(zsend.at[way, step], ends[way], h, way, step - 1 if came else None)
            ring_send(way, step, h)
        bias_step(step)
    terms(0)
    arrived(sibrecv.at[0], S_SIB + 0)

    def terms_x(dx, h, dst, more=None):
        @pl.loop(0, 4, unroll=True)
        def _(b):
            r = pl.ds(pl.multiple_of(512 * h + b * B, B), B)
            value = dot_t(GA[r, :], w_rows(dx))
            if more is not None:
                value += more[pl.ds(pl.multiple_of(b * B, B), B), :].astype(F32)
            dst[r, :] = value.astype(dst.dtype)

    for h in range(2):
        for way in range(2):
            arrived(half(zrecv.at[way, 3], h), S_ZR + way * 8 + 6 + h)

        @pl.loop(0, 4, unroll=True)
        def _(i, h=h):
            t = 4 * h + i
            value = S0[0, t] + sibrecv[0, t].astype(F32) + SL[t]
            value += zrecv[0, 3, t].astype(F32) + zrecv[1, 3, t].astype(F32)
            value = value.astype(BF).astype(F32)
            GAT[:, pl.ds(pl.multiple_of(t * B, B), B)] = value.astype(BF)
            GA[pl.ds(pl.multiple_of(t * B, B), B), :] = value.T.astype(BF)

        if h == 0:
            terms_x(2, 0, xsend2)
            send(xsend2.at[rows_of(0)], xrel.at[0], S_XR + 0, at(dx=1))
            terms_x(3, 0, xsend3)
            send(xsend3.at[rows_of(0)], xin.at[1, rows_of(0)], S_XI + 2, at(dx=-1))

    def weight_terms(core):
        for i in range(2):
            dx = lax.rem(core * 2 + i - x + NX, NX)
            gws[core, B * i : B * i + B, :] = dot(GAT[...], F[dx]).T

    weight_terms(1 - c)
    send(gws.at[1 - c], arc, S_A0, at(oc=1))
    weight_terms(c)
    terms_x(2, 1, xsend2)
    send(xsend2.at[rows_of(1)], xrel.at[1], S_XR + 1, at(dx=-1))

    arrived(arc, S_A0)
    for k in range(NZ):
        value = gws[c, 32 * k : 32 * k + 32, :] + arc[32 * k : 32 * k + 32, :]
        arown[k] = value
        arsend[k] = value.astype(BF)
    for e in range(NZ - 1, 0, -1):
        send(arsend.at[lax.rem(z + DIST[e] + NZ, NZ)], arin.at[z], S_A1 + SLOT[-DIST[e]], at(dz=DIST[e]))
    terms_x(1, 1, xsend1)
    send(xsend1.at[rows_of(1)], xin.at[0, rows_of(1)], S_XI + 1, at(dx=1))

    arrived(xrel.at[0], S_XR + 0)
    terms_x(1, 0, xsend1, xrel.at[0])
    send(xsend1.at[rows_of(0)], xin.at[0, rows_of(0)], S_XI + 0, at(dx=1))
    terms_x(0, 0, PT)
    arrived(xrel.at[1], S_XR + 1)
    terms_x(3, 1, xsend3, xrel.at[1])
    send(xsend3.at[rows_of(1)], xin.at[1, rows_of(1)], S_XI + 3, at(dx=-1))

    total = arown[z]
    for e in range(1, NZ):
        k = lax.rem(z + DIST[e] + NZ, NZ)
        arrived(arin.at[k], S_A1 + e)
        total += arin[k].astype(F32)
    ar2in[y] = total
    for d in range(1, NY):
        send(ar2in.at[y], ar2in.at[y], S_A2 + NY - d, at(dy=d))
    terms_x(0, 1, PT)
    for d in range(1, NY):
        arrived(ar2in.at[lax.rem(y + d, NY)], S_A2 + d)
    gwall[c, z] = (ar2in[0] + ar2in[1] + ar2in[2] + ar2in[3]).astype(BF)
    for e in range(NZ - 1, 0, -1):
        send(gwall.at[c, z], gwall.at[c, z], S_A3 + SLOT[-DIST[e]], at(dz=DIST[e]))

    def input_gradient(h):
        arrived(xin.at[0, rows_of(h)], S_XI + h)
        arrived(xin.at[1, rows_of(h)], S_XI + 2 + h)

        @pl.loop(0, 4, unroll=True)
        def _(b):
            r = pl.ds(pl.multiple_of(512 * h + b * B, B), B)
            giv[r, :] = (PT[r, :] + xin[0, r, :].astype(F32) + xin[1, r, :].astype(F32)).astype(BF)

        leaving.append(local(giv.at[rows_of(h)], gin.at[rows_of(h)], L_GIN + h))

    input_gradient(0)
    input_gradient(1)
    for e in range(1, NZ):
        arrived(gwall.at[c, lax.rem(z + DIST[e] + NZ, NZ)], S_A3 + e)
    send(gwall.at[c], gwall.at[c], S_A4, at(oc=1))
    arrived(gwall.at[1 - c], S_A4)
    for k in range(NC):
        gwf[k] = gwall[k].astype(F32)
    leaving.append(local(gwf, gw, L_GW))
    for made in leaving:
        made.wait()
    for made in started[-S_SEND:]:
        made.wait_send()


def hand_over(*refs):
    given, result, sem = refs[0:4], refs[4:8], refs[8]
    writes = [pltpu.make_async_copy(given[k], result[k], sem.at[k]) for k in range(4)]
    for made in writes:
        made.start()
    for made in writes:
        made.wait()


def shards(
    features, weight, bias, cotangent, tile_vals, tile_row, tile_src, send_blocks, send_count
):
    blocks = lambda *lead, dtype=BF: pltpu.VMEM((*lead, B, B), dtype)
    scratch = [
        pltpu.VMEM((NX, 1024, B), BF),
        blocks(NB),
        blocks(NB),
        *[blocks(NC, NB) for _ in range(NZ - 2)],
        blocks(NB),
        blocks(NB),
        blocks(NY, NZ, 4),
        blocks(2, 4, 4),
        blocks(4),
        blocks(NY, NB, dtype=F32),
        blocks(NB),
        blocks(NB),
        blocks(NB),
        blocks(2, 4),
        blocks(2, NB),
        *[blocks(NB + 1) for _ in range(NY)],
        blocks(8, dtype=F32),
        blocks(NZ, NB, dtype=F32),
        blocks(NB, dtype=F32),
        blocks(2, 4, NB),
        blocks(2, 4, NB),
        blocks(NZ, NB),
        blocks(NZ, NB),
        pltpu.VMEM((B, 1024), BF),
        pltpu.VMEM((1024, B), BF),
        pltpu.VMEM((1024, B), F32),
        pltpu.VMEM((1024, B), BF),
        pltpu.VMEM((1024, B), BF),
        pltpu.VMEM((1024, B), BF),
        pltpu.VMEM((2, 512, B), BF),
        pltpu.VMEM((2, 1024, B), BF),
        pltpu.VMEM((8, B), F32),
        pltpu.VMEM((8, B), F32),
        pltpu.VMEM((NZ, 8, B), F32),
        pltpu.VMEM((NY, 8, B), F32),
        pltpu.VMEM((NC, 256, B), F32),
        pltpu.VMEM((256, B), F32),
        pltpu.VMEM((NZ, 32, B), F32),
        pltpu.VMEM((NZ, 32, B), BF),
        pltpu.VMEM((NZ, 32, B), BF),
        pltpu.VMEM((NY, 32, B), F32),
        pltpu.VMEM((NC, NZ, 32, B), BF),
        pltpu.VMEM((NC, NZ, 32, B), F32),
        pltpu.VMEM((512, B), BF),
        pltpu.VMEM((1024, B), BF),
        pltpu.VMEM((1, B), BF),
        pltpu.VMEM((1024, B), BF),
        pltpu.VMEM((1024, B), BF),
        pltpu.VMEM((1, B), F32),
        pltpu.VMEM((NC, NZ, CAP, 64), jnp.int32),
        pltpu.VMEM((NY, 1, 160), jnp.int32),
        pltpu.SMEM((NC, NZ, CAP, 64), jnp.int32),
        pltpu.SMEM((NY, 1, 160), jnp.int32),
        pltpu.SemaphoreType.DMA((S_SEND,)),
        pltpu.SemaphoreType.DMA((S_RECV,)),
        pltpu.SemaphoreType.DMA((L_N + NZ,)),
    ]
    anywhere = pl.BlockSpec(memory_space=pl.ANY)
    smem = pl.BlockSpec(memory_space=pltpu.SMEM)
    shapes = (
        jax.ShapeDtypeStruct((1024, B), BF),
        jax.ShapeDtypeStruct((1024, B), BF),
        jax.ShapeDtypeStruct((NC, NZ, 32, B), F32),
        jax.ShapeDtypeStruct((1, B), F32),
    )
    results = pl.pallas_call(
        kernel,
        out_shape=tuple(pltpu.VMEM(a.shape, a.dtype) for a in shapes),
        in_specs=[anywhere] * 7 + [smem] * 2,
        out_specs=(pl.BlockSpec(memory_space=pltpu.VMEM),) * 4,
        scratch_shapes=scratch,
        compiler_params=pltpu.CompilerParams(
            collective_id=0, has_side_effects=True, vmem_limit_bytes=56 * 2**20
        ),
    )(
        features,
        weight,
        bias.reshape(1, B),
        cotangent,
        tile_vals.reshape(10, 4, 4, B, B),
        send_blocks.transpose(0, 2, 1).reshape(CAP, 64),
        tile_row,
        tile_row,
        tile_src,
    )
    out, gin, gw, gb = pl.pallas_call(
        hand_over,
        out_shape=shapes,
        in_specs=[pl.BlockSpec(memory_space=pltpu.VMEM)] * 4,
        out_specs=(anywhere,) * 4,
        scratch_shapes=[pltpu.SemaphoreType.DMA((4,))],
        compiler_params=pltpu.CompilerParams(vmem_limit_bytes=8 * 2**20),
    )(*results)
    return out, gin, gw.reshape(512, B), gb.reshape(B)


def solution(mesh):
    in_specs = (
        P("dom", "rep"),
        P(None, "rep"),
        P("rep"),
        P("dom", "rep"),
        P("dom", None, None, None),
        P("dom", None),
        P("dom", None),
        P("dom", None, None),
        P("dom", None),
    )
    out_specs = (P("dom", "rep"), P("dom", "rep"), P(None, "rep"), P("rep"))
    return jax.shard_map(shards, mesh=mesh, in_specs=in_specs, out_specs=out_specs, check_vma=False)
```
